32 devices in a mesh: geo: 8 (over z, x), bins: 4 (over y, core).
Axes of the slice: x: 2, y: 2, z: 4, core: 2. Of those that a mesh axis runs over, the one named last changes fastest.
Arguments:
- spectrum: float32 [1152, 64, 256], P('bins', 'geo'), may hold values from 0.1 to 2
- sea_mask: int32 [64, 256], P('geo'), may hold values 0 or 1
- kernel_linear: bfloat16 [1152, 1152], replicated, may hold values from -0.1875 to 0.1875
- kernel_square: bfloat16 [1152, 1152], replicated, may hold values from -0.1875 to 0.1875
- drift_kernel: bfloat16 [128, 1152], replicated, may hold values from -0.1875 to 0.1875
- ocean: float32 [2, 64, 64, 256], P(None, 'bins', 'geo'), may hold values from -3 to 3
Outputs:
- spectrum_out: float32 [1152, 64, 256], P('bins', 'geo')
- ocean_out: float32 [2, 64, 64, 256], P(None, 'bins', 'geo')
The draws below stay inside these ranges and needn't reach their ends.
Inputs may be any that keep to these rules, and one draw needn't show every extreme that they name: `sea_mask`: 1 marks a sea column, 0 a land column.
All inputs are finite; a program needn't handle non-finite values. No bound on the sum of `sea_mask` on one device may be relied on, other than what follows from the above.
Results may differ from the reference program's by a relative error of at most 0.0018.
Values sent between devices are 32-bit elements; how exact they have to be, the bound alone decides.
No kernel may reach another device: no remote copies, remote signals or barrier semaphores. Data moves between devices by JAX's collectives and lax.ppermute only.
A program may use at most 128 MiB of HBM per device.

```python
import math
import jax
import jax.numpy as jnp
from jax import lax

NDIR = 36
NFREQ = 32
NB = 1152
CY = 256
LEV = 64
STEPS = 3
SUB = 2
NX = 64


def touch_ends(values, key, low, high):
    spot = [jax.random.randint(jax.random.fold_in(key, axis), (), 0, length) for axis, length in enumerate(values.shape)]
    widest = values.shape.index(max(values.shape))
    neighbour = spot[:widest] + [(spot[widest] + 1) % values.shape[widest]] + spot[widest + 1:]
    return values.at[tuple(spot)].set(low).at[tuple(neighbour)].set(high)


def shard_levels(key, shape, pieces, low, high):
    def one(axis_at, blocks):
        steps = jax.random.uniform(jax.random.fold_in(jax.random.fold_in(key, 6), axis_at), (blocks,), jnp.float32, low / len(pieces), high / len(pieces))
        return jnp.repeat(jnp.exp(steps), shape[axis_at] // blocks).reshape((-1,) + (1,) * (len(shape) - axis_at - 1))

    level = one(*pieces[0])
    for cut in pieces[1:]:
        level = level * one(*cut)
    return level


def gaussian(rng, dims, scale, reach, cuts=(), kind=jnp.bfloat16):
    factor_of = shard_levels(rng, dims, cuts, -0.22, 0.18) if cuts else 1.0
    values = jax.random.normal(rng, dims, jnp.float32) * scale * factor_of
    return jnp.minimum(jnp.maximum(values, -reach), reach).astype(kind)


def setup_inputs(seed: int = 0) -> dict:
    arg_keys = jax.random.split(jax.random.key(seed), 7)
    spectrum = jnp.clip(jnp.exp(math.log(2.0) - 2.9957323 * jax.random.uniform(arg_keys[0], (NB, NX, CY), jnp.float32) ** shard_levels(arg_keys[0], (NB, NX, CY), ((0, 4), (1, 8)), -0.2, 0.2)), 0.1, 2.0)
    sea_mask = touch_ends((jax.random.randint(arg_keys[1], (NX, CY), 0, 4) < 3).astype(jnp.int32), jax.random.fold_in(arg_keys[1], 1), 0, 1)
    kernel_linear = gaussian(arg_keys[2], (NB, NB), NB ** -0.5, 0.1875)
    kernel_square = gaussian(arg_keys[3], (NB, NB), NB ** -0.5, 0.1875)
    drift_kernel = gaussian(arg_keys[4], (2 * LEV, NB), NB ** -0.5, 0.1875)
    ocean = gaussian(arg_keys[5], (2, LEV, NX, CY), 0.5, 3.0, ((1, 4), (2, 8)), jnp.float32)
    return {"spectrum": spectrum, "sea_mask": sea_mask, "kernel_linear": kernel_linear, "kernel_square": kernel_square, "drift_kernel": drift_kernel, "ocean": ocean}


DT_SOURCE = 0.5
DT_OCEAN = 0.2
CORIOLIS = 1.0
VISCOSITY = 1.0
DOPPLER = 0.1


def speeds(first_bin, bin_count):
    bin_index = first_bin + jnp.arange(bin_count, dtype=jnp.int32)
    direction = (bin_index // NFREQ).astype(jnp.float32)
    frequency = (bin_index % NFREQ).astype(jnp.float32)
    group_speed = 0.4 / (1.0 + frequency / 16.0)
    bin_angle = (2.0 * jnp.pi / NDIR) * direction
    return group_speed * jnp.cos(bin_angle), group_speed * jnp.sin(bin_angle)


def along_y(energy, speed_y):
    flux_plus = jnp.maximum(speed_y, 0.0) * energy
    flux_minus = jnp.minimum(speed_y, 0.0) * energy
    zeros_edge = jnp.zeros_like(flux_plus[..., :1])
    plus_before = jnp.concatenate([zeros_edge, flux_plus[..., :-1]], axis=-1)
    minus_after = jnp.concatenate([flux_minus[..., 1:], zeros_edge], axis=-1)
    return (flux_plus - plus_before) + (minus_after - flux_minus)


def step_cells(energy, plus_left, flux_plus, flux_minus, minus_right, speed_y, sea_float):
    moved = energy - ((flux_plus - plus_left) + (minus_right - flux_minus)) - along_y(energy, speed_y)
    return moved * sea_float


def renew_source(energy, interaction, squares_sum, sea_float):
    return energy + DT_SOURCE * (sea_float * (interaction * energy / (1.0 + squares_sum / NB)))


def laplace(centre, west_side, east_side):
    zeros_edge = jnp.zeros_like(centre[..., :1])
    north_side = jnp.concatenate([centre[..., 1:], zeros_edge], axis=-1)
    south_side = jnp.concatenate([zeros_edge, centre[..., :-1]], axis=-1)
    return (east_side + west_side) + (north_side + south_side) - 4.0 * centre


def ocean_step(ocean_state, west_side, east_side, stokes_u, stokes_v, sea_float):
    laplacian = laplace(ocean_state, west_side, east_side)
    new_u = (ocean_state[0] + DT_OCEAN * (CORIOLIS * (ocean_state[1] + stokes_v) + VISCOSITY * laplacian[0])) * sea_float
    new_v = (ocean_state[1] + DT_OCEAN * (-(CORIOLIS * (ocean_state[0] + stokes_u)) + VISCOSITY * laplacian[1])) * sea_float
    return jnp.stack([new_u, new_v])


def widen(values):
    return lax.optimization_barrier(values.astype(jnp.bfloat16)).astype(jnp.float32)


def reference(spectrum, sea_mask, kernel_linear, kernel_square, drift_kernel, ocean):
    sea_float = sea_mask.astype(jnp.float32)
    speed_cx, speed_cy = speeds(0, NB)
    energy = spectrum
    ocean_state = ocean
    width_x = spectrum.shape[1]
    width_y = spectrum.shape[2]
    levels = ocean.shape[1]
    wide_linear = kernel_linear.astype(jnp.float32)
    wide_square = kernel_square.astype(jnp.float32)
    wide_drift = drift_kernel.astype(jnp.float32)
    for step_index in range(STEPS):
        tanh_cur = jnp.tanh(ocean_state[:, 0])
        speed_x = speed_cx[:, None, None] + DOPPLER * tanh_cur[0][None]
        speed_y = speed_cy[:, None, None] + DOPPLER * tanh_cur[1][None]
        for substep in range(SUB):
            flux_plus = jnp.maximum(speed_x, 0.0) * energy
            flux_minus = jnp.minimum(speed_x, 0.0) * energy
            energy = step_cells(energy, jnp.roll(flux_plus, 1, axis=1), flux_plus, flux_minus,
                                jnp.roll(flux_minus, -1, axis=1), speed_y, sea_float)
        energy_flat = energy.reshape(NB, width_x * width_y)
        interaction = jnp.dot(wide_linear, widen(energy_flat), precision=lax.Precision.HIGHEST) + \
            jnp.dot(wide_square, widen(energy_flat * energy_flat), precision=lax.Precision.HIGHEST)
        updated = renew_source(energy_flat, interaction, jnp.sum(energy_flat * energy_flat, axis=0),
                               sea_float.reshape(width_x * width_y))
        stokes_drift = jnp.dot(wide_drift, widen(updated), precision=lax.Precision.HIGHEST)
        energy = updated.reshape(NB, width_x, width_y)
        stokes_drift = stokes_drift.reshape(levels, 2, width_x, width_y)
        ocean_state = ocean_step(ocean_state, jnp.roll(ocean_state, 1, axis=2), jnp.roll(ocean_state, -1, axis=2),
                                 stokes_drift[:, 0], stokes_drift[:, 1], sea_float)
    return energy, ocean_state
```

```python
import functools

import jax
import jax.numpy as jnp
from jax import lax
from jax.experimental import pallas as pl
from jax.experimental.pallas import tpu as pltpu
from jax.sharding import PartitionSpec as P

NDIR = 36
NFREQ = 32
STEPS = 3
SUB = 2
DT_SOURCE = 0.5
DT_OCEAN = 0.2
CORIOLIS = 1.0
VISCOSITY = 1.0
DOPPLER = 0.1

LANES = 128
PAD = 8
VMEM = pl.BlockSpec(memory_space=pltpu.VMEM)
SMEM = pl.BlockSpec(memory_space=pltpu.SMEM)


def params(mib):
    return pltpu.CompilerParams(vmem_limit_bytes=mib * 1024 * 1024)


def sizes_of(parts, bins_here, levels_here, rows, width):
    z = dict(B=parts, nb=bins_here, L=levels_here, R=rows, W=width, C=width // parts)
    z["mt"] = bins_here // LANES
    z["main"] = z["mt"] * LANES
    z["nr"] = bins_here - z["main"]
    z["no"] = 2 * levels_here
    z["Fr"] = LANES // z["nr"]
    z["Fo"] = LANES // z["no"]
    z["Rr"] = rows // z["Fr"]
    z["Ro"] = rows // z["Fo"]
    z["slabs"] = rows * z["mt"] + z["Rr"] + z["Ro"]
    z["NB"] = parts * bins_here
    z["CH"] = z["NB"] + LANES
    assert z["nr"] * parts == LANES and z["no"] * parts == LANES
    assert z["Rr"] * z["Fr"] == rows and z["Ro"] * z["Fo"] == rows
    return z


def lane_group(width):
    return lax.broadcasted_iota(jnp.int32, (1, LANES), 1) // width


def pack_kernel(z, who, spec_in, ocean_in, out, spec, ocean):
    B, R, C, mt = z["B"], z["R"], z["C"], z["mt"]
    for half in range(z["W"] // LANES):
        spec[half] = spec_in[:, half * LANES : (half + 1) * LANES]
        ocean[half] = ocean_in[:, half * LANES : (half + 1) * LANES]
    mine = who[0]
    slots = [lax.rem(c - mine + B, B) for c in range(B)]

    def put(slab, half, block):
        turned = block.T
        for i in range(LANES // C):
            c = half * (LANES // C) + i
            out[slots[c], slab] = turned[i * C : (i + 1) * C]

    for half in range(z["W"] // LANES):
        for r in range(R):
            for t in range(mt):
                put(r * mt + t, half, spec[half, pl.ds(t * LANES * R + r, LANES, stride=R), :])
        for src, first, count, fold, base in (
            (spec, z["main"], z["nr"], z["Fr"], R * mt),
            (ocean, 0, z["no"], z["Fo"], R * mt + z["Rr"]),
        ):
            for rr in range(R // fold):
                pieces = [
                    src[half, pl.ds(first * R + rr + i * (R // fold), count, stride=R), :]
                    for i in range(fold)
                ]
                put(base + rr, half, jnp.concatenate(pieces, axis=0))


def unpack_kernel(z, who, *refs):
    B, R, C, mt = z["B"], z["R"], z["C"], z["mt"]
    got, (out, left, right) = refs[:B], refs[B:]
    share = who[0]
    src = [lax.rem(share - k + B, B) for k in range(B)]
    for k in range(B):
        for t in range(mt):
            lanes = pl.ds(pl.multiple_of(src[k] * z["main"] + t * LANES, LANES), LANES)
            for r in range(R):
                out[r, :, lanes] = got[k][r * mt + t]
    for count, fold, base, first in (
        (z["nr"], z["Fr"], R * mt, B * z["main"]),
        (z["no"], z["Fo"], R * mt + z["Rr"], z["NB"]),
    ):
        group = lane_group(count)
        deep = R // fold
        for r in range(R):
            tile = jnp.zeros((C, LANES), jnp.float32)
            for k in range(B):
                shift = lax.rem((src[k] - r // deep) * count + LANES, LANES)
                moved = pltpu.roll(got[k][base + r % deep], shift, axis=1)
                tile = jnp.where(group == src[k], moved, tile)
            out[r, :, first : first + LANES] = tile
    for r in range(R):
        left[2 * r : 2 * r + 2] = out[r, 0:2]
        right[2 * r : 2 * r + 2] = out[r, C - 2 : C]


def send_back_kernel(z, who, state, out):
    B, R, C, mt = z["B"], z["R"], z["C"], z["mt"]
    share = who[0]
    for k in range(B):
        src = lax.rem(share - k + B, B)
        for t in range(mt):
            lanes = pl.ds(pl.multiple_of(src * z["main"] + t * LANES, LANES), LANES)
            for r in range(R):
                out[k, r * mt + t] = state[r, :, lanes]
        for count, fold, base, first in (
            (z["nr"], z["Fr"], R * mt, B * z["main"]),
            (z["no"], z["Fo"], R * mt + z["Rr"], z["NB"]),
        ):
            group = lane_group(count)
            deep = R // fold
            for rr in range(deep):
                tile = jnp.zeros((C, LANES), jnp.float32)
                for i in range(fold):
                    shift = lax.rem((i - src) * count + LANES, LANES)
                    moved = pltpu.roll(
                        state[rr + i * deep, :, first : first + LANES], shift, axis=1
                    )
                    tile = jnp.where(group == i, moved, tile)
                out[k, base + rr] = tile


def restore_kernel(z, who, *refs):
    B, R, C, mt = z["B"], z["R"], z["C"], z["mt"]
    got, (spec_out, ocean_out, wide, spec, ocean) = refs[:B], refs[B:]
    mine = who[0]
    for k in range(B):
        c = lax.rem(mine + k, B)
        wide[:, pl.ds(pl.multiple_of(c * C, C), C), :] = got[k][...]
    for half in range(z["W"] // LANES):
        cols = pl.ds(half * LANES, LANES)
        for r in range(R):
            for t in range(mt):
                at = pl.ds(t * LANES * R + r, LANES, stride=R)
                spec[half, at, :] = wide[r * mt + t, cols].T
        for dst, first, count, fold, base in (
            (spec, z["main"], z["nr"], z["Fr"], R * mt),
            (ocean, 0, z["no"], z["Fo"], R * mt + z["Rr"]),
        ):
            for rr in range(R // fold):
                turned = wide[base + rr, cols].T
                for i in range(fold):
                    at = pl.ds(first * R + rr + i * (R // fold), count, stride=R)
                    dst[half, at, :] = turned[i * count : (i + 1) * count]
        spec_out[:, cols] = spec[half]
        ocean_out[:, cols] = ocean[half]


def step_kernel(
    z, state, up, down, left, right, up_corner, down_corner, sea, speed, weights, drift_weights,
    new, new_left, new_right, ext, moved, moved_twice, east, north,
):
    R, C, NB, CH, L = z["R"], z["C"], z["NB"], z["CH"], z["L"]
    E = C + 2 * PAD
    own = slice(PAD, PAD + C)

    for r in range(R):
        ext[r + 2, own] = state[r]
        ext[r + 2, PAD - 2 : PAD] = left[2 * r : 2 * r + 2]
        ext[r + 2, PAD + C : PAD + C + 2] = right[2 * r : 2 * r + 2]
    for rows, corner, at in ((up, up_corner, 0), (down, down_corner, R + 2)):
        for i in range(2):
            ext[at + i, own] = rows[i]
            ext[at + i, PAD - 2 : PAD] = corner[2 * i : 2 * i + 2]
            ext[at + i, PAD + C : PAD + C + 2] = corner[4 + 2 * i : 6 + 2 * i]

    for r in range(R + 4):
        top = ext[r, :, NB:CH]
        east[r] = DOPPLER * jnp.tanh(jnp.broadcast_to(top[:, 0:1], (E, LANES)))
        north[r] = DOPPLER * jnp.tanh(jnp.broadcast_to(top[:, L : L + 1], (E, LANES)))

    def advect(read, write, first, last, speed_cx, speed_cy):
        def along_x(r):
            energy = read(r)
            speed_x = speed_cx + east[r]
            return (
                energy,
                jnp.maximum(speed_x, 0.0) * energy,
                jnp.minimum(speed_x, 0.0) * energy,
            )

        _, plus_before, _ = along_x(first - 1)
        energy, plus, minus = along_x(first)
        for r in range(first, last):
            energy_next, plus_next, minus_next = along_x(r + 1)
            speed_y = speed_cy + north[r]
            plus_y = jnp.maximum(speed_y, 0.0) * energy
            minus_y = jnp.minimum(speed_y, 0.0) * energy
            result = (
                energy
                - ((plus - plus_before) + (minus_next - minus))
                - (
                    (plus_y - pltpu.roll(plus_y, 1, axis=0))
                    + (pltpu.roll(minus_y, E - 1, axis=0) - minus_y)
                )
            )
            write(r, result * sea[r])
            plus_before, energy, plus, minus = plus, energy_next, plus_next, minus_next

    def one_tile(j, carry):
        lanes = pl.ds(pl.multiple_of(j * LANES, LANES), LANES)
        speed_cx = speed[0:1, lanes]
        speed_cy = speed[1:2, lanes]

        def write_first(r, value):
            moved[r] = value

        def write_second(r, value):
            moved_twice[r - 2, :, lanes] = value[own]

        advect(lambda r: ext[r, :, lanes], write_first, 1, R + 3, speed_cx, speed_cy)
        advect(lambda r: moved[r], write_second, 2, R + 2, speed_cx, speed_cy)
        return carry

    lax.fori_loop(0, NB // LANES, one_tile, 0)

    chunk_rows = max(1, 256 // C)
    comp = (lax.broadcasted_iota(jnp.int32, (1, LANES), 1) // L) % 2
    sign = jnp.where(comp == 0, 1.0, -1.0).astype(jnp.float32)

    def one_chunk(m, carry):
        at = m * chunk_rows
        rows = pl.ds(at, chunk_rows)
        energy = moved_twice[rows].reshape(chunk_rows * C, NB)
        squares = energy * energy
        interaction = jnp.dot(
            energy.astype(jnp.bfloat16), weights[:NB], preferred_element_type=jnp.float32
        ) + jnp.dot(
            squares.astype(jnp.bfloat16), weights[NB:], preferred_element_type=jnp.float32
        )
        total = jnp.sum(squares, axis=1, keepdims=True)
        sea_here = sea[pl.ds(at + 2, chunk_rows), own].reshape(chunk_rows * C, LANES)
        scale = (DT_SOURCE * sea_here[:, 0:1]) / (1.0 + total / NB)
        fresh = energy + scale * (interaction * energy)
        new[rows, :, 0:NB] = fresh.reshape(chunk_rows, C, NB)
        drift = jnp.dot(
            fresh.astype(jnp.bfloat16), drift_weights[...], preferred_element_type=jnp.float32
        )
        for i in range(chunk_rows):
            r = at + i + 2
            here = ext[r, :, NB:CH]
            lap = (
                (ext[r + 1, own, NB:CH] + ext[r - 1, own, NB:CH])
                + (pltpu.roll(here, E - 1, axis=0) + pltpu.roll(here, 1, axis=0))[own]
                - 4.0 * here[own]
            )
            centre = here[own]
            other = jnp.where(
                comp == 0, pltpu.roll(centre, LANES - L, axis=1), pltpu.roll(centre, L, axis=1)
            )
            turn = sign * (CORIOLIS * (other + drift[i * C : (i + 1) * C]))
            new[at + i, :, NB:CH] = (centre + DT_OCEAN * (turn + VISCOSITY * lap)) * sea[r, own]
        return carry

    lax.fori_loop(0, R // chunk_rows, one_chunk, 0)

    for r in range(R):
        new_left[2 * r : 2 * r + 2] = new[r, 0:2]
        new_right[2 * r : 2 * r + 2] = new[r, C - 2 : C]


def speeds(bin_count):
    bin_index = jnp.arange(bin_count, dtype=jnp.int32)
    direction = (bin_index // NFREQ).astype(jnp.float32)
    frequency = (bin_index % NFREQ).astype(jnp.float32)
    group_speed = 0.4 / (1.0 + frequency / 16.0)
    bin_angle = (2.0 * jnp.pi / NDIR) * direction
    return group_speed * jnp.cos(bin_angle), group_speed * jnp.sin(bin_angle)


def per_device(G, B, spectrum, sea_mask, kernel_linear, kernel_square, drift_kernel, ocean):
    nb, R, W = spectrum.shape
    L = ocean.shape[1]
    z = sizes_of(B, nb, L, R, W)
    C, NB, CH, slabs = z["C"], z["NB"], z["CH"], z["slabs"]
    half = B // 2
    axes = ("geo", "bins")
    geo, part = lax.axis_index("geo"), lax.axis_index("bins")

    def tile_of(g, b):
        return (g // 2) * 2 + b % 2

    def share_of(g, b):
        along = b // 2
        return along + half * (g % 2) + (half - 1 - 2 * along) * (g % 2)

    def device_at(q, c):
        m, along = c // half, c % half
        along = along if m == 0 else half - 1 - along
        return ((q // 2) * 2 + m) * B + 2 * along + q % 2

    tile, share = tile_of(geo, part), share_of(geo, part)
    forward = [
        [(g * B + b, device_at(g, (b + k) % B)) for g in range(G) for b in range(B)]
        for k in range(B)
    ]
    pairs = [(q, c) for q in range(G) for c in range(B)]
    to_next_row = [(device_at(q, c), device_at((q + 1) % G, c)) for q, c in pairs]
    to_prev_row = [(t, s) for s, t in to_next_row]
    to_next_col = [(device_at(q, c), device_at(q, c + 1)) for q, c in pairs if c + 1 < B]
    to_prev_col = [(t, s) for s, t in to_next_col]

    part_id = part.astype(jnp.int32).reshape(1)
    share_id = share.astype(jnp.int32).reshape(1)

    def reordered(array, axis):
        shape = array.shape
        split = array.reshape(shape[:axis] + (B, nb) + shape[axis + 1 :])
        head = lax.slice_in_dim(split, 0, z["main"], axis=axis + 1)
        tail = lax.slice_in_dim(split, z["main"], nb, axis=axis + 1)
        pieces = [p.reshape(shape[:axis] + (-1,) + shape[axis + 1 :]) for p in (head, tail)]
        return jnp.concatenate(pieces, axis=axis)

    weights = jnp.concatenate(
        [reordered(reordered(k, 0), 1).T for k in (kernel_linear, kernel_square)], axis=0
    )
    drift_rows = drift_kernel.reshape(B, L, 2, NB)[:, :, ::-1].transpose(0, 2, 1, 3)
    drift_weights = reordered(drift_rows.reshape(2 * B * L, NB), 1).T
    speed = reordered(jnp.stack(speeds(NB)), 1)
    speed = jnp.concatenate([speed, jnp.zeros((6, NB), jnp.float32)], axis=0)

    columns_scratch = [
        pltpu.VMEM((W // LANES, nb * R, LANES), jnp.float32),
        pltpu.VMEM((W // LANES, 2 * L * R, LANES), jnp.float32),
    ]

    packed = pl.pallas_call(
        functools.partial(pack_kernel, z),
        out_shape=jax.ShapeDtypeStruct((B, slabs, C, LANES), jnp.float32),
        in_specs=[SMEM, VMEM, VMEM],
        out_specs=VMEM,
        scratch_shapes=columns_scratch,
        compiler_params=params(32),
        name="pack",
    )(part_id, spectrum.reshape(nb * R, W), ocean.reshape(2 * L * R, W))
    got = [lax.ppermute(packed[k], axes, forward[k]) for k in range(B)]

    mask = lax.all_gather(sea_mask, "geo", axis=0, tiled=True)
    mask = jnp.concatenate([mask[-2:], mask, mask[:2]], axis=0)
    mask = jnp.pad(mask, ((0, 0), (PAD, PAD)))
    mask = lax.dynamic_slice(mask, (tile * R, share * C), (R + 4, C + 2 * PAD))
    sea = jnp.broadcast_to(mask.astype(jnp.float32)[..., None], mask.shape + (LANES,))

    state_shape = jax.ShapeDtypeStruct((R, C, CH), jnp.float32)
    edge_shape = jax.ShapeDtypeStruct((2 * R, CH), jnp.float32)
    state, left, right = pl.pallas_call(
        functools.partial(unpack_kernel, z),
        out_shape=(state_shape, edge_shape, edge_shape),
        in_specs=[SMEM] + [VMEM] * B,
        out_specs=(VMEM,) * 3,
        compiler_params=params(32),
        name="unpack",
    )(share_id, *got)

    E = C + 2 * PAD
    step = pl.pallas_call(
        functools.partial(step_kernel, z),
        out_shape=(state_shape, edge_shape, edge_shape),
        in_specs=[VMEM] * 11,
        out_specs=(VMEM,) * 3,
        scratch_shapes=[
            pltpu.VMEM((R + 4, E, CH), jnp.float32),
            pltpu.VMEM((R + 4, E, LANES), jnp.float32),
            pltpu.VMEM((R, C, NB), jnp.float32),
            pltpu.VMEM((R + 4, E, LANES), jnp.float32),
            pltpu.VMEM((R + 4, E, LANES), jnp.float32),
        ],
        compiler_params=params(48),
        name="coupled_step",
    )
    for _ in range(STEPS):
        from_left = lax.ppermute(right, axes, to_next_col)
        from_right = lax.ppermute(left, axes, to_prev_col)
        up = lax.ppermute(state[R - 2 :], axes, to_next_row)
        down = lax.ppermute(state[:2], axes, to_prev_row)
        bottom = jnp.concatenate([from_left[-4:], from_right[-4:]], axis=0)
        top = jnp.concatenate([from_left[:4], from_right[:4]], axis=0)
        up_corner = lax.ppermute(bottom, axes, to_next_row)
        down_corner = lax.ppermute(top, axes, to_prev_row)
        state, left, right = step(
            state, up, down, from_left, from_right, up_corner, down_corner,
            sea, speed, weights, drift_weights,
        )

    packed = pl.pallas_call(
        functools.partial(send_back_kernel, z),
        out_shape=jax.ShapeDtypeStruct((B, slabs, C, LANES), jnp.float32),
        in_specs=[SMEM, VMEM],
        out_specs=VMEM,
        compiler_params=params(32),
        name="send_back",
    )(share_id, state)
    back = [lax.ppermute(packed[k], axes, [(t, s) for s, t in forward[k]]) for k in range(B)]
    spectrum_out, ocean_out = pl.pallas_call(
        functools.partial(restore_kernel, z),
        out_shape=(
            jax.ShapeDtypeStruct((nb * R, W), jnp.float32),
            jax.ShapeDtypeStruct((2 * L * R, W), jnp.float32),
        ),
        in_specs=[SMEM] + [VMEM] * B,
        out_specs=(VMEM,) * 2,
        scratch_shapes=[pltpu.VMEM((slabs, W, LANES), jnp.float32)] + columns_scratch,
        compiler_params=params(32),
        name="restore",
    )(part_id, *back)
    return spectrum_out.reshape(nb, R, W), ocean_out.reshape(2, L, R, W)


def solution(mesh):
    return jax.shard_map(
        functools.partial(per_device, mesh.shape["geo"], mesh.shape["bins"]),
        mesh=mesh,
        in_specs=(
            P("bins", "geo", None),
            P("geo", None),
            P(),
            P(),
            P(),
            P(None, "bins", "geo", None),
        ),
        out_specs=(P("bins", "geo", None), P(None, "bins", "geo", None)),
        check_vma=False,
    )
```

```python
import functools

import jax
import jax.numpy as jnp
from jax import lax
from jax.experimental import pallas as pl
from jax.experimental.pallas import tpu as pltpu
from jax.sharding import PartitionSpec as P

NDIR = 36
NFREQ = 32
STEPS = 3
SUB = 2
DT_SOURCE = 0.5
DT_OCEAN = 0.2
CORIOLIS = 1.0
VISCOSITY = 1.0
DOPPLER = 0.1

LANES = 128
PAD = 8
EDGE = 2
VMEM = pl.BlockSpec(memory_space=pltpu.VMEM)
SMEM = pl.BlockSpec(memory_space=pltpu.SMEM)
F32 = jnp.float32
BF16 = jnp.bfloat16


def params(mib):
    return pltpu.CompilerParams(vmem_limit_bytes=mib * 1024 * 1024)


class Sizes:
    def __init__(self, parts, bins_here, levels_here, rows, width):
        self.B, self.nb, self.L, self.R, self.W = parts, bins_here, levels_here, rows, width
        self.C = width // parts
        self.mt = bins_here // LANES
        self.main = self.mt * LANES
        self.nr = bins_here - self.main
        self.no = 2 * levels_here
        self.NB = parts * bins_here
        self.CH = self.NB + LANES
        self.edge_rows = (0, 1, rows - 2, rows - 1)
        self.inner_rows = tuple(range(2, rows - 2))
        assert self.nr * parts == LANES and self.no * parts == LANES

    def folds(self, rows):
        out, base = [], len(rows) * self.mt
        for count, lane in ((self.nr, self.B * self.main), (self.no, self.NB)):
            used = min(LANES // count, len(rows))
            deep = len(rows) // used
            assert deep * used == len(rows)
            out.append((count, used, deep, base, lane))
            base += deep
        return out, base

    def slabs(self, rows):
        return self.folds(rows)[1]


def lane_group(width):
    return lax.broadcasted_iota(jnp.int32, (1, LANES), 1) // width


def pack_kernel(z, who, spec_in, ocean_in, *refs):
    B, R, C, W, mt = z.B, z.R, z.C, z.W, z.mt
    outs, (spec, ocean, wide) = refs[: 2 * B], refs[2 * B :]
    mine = who[0]
    at = 0
    for half in range(W // LANES):
        spec[half] = spec_in[:, half * LANES : (half + 1) * LANES]
        ocean[half] = ocean_in[:, half * LANES : (half + 1) * LANES]
    wide[:, 0:PAD, :] = jnp.zeros((wide.shape[0], PAD, LANES), F32)
    wide[:, PAD + W : W + 2 * PAD, :] = jnp.zeros((wide.shape[0], PAD, LANES), F32)
    for which, rows in enumerate((z.edge_rows, z.inner_rows)):
        folds, slabs = z.folds(rows)
        for half in range(W // LANES):
            cols = slice(PAD + half * LANES, PAD + (half + 1) * LANES)
            for i, r in enumerate(rows):
                for t in range(mt):
                    block = spec[half, pl.ds(t * LANES * R + r, LANES, stride=R), :]
                    wide[at + i * mt + t, cols] = block.T
            for (count, used, deep, base, _), src, first in zip(folds, (spec, ocean), (z.main, 0)):
                for rr in range(deep):
                    pieces = [
                        src[half, pl.ds(first * R + rows[rr + i * deep], count, stride=R), :]
                        for i in range(used)
                    ]
                    if used * count < LANES:
                        pieces.append(jnp.zeros((LANES - used * count, LANES), F32))
                    wide[at + base + rr, cols] = jnp.concatenate(pieces, axis=0).T
        for k in range(B):
            start = pl.multiple_of(lax.rem(mine + k, B) * C, PAD)
            outs[which * B + k][...] = wide[at : at + slabs, pl.ds(start, C + 2 * PAD), :]
        at += slabs


def unpack_kernel(z, rows, who, *refs):
    B, mt = z.B, z.mt
    got, outs = refs[:B], refs[B:]
    share = who[0]
    places = [(ref, i) for ref in outs for i in range(ref.shape[0])]
    src = [lax.rem(share - k + B, B) for k in range(B)]
    for k in range(B):
        for t in range(mt):
            lanes = pl.ds(pl.multiple_of(src[k] * z.main + t * LANES, LANES), LANES)
            for i, (ref, at) in enumerate(places):
                ref[at, :, lanes] = got[k][i * mt + t]
    for count, used, deep, base, lane in z.folds(rows)[0]:
        group = lane_group(count)
        for i, (ref, at) in enumerate(places):
            tile = jnp.zeros(ref.shape[1:2] + (LANES,), F32)
            for k in range(B):
                shift = lax.rem((src[k] - i // deep) * count + LANES, LANES)
                moved = pltpu.roll(got[k][base + i % deep], shift, axis=1)
                tile = jnp.where(group == src[k], moved, tile)
            ref[at, :, lane : lane + LANES] = tile


def send_back_kernel(z, rows, who, *refs):
    B, mt = z.B, z.mt
    states, outs = refs[:-B], refs[-B:]
    share = who[0]
    places = [(ref, i) for ref in states for i in range(ref.shape[0])]
    for k in range(B):
        src = lax.rem(share - k + B, B)
        for t in range(mt):
            lanes = pl.ds(pl.multiple_of(src * z.main + t * LANES, LANES), LANES)
            for i, (ref, at) in enumerate(places):
                outs[k][i * mt + t] = ref[at, :, lanes]
        for count, used, deep, base, lane in z.folds(rows)[0]:
            group = lane_group(count)
            for rr in range(deep):
                tile = jnp.zeros((z.C, LANES), F32)
                for i in range(used):
                    ref, at = places[rr + i * deep]
                    shift = lax.rem((i - src) * count + LANES, LANES)
                    moved = pltpu.roll(ref[at, :, lane : lane + LANES], shift, axis=1)
                    tile = jnp.where(group == i, moved, tile)
                outs[k][base + rr] = tile


def restore_kernel(z, who, *refs):
    B, R, C, mt = z.B, z.R, z.C, z.mt
    got, (spec_out, ocean_out, wide, spec, ocean) = refs[: 2 * B], refs[2 * B :]
    mine = who[0]
    at = 0
    for which, rows in enumerate((z.edge_rows, z.inner_rows)):
        folds, slabs = z.folds(rows)
        for k in range(B):
            c = lax.rem(mine + k, B)
            wide[at : at + slabs, pl.ds(pl.multiple_of(c * C, PAD), C), :] = got[which * B + k][...]
        for half in range(z.W // LANES):
            cols = slice(half * LANES, (half + 1) * LANES)
            for i, r in enumerate(rows):
                for t in range(mt):
                    place = pl.ds(t * LANES * R + r, LANES, stride=R)
                    spec[half, place, :] = wide[at + i * mt + t, cols].T
            for (count, used, deep, base, _), dst, first in zip(folds, (spec, ocean), (z.main, 0)):
                for rr in range(deep):
                    turned = wide[at + base + rr, cols].T
                    for i in range(used):
                        place = pl.ds(first * R + rows[rr + i * deep], count, stride=R)
                        dst[half, place, :] = turned[i * count : (i + 1) * count]
        at += slabs
    for half in range(z.W // LANES):
        cols = slice(half * LANES, (half + 1) * LANES)
        spec_out[:, cols] = spec[half]
        ocean_out[:, cols] = ocean[half]


def weights_kernel(z, linear, square, drift, weights, drift_weights):
    B, nb, main, nr, NB, L = z.B, z.nb, z.main, z.nr, z.NB, z.L

    def put(dst, first, lanes, turned):
        for s in range(B):
            dst[first + s * main : first + (s + 1) * main, lanes] = turned[
                s * nb : s * nb + main
            ]
            tail = first + B * main + s * nr
            dst[tail : tail + nr, lanes] = turned[s * nb + main : (s + 1) * nb]

    for n, source in enumerate((linear, square)):
        for s in range(B):
            for t in range(z.mt):
                block = source[s * nb + t * LANES : s * nb + (t + 1) * LANES, :]
                lane = s * main + t * LANES
                put(weights, n * NB, slice(lane, lane + LANES), block.T)
        tails = [source[s * nb + main : (s + 1) * nb, :] for s in range(B)]
        block = jnp.concatenate(tails, axis=0)
        put(weights, n * NB, slice(B * main, NB), block.T)

    row = lax.broadcasted_iota(jnp.int32, (LANES, LANES), 0)
    lane = lax.broadcasted_iota(jnp.int32, (LANES, LANES), 1)
    part, comp, level = lane // (2 * L), (lane // L) % 2, lane % L
    pick = jnp.where(row == 2 * (part * L + level) + 1 - comp, 1.0, 0.0).astype(BF16)
    turned = jnp.dot(drift[...].T, pick, preferred_element_type=F32).astype(BF16)
    put(drift_weights, 0, slice(0, LANES), turned)


def advance(z, groups, outs, cut, sea_at, sea, speed, weights, drift_weights, moved, moved_twice):
    NB, CH, L = z.NB, z.CH, z.L
    E = groups[0][1][0][0].shape[1]
    N = E - 2 * cut
    keep = slice(cut, cut + N)
    sea_cols = pl.ds(sea_at, E)
    places = [(ref, i) for ref in outs for i in range(ref.shape[0])]

    def sea_row(r):
        return sea[r, sea_cols]

    for g, (sea_first, rows) in enumerate(groups):
        n = len(rows)
        tops = [ref[i, :, NB:CH] for ref, i in rows]
        for r in range(n):
            moved[g, 0, r] = DOPPLER * jnp.tanh(jnp.broadcast_to(tops[r][:, 0:1], (E, LANES)))
            moved[g, 1, r] = DOPPLER * jnp.tanh(jnp.broadcast_to(tops[r][:, L : L + 1], (E, LANES)))

    def advect(g, sea_first, read, write, first, last, speed_cx, speed_cy):
        def along_x(r):
            energy = read(r)
            speed_x = speed_cx + moved[g, 0, r]
            return (
                energy,
                jnp.maximum(speed_x, 0.0) * energy,
                jnp.minimum(speed_x, 0.0) * energy,
            )

        _, plus_before, _ = along_x(first - 1)
        energy, plus, minus = along_x(first)
        for r in range(first, last):
            energy_next, plus_next, minus_next = along_x(r + 1)
            speed_y = speed_cy + moved[g, 1, r]
            plus_y = jnp.maximum(speed_y, 0.0) * energy
            minus_y = jnp.minimum(speed_y, 0.0) * energy
            result = (
                energy
                - ((plus - plus_before) + (minus_next - minus))
                - (
                    (plus_y - pltpu.roll(plus_y, 1, axis=0))
                    + (pltpu.roll(minus_y, E - 1, axis=0) - minus_y)
                )
            )
            write(r, result * sea_row(sea_first + r))
            plus_before, energy, plus, minus = plus, energy_next, plus_next, minus_next

    def one_tile(j, carry):
        lanes = pl.ds(pl.multiple_of(j * LANES, LANES), LANES)
        speed_cx = speed[0:1, lanes]
        speed_cy = speed[1:2, lanes]
        done = 0
        for g, (sea_first, rows) in enumerate(groups):
            n = len(rows)

            def read_state(r):
                ref, i = rows[r]
                return ref[i, :, lanes]

            def write_first(r, value):
                moved[g, 2, r] = value

            def write_second(r, value):
                moved_twice[done + r - 2, :, lanes] = value[keep]

            advect(g, sea_first, read_state, write_first, 1, n - 1, speed_cx, speed_cy)
            advect(
                g, sea_first, lambda r: moved[g, 2, r], write_second, 2, n - 2, speed_cx, speed_cy
            )
            done += n - 4
        return carry

    lax.fori_loop(0, NB // LANES, one_tile, 0)

    count = len(places)
    sea_rows = [f + r for f, rows in groups for r in range(2, len(rows) - 2)]
    energy = moved_twice[...].reshape(count * N, NB)
    squares = energy * energy
    interaction = jnp.dot(
        energy.astype(BF16), weights[:NB], preferred_element_type=F32
    ) + jnp.dot(squares.astype(BF16), weights[NB:], preferred_element_type=F32)
    total = jnp.sum(squares, axis=1, keepdims=True)
    sea_here = jnp.concatenate([sea_row(r)[keep] for r in sea_rows], axis=0)
    scale = (DT_SOURCE * sea_here[:, 0:1]) / (1.0 + total / NB)
    fresh = energy + scale * (interaction * energy)
    for i, (ref, at) in enumerate(places):
        ref[at, :, 0:NB] = fresh[i * N : (i + 1) * N]
    drift = jnp.dot(fresh.astype(BF16), drift_weights[...], preferred_element_type=F32)

    comp = (lax.broadcasted_iota(jnp.int32, (1, LANES), 1) // L) % 2
    sign = jnp.where(comp == 0, 1.0, -1.0).astype(F32)
    i = 0
    for sea_first, rows in groups:
        for r in range(2, len(rows) - 2):
            here, before, after = [
                rows[r + d][0][rows[r + d][1], :, NB:CH] for d in (0, -1, 1)
            ]
            lap = (
                (after + before)
                + (pltpu.roll(here, E - 1, axis=0) + pltpu.roll(here, 1, axis=0))
                - 4.0 * here
            )[keep]
            centre = here[keep]
            other = jnp.where(
                comp == 0, pltpu.roll(centre, LANES - L, axis=1), pltpu.roll(centre, L, axis=1)
            )
            turn = sign * (CORIOLIS * (other + drift[i * N : (i + 1) * N]))
            ref, at = places[i]
            ref[at, :, NB:CH] = (
                centre + DT_OCEAN * (turn + VISCOSITY * lap)
            ) * sea_row(sea_first + r)[keep]
            i += 1


def listed(*refs):
    return [(ref, i) for ref in refs for i in range(ref.shape[0])]


def inner_kernel(z, cut, sea_at, top, inner, bottom, sea, *refs):
    (speed, weights, drift_weights, out, moved, moved_twice) = refs
    groups = [(EDGE, listed(top, inner, bottom))]
    advance(
        z, groups, [out], cut, sea_at, sea, speed, weights, drift_weights, moved, moved_twice
    )


def edge_kernel(z, cut, sea_at, up, top, inner, bottom, down, sea, *refs):
    (speed, weights, drift_weights, new_top, new_bottom, moved, moved_twice) = refs
    inside = listed(inner)
    groups = [
        (0, listed(up, top) + inside[:EDGE]),
        (z.R - EDGE, inside[-EDGE:] + listed(bottom, down)),
    ]
    outs = [new_top, new_bottom]
    advance(
        z, groups, outs, cut, sea_at, sea, speed, weights, drift_weights, moved, moved_twice
    )


def speeds(z):
    lane = jnp.arange(z.NB, dtype=jnp.int32)
    head = (lane // z.main) * z.nb + lane % z.main
    rest = lane - z.B * z.main
    tail = (rest // z.nr) * z.nb + z.main + rest % z.nr
    bin_index = jnp.where(lane < z.B * z.main, head, tail)
    direction = (bin_index // NFREQ).astype(F32)
    frequency = (bin_index % NFREQ).astype(F32)
    group_speed = 0.4 / (1.0 + frequency / 16.0)
    bin_angle = (2.0 * jnp.pi / NDIR) * direction
    zeros = jnp.zeros_like(bin_angle)
    rows = [group_speed * jnp.cos(bin_angle), group_speed * jnp.sin(bin_angle)] + [zeros] * 6
    return jnp.stack(rows)


def cost(flops, moved):
    return pl.CostEstimate(flops=int(flops), bytes_accessed=int(moved), transcendentals=0)


def per_device(G, B, spectrum, sea_mask, kernel_linear, kernel_square, drift_kernel, ocean):
    nb, R, W = spectrum.shape
    L = ocean.shape[1]
    z = Sizes(B, nb, L, R, W)
    C, NB, CH = z.C, z.NB, z.CH
    half = B // 2
    axes = ("geo", "bins")
    geo, part = lax.axis_index("geo"), lax.axis_index("bins")

    def device_at(q, c):
        m, along = c // half, c % half
        along = along if m == 0 else half - 1 - along
        return ((q // 2) * 2 + m) * B + 2 * along + q % 2

    along, odd = part // 2, geo % 2
    tile = geo - odd + part % 2
    share = along + (half + half - 1 - 2 * along) * odd
    forward = [
        [(g * B + b, device_at(g, (b + k) % B)) for g in range(G) for b in range(B)]
        for k in range(B)
    ]
    pairs = [(q, c) for q in range(G) for c in range(B)]
    to_next_row = [(device_at(q, c), device_at((q + 1) % G, c)) for q, c in pairs]
    to_prev_row = [(t, s) for s, t in to_next_row]
    part_id = part.astype(jnp.int32).reshape(1)
    share_id = share.astype(jnp.int32).reshape(1)

    def blocks(width):
        return [
            jax.ShapeDtypeStruct((z.slabs(rows), width, LANES), F32)
            for rows in (z.edge_rows, z.inner_rows)
            for _ in range(B)
        ]

    all_slabs = z.slabs(z.edge_rows) + z.slabs(z.inner_rows)
    columns_scratch = [
        pltpu.VMEM((W // LANES, nb * R, LANES), F32),
        pltpu.VMEM((W // LANES, 2 * L * R, LANES), F32),
    ]
    packed = pl.pallas_call(
        functools.partial(pack_kernel, z),
        out_shape=blocks(C + 2 * PAD),
        in_specs=[SMEM, VMEM, VMEM],
        out_specs=[VMEM] * (2 * B),
        scratch_shapes=columns_scratch + [pltpu.VMEM((all_slabs, W + 2 * PAD, LANES), F32)],
        compiler_params=params(24),
        name="pack",
    )(part_id, spectrum.reshape(nb * R, W), ocean.reshape(2 * L * R, W))
    got = [lax.ppermute(packed[i], axes, forward[i % B]) for i in range(2 * B)]

    def mask_of(offset, block):
        perm = [
            (((q + offset) % G) * B + c, device_at(q, c)) for q in range(G) for c in range(B)
        ]
        return lax.ppermute(block, axes, perm)

    mask = jnp.concatenate(
        [mask_of(-1, sea_mask[R - EDGE :]), mask_of(0, sea_mask), mask_of(1, sea_mask[:EDGE])],
        axis=0,
    )
    mask = jnp.pad(mask, ((0, 0), (PAD, PAD)))
    mask = lax.dynamic_slice_in_dim(mask, share * C, C + 2 * PAD, axis=1)
    sea = jnp.broadcast_to(mask.astype(F32)[..., None], mask.shape + (LANES,))

    weights, drift_weights = pl.pallas_call(
        functools.partial(weights_kernel, z),
        out_shape=(
            jax.ShapeDtypeStruct((2 * NB, NB), BF16),
            jax.ShapeDtypeStruct((NB, LANES), BF16),
        ),
        in_specs=[VMEM] * 3,
        out_specs=(VMEM,) * 2,
        compiler_params=params(24),
        cost_estimate=cost(2e9, 4 * NB * NB * 2),
        name="weights",
    )(kernel_linear, kernel_square, drift_kernel)
    speed = speeds(z)

    def unpack(rows, received, counts):
        return pl.pallas_call(
            functools.partial(unpack_kernel, z, rows),
            out_shape=[jax.ShapeDtypeStruct((n, C + 2 * PAD, CH), F32) for n in counts],
            in_specs=[SMEM] + [VMEM] * B,
            out_specs=[VMEM] * len(counts),
            compiler_params=params(16),
            name="unpack",
        )(share_id, *received)

    top, bottom = unpack(z.edge_rows, got[:B], (EDGE, EDGE))
    (inner,) = unpack(z.inner_rows, got[B:], (R - 2 * EDGE,))

    def step_call(body, width, cut, sea_at, counts, groups, deepest, inputs):
        n = width - 2 * cut
        return pl.pallas_call(
            functools.partial(body, z, cut, sea_at),
            out_shape=[jax.ShapeDtypeStruct((k, n, CH), F32) for k in counts],
            in_specs=[VMEM] * (len(inputs) + 4),
            out_specs=[VMEM] * len(counts),
            scratch_shapes=[
                pltpu.VMEM((groups, 3, deepest, width, LANES), F32),
                pltpu.VMEM((sum(counts), n, NB), F32),
            ],
            compiler_params=params(32),
            cost_estimate=cost(6e9, 8e6),
            name=body.__name__,
        )(*inputs, sea, speed, weights, drift_weights)

    width = C + 2 * PAD
    for step in range(STEPS):
        valid = EDGE * (STEPS - 1 - step)
        margin = (width - C) // 2
        cut = margin - valid if valid == 0 or (margin - valid) % 4 == 0 else 0
        sea_at = PAD - margin
        up = lax.ppermute(bottom, axes, to_next_row)
        down = lax.ppermute(top, axes, to_prev_row)
        (new_inner,) = step_call(
            inner_kernel, width, cut, sea_at, (R - 2 * EDGE,), 1, R, (top, inner, bottom)
        )
        top, bottom = step_call(
            edge_kernel, width, cut, sea_at, (EDGE, EDGE), 2, 3 * EDGE,
            (up, top, inner, bottom, down),
        )
        inner = new_inner
        width -= 2 * cut

    def send_back(rows, states):
        shape = jax.ShapeDtypeStruct((z.slabs(rows), C, LANES), F32)
        return pl.pallas_call(
            functools.partial(send_back_kernel, z, rows),
            out_shape=[shape] * B,
            in_specs=[SMEM] + [VMEM] * len(states),
            out_specs=[VMEM] * B,
            compiler_params=params(16),
            name="send_back",
        )(share_id, *states)

    packed = send_back(z.inner_rows, [inner]), send_back(z.edge_rows, [top, bottom])
    packed = list(packed[1]) + list(packed[0])
    back = [
        lax.ppermute(packed[i], axes, [(t, s) for s, t in forward[i % B]]) for i in range(2 * B)
    ]
    spectrum_out, ocean_out = pl.pallas_call(
        functools.partial(restore_kernel, z),
        out_shape=(
            jax.ShapeDtypeStruct((nb * R, W), F32),
            jax.ShapeDtypeStruct((2 * L * R, W), F32),
        ),
        in_specs=[SMEM] + [VMEM] * (2 * B),
        out_specs=(VMEM,) * 2,
        scratch_shapes=[pltpu.VMEM((all_slabs, W, LANES), F32)] + columns_scratch,
        compiler_params=params(24),
        name="restore",
    )(part_id, *back)
    return spectrum_out.reshape(nb, R, W), ocean_out.reshape(2, L, R, W)


def solution(mesh):
    return jax.shard_map(
        functools.partial(per_device, mesh.shape["geo"], mesh.shape["bins"]),
        mesh=mesh,
        in_specs=(
            P("bins", "geo", None),
            P("geo", None),
            P(),
            P(),
            P(),
            P(None, "bins", "geo", None),
        ),
        out_specs=(P("bins", "geo", None), P(None, "bins", "geo", None)),
        check_vma=False,
    )
```

```python
import functools

import jax
import jax.numpy as jnp
from jax import lax
from jax.experimental import pallas as pl
from jax.experimental.pallas import tpu as pltpu
from jax.sharding import PartitionSpec as P

NDIR = 36
NFREQ = 32
STEPS = 3
SUB = 2
DT_SOURCE = 0.5
DT_OCEAN = 0.2
CORIOLIS = 1.0
VISCOSITY = 1.0
DOPPLER = 0.1

LANES = 128
PAD = 8
EDGE = 2
VMEM = pl.BlockSpec(memory_space=pltpu.VMEM)
SMEM = pl.BlockSpec(memory_space=pltpu.SMEM)
F32 = jnp.float32
BF16 = jnp.bfloat16


def params(mib):
    return pltpu.CompilerParams(vmem_limit_bytes=mib * 1024 * 1024)


class Sizes:
    def __init__(self, parts, bins_here, levels_here, rows, width):
        self.B, self.nb, self.L, self.R, self.W = parts, bins_here, levels_here, rows, width
        self.C = width // parts
        self.mt = bins_here // LANES
        self.main = self.mt * LANES
        self.nr = bins_here - self.main
        self.no = 2 * levels_here
        self.NB = parts * bins_here
        self.CH = self.NB + LANES
        self.edge_rows = (0, 1, rows - 2, rows - 1)
        self.inner_rows = tuple(range(2, rows - 2))
        self.half = parts // 2
        assert self.half & (self.half - 1) == 0 and self.half > 1
        assert self.nr * parts == LANES and self.no * parts == LANES

    def folds(self, rows):
        out, base = [], len(rows) * self.mt
        for count, lane in ((self.nr, self.B * self.main), (self.no, self.NB)):
            used = min(LANES // count, len(rows))
            deep = len(rows) // used
            assert deep * used == len(rows)
            out.append((count, used, deep, base, lane))
            base += deep
        return out, base

    def slabs(self, rows):
        return self.folds(rows)[1]


def exchange_share(z, k, odd, part):
    core = part % 2
    flip, delta = (k // z.half) ^ core, (k % z.half) ^ core
    return (odd ^ flip) * z.half + ((part // 2) ^ delta)


def exchange_part(z, k, odd, part):
    core = (k // z.half) ^ odd ^ (part % 2)
    delta = (k % z.half) ^ core
    return ((part // 2) ^ delta) * 2 + core


def lane_group(width):
    return lax.broadcasted_iota(jnp.int32, (1, LANES), 1) // width


def pack_kernel(z, odd, part, spec_in, ocean_in, mask, *refs):
    B, R, C, W, mt = z.B, z.R, z.C, z.W, z.mt
    outs, (spec, ocean, wide) = refs[: 2 * B], refs[2 * B :]
    E = C + 2 * PAD
    at = 0
    sea = mask[...].astype(F32)
    sea = jnp.concatenate([sea, jnp.zeros((R, LANES), F32)], axis=1)
    for half in range(W // LANES):
        spec[half] = spec_in[:, half * LANES : (half + 1) * LANES]
        ocean[half] = ocean_in[:, half * LANES : (half + 1) * LANES]
    wide[:, 0:PAD, :] = jnp.zeros((wide.shape[0], PAD, LANES), F32)
    wide[:, PAD + W : W + 2 * PAD, :] = jnp.zeros((wide.shape[0], PAD, LANES), F32)
    for which, rows in enumerate((z.edge_rows, z.inner_rows)):
        folds, slabs = z.folds(rows)
        for half in range(W // LANES):
            cols = slice(PAD + half * LANES, PAD + (half + 1) * LANES)
            for i, r in enumerate(rows):
                for t in range(mt):
                    block = spec[half, pl.ds(t * LANES * R + r, LANES, stride=R), :]
                    wide[at + i * mt + t, cols] = block.T
            for (count, used, deep, base, _), src, first in zip(folds, (spec, ocean), (z.main, 0)):
                for rr in range(deep):
                    pieces = [
                        src[half, pl.ds(first * R + rows[rr + i * deep], count, stride=R), :]
                        for i in range(used)
                    ]
                    if used * count < LANES:
                        pieces.append(jnp.zeros((LANES - used * count, LANES), F32))
                    wide[at + base + rr, cols] = jnp.concatenate(pieces, axis=0).T
        for k in range(B):
            out = outs[which * B + k]
            share = exchange_share(z, k, odd[0], part[0])
            start = pl.multiple_of(share * C, PAD)
            block = wide[at : at + slabs, pl.ds(start, E), :]
            out[0 : slabs * E] = block.reshape(slabs * E, LANES)
            if which == 0:
                shift = lax.rem(W + LANES + PAD - start, W + LANES)
                out[slabs * E : slabs * E + R] = pltpu.roll(sea, shift, axis=1)[:, :LANES]
        at += slabs


def unpack_kernel(z, rows, odd, part, *refs):
    B, mt = z.B, z.mt
    got, outs = refs[:B], refs[B:]
    E = z.C + 2 * PAD
    if rows == z.edge_rows:
        sea = outs[-1]
        outs = outs[:-1]
        at = z.slabs(rows) * E
        for r in range(z.R):
            line = jnp.broadcast_to(got[0][at + r : at + r + 1], (LANES, LANES))
            sea[r] = line.T[:E]
        for ref, first in zip(outs, (0, z.R - EDGE)):
            for i in range(EDGE):
                ref[i, :, z.CH :] = sea[first + i]
    places = [(ref, i) for ref in outs for i in range(ref.shape[0])]
    src = [exchange_part(z, k, odd[0], part[0]) for k in range(B)]
    for k in range(B):
        for t in range(mt):
            lanes = pl.ds(pl.multiple_of(src[k] * z.main + t * LANES, LANES), LANES)
            for i, (ref, at) in enumerate(places):
                ref[at, :, lanes] = got[k][(i * mt + t) * E : (i * mt + t + 1) * E]
    for count, used, deep, base, lane in z.folds(rows)[0]:
        group = lane_group(count)
        for i, (ref, at) in enumerate(places):
            tile = jnp.zeros(ref.shape[1:2] + (LANES,), F32)
            for k in range(B):
                shift = lax.rem((src[k] - i // deep) * count + LANES, LANES)
                slab = base + i % deep
                moved = pltpu.roll(got[k][slab * E : (slab + 1) * E], shift, axis=1)
                tile = jnp.where(group == src[k], moved, tile)
            ref[at, :, lane : lane + LANES] = tile


def send_back_kernel(z, rows, odd, part, *refs):
    B, mt = z.B, z.mt
    states, outs = refs[:-B], refs[-B:]
    places = [(ref, i) for ref in states for i in range(ref.shape[0])]
    for k in range(B):
        src = exchange_part(z, k, odd[0], part[0])
        for t in range(mt):
            lanes = pl.ds(pl.multiple_of(src * z.main + t * LANES, LANES), LANES)
            for i, (ref, at) in enumerate(places):
                outs[k][i * mt + t] = ref[at, :, lanes]
        for count, used, deep, base, lane in z.folds(rows)[0]:
            group = lane_group(count)
            for rr in range(deep):
                tile = jnp.zeros((z.C, LANES), F32)
                for i in range(used):
                    ref, at = places[rr + i * deep]
                    shift = lax.rem((i - src) * count + LANES, LANES)
                    moved = pltpu.roll(ref[at, :, lane : lane + LANES], shift, axis=1)
                    tile = jnp.where(group == i, moved, tile)
                outs[k][base + rr] = tile


def restore_kernel(z, odd, part, *refs):
    B, R, C, mt = z.B, z.R, z.C, z.mt
    got, (spec_out, ocean_out, wide, spec, ocean) = refs[: 2 * B], refs[2 * B :]
    at = 0
    for which, rows in enumerate((z.edge_rows, z.inner_rows)):
        folds, slabs = z.folds(rows)
        for k in range(B):
            c = exchange_share(z, k, odd[0], part[0])
            wide[at : at + slabs, pl.ds(pl.multiple_of(c * C, PAD), C), :] = got[which * B + k][...]
        for half in range(z.W // LANES):
            cols = slice(half * LANES, (half + 1) * LANES)
            for i, r in enumerate(rows):
                for t in range(mt):
                    place = pl.ds(t * LANES * R + r, LANES, stride=R)
                    spec[half, place, :] = wide[at + i * mt + t, cols].T
            for (count, used, deep, base, _), dst, first in zip(folds, (spec, ocean), (z.main, 0)):
                for rr in range(deep):
                    turned = wide[at + base + rr, cols].T
                    for i in range(used):
                        place = pl.ds(first * R + rows[rr + i * deep], count, stride=R)
                        dst[half, place, :] = turned[i * count : (i + 1) * count]
        at += slabs
    for half in range(z.W // LANES):
        cols = slice(half * LANES, (half + 1) * LANES)
        spec_out[:, cols] = spec[half]
        ocean_out[:, cols] = ocean[half]


def weights_kernel(z, linear, square, drift, weights, drift_weights):
    B, nb, main, nr, NB, L = z.B, z.nb, z.main, z.nr, z.NB, z.L

    def put(dst, first, lanes, turned):
        for s in range(B):
            dst[first + s * main : first + (s + 1) * main, lanes] = turned[
                s * nb : s * nb + main
            ]
            tail = first + B * main + s * nr
            dst[tail : tail + nr, lanes] = turned[s * nb + main : (s + 1) * nb]

    for n, source in enumerate((linear, square)):
        for s in range(B):
            for t in range(z.mt):
                block = source[s * nb + t * LANES : s * nb + (t + 1) * LANES, :]
                lane = s * main + t * LANES
                put(weights, n * NB, slice(lane, lane + LANES), block.T)
        tails = [source[s * nb + main : (s + 1) * nb, :] for s in range(B)]
        block = jnp.concatenate(tails, axis=0)
        put(weights, n * NB, slice(B * main, NB), block.T)

    row = lax.broadcasted_iota(jnp.int32, (LANES, LANES), 0)
    lane = lax.broadcasted_iota(jnp.int32, (LANES, LANES), 1)
    part, comp, level = lane // (2 * L), (lane // L) % 2, lane % L
    pick = jnp.where(row == 2 * (part * L + level) + 1 - comp, 1.0, 0.0).astype(BF16)
    turned = jnp.dot(drift[...].T, pick, preferred_element_type=F32).astype(BF16)
    put(drift_weights, 0, slice(0, LANES), turned)


def advance(z, groups, outs, cut, sea_at, speed, weights, drift_weights, moved, moved_twice):
    NB, CH, L = z.NB, z.CH, z.L
    E = groups[0][1][0][0].shape[1]
    N = E - 2 * cut
    keep = slice(cut, cut + N)
    sea_cols = pl.ds(sea_at, E)
    places = [(ref, i) for ref in outs for i in range(ref.shape[0])]

    def sea_row(place):
        return place[0][place[1], sea_cols]

    for g, (sea_rows, rows) in enumerate(groups):
        n = len(rows)
        tops = [ref[i, :, NB:CH] for ref, i in rows]
        for r in range(n):
            moved[g, 0, r] = DOPPLER * jnp.tanh(jnp.broadcast_to(tops[r][:, 0:1], (E, LANES)))
            moved[g, 1, r] = DOPPLER * jnp.tanh(jnp.broadcast_to(tops[r][:, L : L + 1], (E, LANES)))

    def advect(g, sea_rows, read, write, first, last, speed_cx, speed_cy):
        def along_x(r):
            energy = read(r)
            speed_x = speed_cx + moved[g, 0, r]
            return (
                energy,
                jnp.maximum(speed_x, 0.0) * energy,
                jnp.minimum(speed_x, 0.0) * energy,
            )

        _, plus_before, _ = along_x(first - 1)
        energy, plus, minus = along_x(first)
        for r in range(first, last):
            energy_next, plus_next, minus_next = along_x(r + 1)
            speed_y = speed_cy + moved[g, 1, r]
            plus_y = jnp.maximum(speed_y, 0.0) * energy
            minus_y = jnp.minimum(speed_y, 0.0) * energy
            result = (
                energy
                - ((plus - plus_before) + (minus_next - minus))
                - (
                    (plus_y - pltpu.roll(plus_y, 1, axis=0))
                    + (pltpu.roll(minus_y, E - 1, axis=0) - minus_y)
                )
            )
            write(r, result * sea_row(sea_rows[r]))
            plus_before, energy, plus, minus = plus, energy_next, plus_next, minus_next

    def one_tile(j, carry):
        lanes = pl.ds(pl.multiple_of(j * LANES, LANES), LANES)
        speed_cx = speed[0:1, lanes]
        speed_cy = speed[1:2, lanes]
        done = 0
        for g, (sea_rows, rows) in enumerate(groups):
            n = len(rows)

            def read_state(r):
                ref, i = rows[r]
                return ref[i, :, lanes]

            def write_first(r, value):
                moved[g, 2, r] = value

            def write_second(r, value):
                moved_twice[done + r - 2, :, lanes] = value[keep]

            advect(g, sea_rows, read_state, write_first, 1, n - 1, speed_cx, speed_cy)
            advect(
                g, sea_rows, lambda r: moved[g, 2, r], write_second, 2, n - 2, speed_cx, speed_cy
            )
            done += n - 4
        return carry

    lax.fori_loop(0, NB // LANES, one_tile, 0)

    count = len(places)
    own_sea = [place for sea_rows, rows in groups for place in sea_rows[2 : len(rows) - 2]]
    energy = moved_twice[...].reshape(count * N, NB)
    squares = energy * energy
    interaction = jnp.dot(
        energy.astype(BF16), weights[:NB], preferred_element_type=F32
    ) + jnp.dot(squares.astype(BF16), weights[NB:], preferred_element_type=F32)
    total = jnp.sum(squares, axis=1, keepdims=True)
    sea_here = jnp.concatenate([sea_row(place)[keep] for place in own_sea], axis=0)
    scale = (DT_SOURCE * sea_here[:, 0:1]) / (1.0 + total / NB)
    fresh = energy + scale * (interaction * energy)
    for i, (ref, at) in enumerate(places):
        ref[at, :, 0:NB] = fresh[i * N : (i + 1) * N]
    drift = jnp.dot(fresh.astype(BF16), drift_weights[...], preferred_element_type=F32)

    comp = (lax.broadcasted_iota(jnp.int32, (1, LANES), 1) // L) % 2
    sign = jnp.where(comp == 0, 1.0, -1.0).astype(F32)
    i = 0
    for _, rows in groups:
        for r in range(2, len(rows) - 2):
            here, before, after = [
                rows[r + d][0][rows[r + d][1], :, NB:CH] for d in (0, -1, 1)
            ]
            lap = (
                (after + before)
                + (pltpu.roll(here, E - 1, axis=0) + pltpu.roll(here, 1, axis=0))
                - 4.0 * here
            )[keep]
            centre = here[keep]
            other = jnp.where(
                comp == 0, pltpu.roll(centre, LANES - L, axis=1), pltpu.roll(centre, L, axis=1)
            )
            turn = sign * (CORIOLIS * (other + drift[i * N : (i + 1) * N]))
            ref, at = places[i]
            ref[at, :, NB:CH] = (
                centre + DT_OCEAN * (turn + VISCOSITY * lap)
            ) * sea_row(own_sea[i])[keep]
            i += 1


def listed(*refs):
    return [(ref, i) for ref in refs for i in range(ref.shape[0])]


def inner_kernel(z, cut, sea_at, top, inner, bottom, sea, *refs):
    (speed, weights, drift_weights, out, moved, moved_twice) = refs
    groups = [(listed(sea), listed(top, inner, bottom))]
    advance(z, groups, [out], cut, sea_at, speed, weights, drift_weights, moved, moved_twice)


def edge_kernel(z, cut, sea_at, up, top, inner, bottom, down, sea_up, sea, sea_down, *refs):
    (speed, weights, drift_weights, new_top, new_bottom, moved, moved_twice) = refs
    inside = listed(inner)
    sea_rows = listed(sea_up, sea, sea_down)
    groups = [
        (sea_rows[: 3 * EDGE], listed(up, top) + inside[:EDGE]),
        (sea_rows[-3 * EDGE :], inside[-EDGE:] + listed(bottom, down)),
    ]
    outs = [new_top, new_bottom]
    advance(z, groups, outs, cut, sea_at, speed, weights, drift_weights, moved, moved_twice)


def speeds(z):
    lane = jnp.arange(z.NB, dtype=jnp.int32)
    head = (lane // z.main) * z.nb + lane % z.main
    rest = lane - z.B * z.main
    tail = (rest // z.nr) * z.nb + z.main + rest % z.nr
    bin_index = jnp.where(lane < z.B * z.main, head, tail)
    direction = (bin_index // NFREQ).astype(F32)
    frequency = (bin_index % NFREQ).astype(F32)
    group_speed = 0.4 / (1.0 + frequency / 16.0)
    bin_angle = (2.0 * jnp.pi / NDIR) * direction
    zeros = jnp.zeros_like(bin_angle)
    rows = [group_speed * jnp.cos(bin_angle), group_speed * jnp.sin(bin_angle)] + [zeros] * 6
    return jnp.stack(rows)


def cost(flops, moved):
    return pl.CostEstimate(flops=int(flops), bytes_accessed=int(moved), transcendentals=0)


def per_device(G, B, spectrum, sea_mask, kernel_linear, kernel_square, drift_kernel, ocean):
    nb, R, W = spectrum.shape
    L = ocean.shape[1]
    z = Sizes(B, nb, L, R, W)
    C, NB, CH = z.C, z.NB, z.CH
    half = B // 2
    axes = ("geo", "bins")
    geo, part = lax.axis_index("geo"), lax.axis_index("bins")

    def device_at(q, c):
        return ((q // 2) * 2 + c // half) * B + 2 * (c % half) + q % 2

    forward = [
        [
            (g * B + b, device_at(g, exchange_share(z, k, g % 2, b)))
            for g in range(G)
            for b in range(B)
        ]
        for k in range(B)
    ]
    pairs = [(q, c) for q in range(G) for c in range(B)]
    to_next_row = [(device_at(q, c), device_at((q + 1) % G, c)) for q, c in pairs]
    to_prev_row = [(t, s) for s, t in to_next_row]
    who = ((geo % 2).astype(jnp.int32).reshape(1), part.astype(jnp.int32).reshape(1))

    width = C + 2 * PAD
    blocks = [
        jax.ShapeDtypeStruct((z.slabs(rows) * width + more, LANES), F32)
        for rows, more in ((z.edge_rows, R), (z.inner_rows, 0))
        for _ in range(B)
    ]
    all_slabs = z.slabs(z.edge_rows) + z.slabs(z.inner_rows)
    columns_scratch = [
        pltpu.VMEM((W // LANES, nb * R, LANES), F32),
        pltpu.VMEM((W // LANES, 2 * L * R, LANES), F32),
    ]
    packed = pl.pallas_call(
        functools.partial(pack_kernel, z),
        out_shape=blocks,
        in_specs=[SMEM] * 2 + [VMEM] * 3,
        out_specs=[VMEM] * (2 * B),
        scratch_shapes=columns_scratch + [pltpu.VMEM((all_slabs, W + 2 * PAD, LANES), F32)],
        compiler_params=params(24),
        name="pack",
    )(*who, spectrum.reshape(nb * R, W), ocean.reshape(2 * L * R, W), sea_mask)
    got = [lax.ppermute(packed[i], axes, forward[i % B]) for i in range(2 * B)]

    weights, drift_weights = pl.pallas_call(
        functools.partial(weights_kernel, z),
        out_shape=(
            jax.ShapeDtypeStruct((2 * NB, NB), BF16),
            jax.ShapeDtypeStruct((NB, LANES), BF16),
        ),
        in_specs=[VMEM] * 3,
        out_specs=(VMEM,) * 2,
        compiler_params=params(24),
        cost_estimate=cost(2e9, 4 * NB * NB * 2),
        name="weights",
    )(kernel_linear, kernel_square, drift_kernel)
    speed = speeds(z)

    def unpack(rows, received, shapes):
        return pl.pallas_call(
            functools.partial(unpack_kernel, z, rows),
            out_shape=[jax.ShapeDtypeStruct((n, width, lanes), F32) for n, lanes in shapes],
            in_specs=[SMEM] * 2 + [VMEM] * B,
            out_specs=[VMEM] * len(shapes),
            compiler_params=params(16),
            name="unpack",
        )(*who, *received)

    top, bottom, sea = unpack(
        z.edge_rows, got[:B], [(EDGE, CH + LANES), (EDGE, CH + LANES), (R, LANES)]
    )
    (inner,) = unpack(z.inner_rows, got[B:], [(R - 2 * EDGE, CH)])

    def step_call(body, width, cut, sea_at, counts, groups, deepest, inputs):
        n = width - 2 * cut
        return pl.pallas_call(
            functools.partial(body, z, cut, sea_at),
            out_shape=[jax.ShapeDtypeStruct((k, n, CH), F32) for k in counts],
            in_specs=[VMEM] * (len(inputs) + 3),
            out_specs=[VMEM] * len(counts),
            scratch_shapes=[
                pltpu.VMEM((groups, 3, deepest, width, LANES), F32),
                pltpu.VMEM((sum(counts), n, NB), F32),
            ],
            compiler_params=params(32),
            cost_estimate=cost(6e9, 8e6),
            name=body.__name__,
        )(*inputs, speed, weights, drift_weights)

    for step in range(STEPS):
        valid = EDGE * (STEPS - 1 - step)
        margin = (width - C) // 2
        cut = margin - valid if valid == 0 or (margin - valid) % 4 == 0 else 0
        sea_at = PAD - margin
        up = lax.ppermute(bottom, axes, to_next_row)
        down = lax.ppermute(top, axes, to_prev_row)
        (new_inner,) = step_call(
            inner_kernel, width, cut, sea_at, (R - 2 * EDGE,), 1, R, (top, inner, bottom, sea)
        )
        if step == 0:
            sea_up, sea_down = up[:, :, CH:], down[:, :, CH:]
        top, bottom = step_call(
            edge_kernel, width, cut, sea_at, (EDGE, EDGE), 2, 3 * EDGE,
            (up, top, inner, bottom, down, sea_up, sea, sea_down),
        )
        inner = new_inner
        width -= 2 * cut

    def send_back(rows, states):
        shape = jax.ShapeDtypeStruct((z.slabs(rows), C, LANES), F32)
        return pl.pallas_call(
            functools.partial(send_back_kernel, z, rows),
            out_shape=[shape] * B,
            in_specs=[SMEM] * 2 + [VMEM] * len(states),
            out_specs=[VMEM] * B,
            compiler_params=params(16),
            name="send_back",
        )(*who, *states)

    packed = send_back(z.inner_rows, [inner]), send_back(z.edge_rows, [top, bottom])
    packed = list(packed[1]) + list(packed[0])
    back = [
        lax.ppermute(packed[i], axes, [(t, s) for s, t in forward[i % B]]) for i in range(2 * B)
    ]
    spectrum_out, ocean_out = pl.pallas_call(
        functools.partial(restore_kernel, z),
        out_shape=(
            jax.ShapeDtypeStruct((nb * R, W), F32),
            jax.ShapeDtypeStruct((2 * L * R, W), F32),
        ),
        in_specs=[SMEM] * 2 + [VMEM] * (2 * B),
        out_specs=(VMEM,) * 2,
        scratch_shapes=[pltpu.VMEM((all_slabs, W, LANES), F32)] + columns_scratch,
        compiler_params=params(24),
        name="restore",
    )(*who, *back)
    return spectrum_out.reshape(nb, R, W), ocean_out.reshape(2, L, R, W)


def solution(mesh):
    return jax.shard_map(
        functools.partial(per_device, mesh.shape["geo"], mesh.shape["bins"]),
        mesh=mesh,
        in_specs=(
            P("bins", "geo", None),
            P("geo", None),
            P(),
            P(),
            P(),
            P(None, "bins", "geo", None),
        ),
        out_specs=(P("bins", "geo", None), P(None, "bins", "geo", None)),
        check_vma=False,
    )
```

```python
import functools

import jax
import jax.numpy as jnp
from jax import lax
from jax.experimental import pallas as pl
from jax.experimental.pallas import tpu as pltpu
from jax.sharding import PartitionSpec as P

NDIR = 36
NFREQ = 32
STEPS = 3
SUB = 2
DT_SOURCE = 0.5
DT_OCEAN = 0.2
CORIOLIS = 1.0
VISCOSITY = 1.0
DOPPLER = 0.1

LANES = 128
PAD = 8
EDGE = 2
VMEM = pl.BlockSpec(memory_space=pltpu.VMEM)
SMEM = pl.BlockSpec(memory_space=pltpu.SMEM)
ANY = pl.BlockSpec(memory_space=pl.ANY)
F32 = jnp.float32
BF16 = jnp.bfloat16


def params(mib):
    return pltpu.CompilerParams(vmem_limit_bytes=mib * 1024 * 1024)


class Sizes:
    def __init__(self, parts, bins_here, levels_here, rows, width):
        self.B, self.nb, self.L, self.R, self.W = parts, bins_here, levels_here, rows, width
        self.C = width // parts
        self.mt = bins_here // LANES
        self.main = self.mt * LANES
        self.nr = bins_here - self.main
        self.no = 2 * levels_here
        self.NB = parts * bins_here
        self.CH = self.NB + LANES
        self.edge_rows = (0, 1, rows - 2, rows - 1)
        self.inner_rows = tuple(range(2, rows - 2))
        self.half = parts // 2
        assert self.half & (self.half - 1) == 0 and self.half > 1
        assert self.nr * parts == LANES and self.no * parts == LANES

    def folds(self, rows):
        out, base = [], len(rows) * self.mt
        for count, lane in ((self.nr, self.B * self.main), (self.no, self.NB)):
            used = min(LANES // count, len(rows))
            deep = len(rows) // used
            assert deep * used == len(rows)
            out.append((count, used, deep, base, lane))
            base += deep
        return out, base

    def slabs(self, rows):
        return self.folds(rows)[1]


def exchange_share(z, k, odd, part):
    core = part % 2
    flip, delta = (k // z.half) ^ core, (k % z.half) ^ core
    return (odd ^ flip) * z.half + ((part // 2) ^ delta)


def exchange_part(z, k, odd, part):
    core = (k // z.half) ^ odd ^ (part % 2)
    delta = (k % z.half) ^ core
    return ((part // 2) ^ delta) * 2 + core


def lane_group(width):
    return lax.broadcasted_iota(jnp.int32, (1, LANES), 1) // width


def pack_kernel(z, odd, part, spec_in, ocean_in, mask, *refs):
    B, R, C, W, mt = z.B, z.R, z.C, z.W, z.mt
    outs, (spec, ocean, wide) = refs[: 2 * B], refs[2 * B :]
    E = C + 2 * PAD
    at = 0
    sea = mask[...].astype(F32)
    sea = jnp.concatenate([sea, jnp.zeros((R, LANES), F32)], axis=1)
    for half in range(W // LANES):
        spec[half] = spec_in[:, half * LANES : (half + 1) * LANES]
        ocean[half] = ocean_in[:, half * LANES : (half + 1) * LANES]
    wide[:, 0:PAD, :] = jnp.zeros((wide.shape[0], PAD, LANES), F32)
    wide[:, PAD + W : W + 2 * PAD, :] = jnp.zeros((wide.shape[0], PAD, LANES), F32)
    for which, rows in enumerate((z.edge_rows, z.inner_rows)):
        folds, slabs = z.folds(rows)
        for half in range(W // LANES):
            cols = slice(PAD + half * LANES, PAD + (half + 1) * LANES)
            for i, r in enumerate(rows):
                for t in range(mt):
                    block = spec[half, pl.ds(t * LANES * R + r, LANES, stride=R), :]
                    wide[at + i * mt + t, cols] = block.T
            for (count, used, deep, base, _), src, first in zip(folds, (spec, ocean), (z.main, 0)):
                for rr in range(deep):
                    pieces = [
                        src[half, pl.ds(first * R + rows[rr + i * deep], count, stride=R), :]
                        for i in range(used)
                    ]
                    if used * count < LANES:
                        pieces.append(jnp.zeros((LANES - used * count, LANES), F32))
                    wide[at + base + rr, cols] = jnp.concatenate(pieces, axis=0).T
        for k in range(B):
            out = outs[which * B + k]
            share = exchange_share(z, k, odd[0], part[0])
            start = pl.multiple_of(share * C, PAD)
            block = wide[at : at + slabs, pl.ds(start, E), :]
            out[0 : slabs * E] = block.reshape(slabs * E, LANES)
            if which == 0:
                shift = lax.rem(W + LANES + PAD - start, W + LANES)
                out[slabs * E : slabs * E + R] = pltpu.roll(sea, shift, axis=1)[:, :LANES]
        at += slabs


def unpack_kernel(z, rows, odd, part, *refs):
    B, mt = z.B, z.mt
    got, outs = refs[:B], refs[B:]
    E = z.C + 2 * PAD
    if rows == z.edge_rows:
        outs = outs[1:]
        sea = outs[-1]
        outs = outs[:-1]
        at = z.slabs(rows) * E
        for r in range(z.R):
            line = jnp.broadcast_to(got[0][at + r : at + r + 1], (LANES, LANES))
            sea[r] = line.T[:E]
        for ref, first in zip(outs, (0, z.R - EDGE)):
            for i in range(EDGE):
                ref[i, :, z.CH :] = sea[first + i]
    places = [(ref, i) for ref in outs for i in range(ref.shape[0])]
    src = [exchange_part(z, k, odd[0], part[0]) for k in range(B)]
    for k in range(B):
        for t in range(mt):
            lanes = pl.ds(pl.multiple_of(src[k] * z.main + t * LANES, LANES), LANES)
            for i, (ref, at) in enumerate(places):
                ref[at, :, lanes] = got[k][(i * mt + t) * E : (i * mt + t + 1) * E]
    for count, used, deep, base, lane in z.folds(rows)[0]:
        group = lane_group(count)
        for i, (ref, at) in enumerate(places):
            tile = jnp.zeros(ref.shape[1:2] + (LANES,), F32)
            for k in range(B):
                shift = lax.rem((src[k] - i // deep) * count + LANES, LANES)
                slab = base + i % deep
                moved = pltpu.roll(got[k][slab * E : (slab + 1) * E], shift, axis=1)
                tile = jnp.where(group == src[k], moved, tile)
            ref[at, :, lane : lane + LANES] = tile


def send_back_kernel(z, rows, odd, part, *refs):
    B, mt = z.B, z.mt
    states, outs = refs[:-B], refs[-B:]
    places = [(ref, i) for ref in states for i in range(ref.shape[0])]
    for k in range(B):
        src = exchange_part(z, k, odd[0], part[0])
        for t in range(mt):
            lanes = pl.ds(pl.multiple_of(src * z.main + t * LANES, LANES), LANES)
            for i, (ref, at) in enumerate(places):
                outs[k][i * mt + t] = ref[at, :, lanes]
        for count, used, deep, base, lane in z.folds(rows)[0]:
            group = lane_group(count)
            for rr in range(deep):
                tile = jnp.zeros((z.C, LANES), F32)
                for i in range(used):
                    ref, at = places[rr + i * deep]
                    shift = lax.rem((i - src) * count + LANES, LANES)
                    moved = pltpu.roll(ref[at, :, lane : lane + LANES], shift, axis=1)
                    tile = jnp.where(group == i, moved, tile)
                outs[k][base + rr] = tile


def restore_kernel(z, odd, part, *refs):
    B, R, C, mt = z.B, z.R, z.C, z.mt
    got, (spec_out, ocean_out, wide, spec, ocean) = refs[: 2 * B], refs[2 * B :]
    at = 0
    for which, rows in enumerate((z.edge_rows, z.inner_rows)):
        folds, slabs = z.folds(rows)
        for k in range(B):
            c = exchange_share(z, k, odd[0], part[0])
            wide[at : at + slabs, pl.ds(pl.multiple_of(c * C, PAD), C), :] = got[which * B + k][...]
        for half in range(z.W // LANES):
            cols = slice(half * LANES, (half + 1) * LANES)
            for i, r in enumerate(rows):
                for t in range(mt):
                    place = pl.ds(t * LANES * R + r, LANES, stride=R)
                    spec[half, place, :] = wide[at + i * mt + t, cols].T
            for (count, used, deep, base, _), dst, first in zip(folds, (spec, ocean), (z.main, 0)):
                for rr in range(deep):
                    turned = wide[at + base + rr, cols].T
                    for i in range(used):
                        place = pl.ds(first * R + rows[rr + i * deep], count, stride=R)
                        dst[half, place, :] = turned[i * count : (i + 1) * count]
        at += slabs
    for half in range(z.W // LANES):
        cols = slice(half * LANES, (half + 1) * LANES)
        spec_out[:, cols] = spec[half]
        ocean_out[:, cols] = ocean[half]


def weights_kernel(z, linear, square, drift, weights, drift_weights):
    B, nb, main, nr, NB, L = z.B, z.nb, z.main, z.nr, z.NB, z.L

    def put(dst, first, lanes, turned):
        for s in range(B):
            dst[first + s * main : first + (s + 1) * main, lanes] = turned[
                s * nb : s * nb + main
            ]
            tail = first + B * main + s * nr
            dst[tail : tail + nr, lanes] = turned[s * nb + main : (s + 1) * nb]

    for n, source in enumerate((linear, square)):
        for s in range(B):
            for t in range(z.mt):
                block = source[s * nb + t * LANES : s * nb + (t + 1) * LANES, :]
                lane = s * main + t * LANES
                put(weights, n * NB, slice(lane, lane + LANES), block.T)
        tails = [source[s * nb + main : (s + 1) * nb, :] for s in range(B)]
        block = jnp.concatenate(tails, axis=0)
        put(weights, n * NB, slice(B * main, NB), block.T)

    row = lax.broadcasted_iota(jnp.int32, (LANES, LANES), 0)
    lane = lax.broadcasted_iota(jnp.int32, (LANES, LANES), 1)
    part, comp, level = lane // (2 * L), (lane // L) % 2, lane % L
    pick = jnp.where(row == 2 * (part * L + level) + 1 - comp, 1.0, 0.0).astype(BF16)
    turned = jnp.dot(drift[...].T, pick, preferred_element_type=F32).astype(BF16)
    put(drift_weights, 0, slice(0, LANES), turned)


def advance(
    z, sea_rows, rows, outs, cut, sea_at, speed, weights, drift_weights, moved, moved_twice,
    known=None, kept=None,
):
    NB, CH, L = z.NB, z.CH, z.L
    known, kept = known or {}, kept or {}
    n = len(rows)
    first = [r for r in range(1, n - 1) if r not in known]
    assert first == list(range(first[0], first[-1] + 1))
    E = rows[0][0].shape[1]
    N = E - 2 * cut
    keep = slice(cut, cut + N)
    sea_cols = pl.ds(sea_at, E)
    places = [(ref, i) for ref in outs for i in range(ref.shape[0])]

    def sea_row(place):
        return place[0][place[1], sea_cols]

    for r in range(min(first[0] - 1, 1), max(first[-1] + 2, n - 1)):
        ref, i = rows[r]
        surface = ref[i, :, NB:CH]
        moved[0, r] = DOPPLER * jnp.tanh(jnp.broadcast_to(surface[:, 0:1], (E, LANES)))
        moved[1, r] = DOPPLER * jnp.tanh(jnp.broadcast_to(surface[:, L : L + 1], (E, LANES)))

    def advect(read, write, start, stop, speed_cx, speed_cy):
        def along_x(r):
            energy = read(r)
            speed_x = speed_cx + moved[0, r]
            return (
                energy,
                jnp.maximum(speed_x, 0.0) * energy,
                jnp.minimum(speed_x, 0.0) * energy,
            )

        _, plus_before, _ = along_x(start - 1)
        energy, plus, minus = along_x(start)
        for r in range(start, stop):
            energy_next, plus_next, minus_next = along_x(r + 1)
            speed_y = speed_cy + moved[1, r]
            plus_y = jnp.maximum(speed_y, 0.0) * energy
            minus_y = jnp.minimum(speed_y, 0.0) * energy
            result = (
                energy
                - ((plus - plus_before) + (minus_next - minus))
                - (
                    (plus_y - pltpu.roll(plus_y, 1, axis=0))
                    + (pltpu.roll(minus_y, E - 1, axis=0) - minus_y)
                )
            )
            write(r, result * sea_row(sea_rows[r]))
            plus_before, energy, plus, minus = plus, energy_next, plus_next, minus_next

    def one_tile(j, carry):
        lanes = pl.ds(pl.multiple_of(j * LANES, LANES), LANES)
        speed_cx = speed[0:1, lanes]
        speed_cy = speed[1:2, lanes]

        def read_first(r):
            ref, i = rows[r]
            return ref[i, :, lanes]

        def write_first(r, value):
            moved[2, r] = value
            if r in kept:
                ref, i = kept[r]
                ref[i, :, lanes] = value

        def read_second(r):
            if r in known:
                ref, i = known[r]
                return ref[i, :, lanes]
            return moved[2, r]

        def write_second(r, value):
            moved_twice[r - 2, :, lanes] = value[keep]

        advect(read_first, write_first, first[0], first[-1] + 1, speed_cx, speed_cy)
        advect(read_second, write_second, 2, n - 2, speed_cx, speed_cy)
        return carry

    lax.fori_loop(0, NB // LANES, one_tile, 0)

    count = len(places)
    own_sea = sea_rows[2 : n - 2]
    energy = moved_twice[...].reshape(count * N, NB)
    squares = energy * energy
    interaction = jnp.dot(
        energy.astype(BF16), weights[:NB], preferred_element_type=F32
    ) + jnp.dot(squares.astype(BF16), weights[NB:], preferred_element_type=F32)
    total = jnp.sum(squares, axis=1, keepdims=True)
    sea_here = jnp.concatenate([sea_row(place)[keep] for place in own_sea], axis=0)
    scale = (DT_SOURCE * sea_here[:, 0:1]) / (1.0 + total / NB)
    fresh = energy + scale * (interaction * energy)
    for i, (ref, at) in enumerate(places):
        ref[at, :, 0:NB] = fresh[i * N : (i + 1) * N]
    drift = jnp.dot(fresh.astype(BF16), drift_weights[...], preferred_element_type=F32)

    comp = (lax.broadcasted_iota(jnp.int32, (1, LANES), 1) // L) % 2
    sign = jnp.where(comp == 0, 1.0, -1.0).astype(F32)
    for i, (out, at) in enumerate(places):
        here, before, after = [
            ref[row, :, NB:CH] for ref, row in (rows[i + 2], rows[i + 1], rows[i + 3])
        ]
        lap = (
            (after + before)
            + (pltpu.roll(here, E - 1, axis=0) + pltpu.roll(here, 1, axis=0))
            - 4.0 * here
        )[keep]
        centre = here[keep]
        other = jnp.where(
            comp == 0, pltpu.roll(centre, LANES - L, axis=1), pltpu.roll(centre, L, axis=1)
        )
        turn = sign * (CORIOLIS * (other + drift[i * N : (i + 1) * N]))
        out[at, :, NB:CH] = (
            centre + DT_OCEAN * (turn + VISCOSITY * lap)
        ) * sea_row(own_sea[i])[keep]


def listed(*refs):
    return [(ref, i) for ref in refs for i in range(ref.shape[0])]


def inner_kernel(z, cut, sea_at, top, inner, bottom, sea, speed, weights, drift_weights, *refs):
    out, for_edges, (moved, moved_twice) = refs[0], refs[1:-2], refs[-2:]
    kept = {}
    if for_edges:
        kept = {1 + i: (for_edges[0], i) for i in range(EDGE)}
        kept |= {z.R - 1 - EDGE + i: (for_edges[1], i) for i in range(EDGE)}
    advance(
        z, listed(sea), listed(top, inner, bottom), [out], cut, sea_at, speed, weights,
        drift_weights, moved, moved_twice, kept=kept,
    )


def top_kernel(z, cut, sea_at, up, top, inner, sea_up, sea, *refs):
    given, (speed, weights, drift_weights, out, moved, moved_twice) = refs[:-6], refs[-6:]
    known = {3 + i: (given[0], i) for i in range(EDGE)} if given else {}
    rows = listed(up, top) + listed(inner)[:EDGE]
    sea_rows = (listed(sea_up) + listed(sea))[: len(rows)]
    advance(
        z, sea_rows, rows, [out], cut, sea_at, speed, weights, drift_weights, moved,
        moved_twice, known=known,
    )


def bottom_kernel(z, cut, sea_at, down, bottom, inner, sea_down, sea, *refs):
    given, (speed, weights, drift_weights, out, moved, moved_twice) = refs[:-6], refs[-6:]
    known = {1 + i: (given[0], i) for i in range(EDGE)} if given else {}
    rows = listed(inner)[-EDGE:] + listed(bottom, down)
    sea_rows = (listed(sea) + listed(sea_down))[-len(rows) :]
    advance(
        z, sea_rows, rows, [out], cut, sea_at, speed, weights, drift_weights, moved,
        moved_twice, known=known,
    )


def speeds(z):
    lane = jnp.arange(z.NB, dtype=jnp.int32)
    head = (lane // z.main) * z.nb + lane % z.main
    rest = lane - z.B * z.main
    tail = (rest // z.nr) * z.nb + z.main + rest % z.nr
    bin_index = jnp.where(lane < z.B * z.main, head, tail)
    direction = (bin_index // NFREQ).astype(F32)
    frequency = (bin_index % NFREQ).astype(F32)
    group_speed = 0.4 / (1.0 + frequency / 16.0)
    bin_angle = (2.0 * jnp.pi / NDIR) * direction
    zeros = jnp.zeros_like(bin_angle)
    rows = [group_speed * jnp.cos(bin_angle), group_speed * jnp.sin(bin_angle)] + [zeros] * 6
    return jnp.stack(rows)


def cost(flops, moved):
    return pl.CostEstimate(flops=int(flops), bytes_accessed=int(moved), transcendentals=0)


def per_device(G, B, spectrum, sea_mask, kernel_linear, kernel_square, drift_kernel, ocean):
    nb, R, W = spectrum.shape
    L = ocean.shape[1]
    z = Sizes(B, nb, L, R, W)
    C, NB, CH = z.C, z.NB, z.CH
    half = B // 2
    axes = ("geo", "bins")
    geo, part = lax.axis_index("geo"), lax.axis_index("bins")

    def device_at(q, c):
        return ((q // 2) * 2 + c // half) * B + 2 * (c % half) + q % 2

    forward = [
        [
            (g * B + b, device_at(g, exchange_share(z, k, g % 2, b)))
            for g in range(G)
            for b in range(B)
        ]
        for k in range(B)
    ]
    pairs = [(q, c) for q in range(G) for c in range(B)]
    to_next_row = [(device_at(q, c), device_at((q + 1) % G, c)) for q, c in pairs]
    to_prev_row = [(t, s) for s, t in to_next_row]
    who = ((geo % 2).astype(jnp.int32).reshape(1), part.astype(jnp.int32).reshape(1))

    width = C + 2 * PAD
    blocks = [
        jax.ShapeDtypeStruct((z.slabs(rows) * width + more, LANES), F32)
        for rows, more in ((z.edge_rows, R), (z.inner_rows, 0))
        for _ in range(B)
    ]
    all_slabs = z.slabs(z.edge_rows) + z.slabs(z.inner_rows)
    columns_scratch = [
        pltpu.VMEM((W // LANES, nb * R, LANES), F32),
        pltpu.VMEM((W // LANES, 2 * L * R, LANES), F32),
    ]
    packed = pl.pallas_call(
        functools.partial(pack_kernel, z),
        out_shape=blocks,
        in_specs=[SMEM] * 2 + [VMEM] * 3,
        out_specs=[VMEM] * (2 * B),
        scratch_shapes=columns_scratch + [pltpu.VMEM((all_slabs, W + 2 * PAD, LANES), F32)],
        compiler_params=params(24),
        name="pack",
    )(*who, spectrum.reshape(nb * R, W), ocean.reshape(2 * L * R, W), sea_mask)
    got = [lax.ppermute(packed[i], axes, forward[i % B]) for i in range(2 * B)]

    weights, drift_weights = pl.pallas_call(
        functools.partial(weights_kernel, z),
        out_shape=(
            jax.ShapeDtypeStruct((2 * NB, NB), BF16),
            jax.ShapeDtypeStruct((NB, LANES), BF16),
        ),
        in_specs=[VMEM] * 3,
        out_specs=(VMEM,) * 2,
        compiler_params=params(24),
        cost_estimate=cost(2e9, 4 * NB * NB * 2),
        name="weights",
    )(kernel_linear, kernel_square, drift_kernel)
    speed = speeds(z)

    def unpack(rows, received, shapes):
        return pl.pallas_call(
            functools.partial(unpack_kernel, z, rows),
            out_shape=[jax.ShapeDtypeStruct((n, width, lanes), F32) for n, lanes in shapes],
            in_specs=[SMEM] * 2 + [VMEM] * B + [ANY] * (len(received) - B),
            out_specs=[VMEM] * len(shapes),
            compiler_params=params(16),
            name="unpack",
        )(*who, *received)

    top, bottom, sea = unpack(
        z.edge_rows, got[: B + 1], [(EDGE, CH + LANES), (EDGE, CH + LANES), (R, LANES)]
    )
    (inner,) = unpack(z.inner_rows, got[B:], [(R - 2 * EDGE, CH)])

    def step_call(body, cut, sea_at, count, deepest, inputs, more=0):
        width = inputs[0].shape[1]
        n = width - 2 * cut
        shapes = [(count, n, CH)] + [(EDGE, width, NB)] * more
        return pl.pallas_call(
            functools.partial(body, z, cut, sea_at),
            out_shape=[jax.ShapeDtypeStruct(shape, F32) for shape in shapes],
            in_specs=[VMEM] * (len(inputs) + 3),
            out_specs=[VMEM] * len(shapes),
            scratch_shapes=[
                pltpu.VMEM((3, deepest, width, LANES), F32),
                pltpu.VMEM((count, n, NB), F32),
            ],
            compiler_params=params(24),
            cost_estimate=cost(count * 1.5e9, count * 2e6),
            name=body.__name__,
        )(*inputs, speed, weights, drift_weights)

    for step in range(STEPS):
        valid = EDGE * (STEPS - 1 - step)
        margin = (width - C) // 2
        cut = margin - valid if valid == 0 or (margin - valid) % 4 == 0 else 0
        sea_at = PAD - margin
        down = lax.ppermute(top, axes, to_prev_row)
        up = lax.ppermute(bottom, axes, to_next_row)
        if step == 0:
            sea_up, sea_down = up[:, :, CH:], down[:, :, CH:]
        new_inner, *given = step_call(
            inner_kernel, cut, sea_at, R - 2 * EDGE, R, (top, inner, bottom, sea),
            2 if step > 0 else 0,
        )
        (new_bottom,) = step_call(
            bottom_kernel, cut, sea_at, EDGE, 3 * EDGE,
            (down, bottom, inner, sea_down, sea, *given[1:]),
        )
        (new_top,) = step_call(
            top_kernel, cut, sea_at, EDGE, 3 * EDGE, (up, top, inner, sea_up, sea, *given[:1])
        )
        top, inner, bottom = new_top, new_inner, new_bottom
        width -= 2 * cut

    def send_back(rows, states):
        shape = jax.ShapeDtypeStruct((z.slabs(rows), C, LANES), F32)
        return pl.pallas_call(
            functools.partial(send_back_kernel, z, rows),
            out_shape=[shape] * B,
            in_specs=[SMEM] * 2 + [VMEM] * len(states),
            out_specs=[VMEM] * B,
            compiler_params=params(16),
            name="send_back",
        )(*who, *states)

    packed = send_back(z.inner_rows, [inner]), send_back(z.edge_rows, [top, bottom])
    packed = list(packed[1]) + list(packed[0])
    back = [
        lax.ppermute(packed[i], axes, [(t, s) for s, t in forward[i % B]]) for i in range(2 * B)
    ]
    spectrum_out, ocean_out = pl.pallas_call(
        functools.partial(restore_kernel, z),
        out_shape=(
            jax.ShapeDtypeStruct((nb * R, W), F32),
            jax.ShapeDtypeStruct((2 * L * R, W), F32),
        ),
        in_specs=[SMEM] * 2 + [VMEM] * (2 * B),
        out_specs=(VMEM,) * 2,
        scratch_shapes=[pltpu.VMEM((all_slabs, W, LANES), F32)] + columns_scratch,
        compiler_params=params(24),
        name="restore",
    )(*who, *back)
    return spectrum_out.reshape(nb, R, W), ocean_out.reshape(2, L, R, W)


def solution(mesh):
    return jax.shard_map(
        functools.partial(per_device, mesh.shape["geo"], mesh.shape["bins"]),
        mesh=mesh,
        in_specs=(
            P("bins", "geo", None),
            P("geo", None),
            P(),
            P(),
            P(),
            P(None, "bins", "geo", None),
        ),
        out_specs=(P("bins", "geo", None), P(None, "bins", "geo", None)),
        check_vma=False,
    )
```

```python
import functools

import jax
import jax.numpy as jnp
from jax import lax
from jax.experimental import pallas as pl
from jax.experimental.pallas import tpu as pltpu
from jax.sharding import PartitionSpec as P

NDIR = 36
NFREQ = 32
STEPS = 3
SUB = 2
DT_SOURCE = 0.5
DT_OCEAN = 0.2
CORIOLIS = 1.0
VISCOSITY = 1.0
DOPPLER = 0.1

LANES = 128
PAD = 8
EDGE = 2
VMEM = pl.BlockSpec(memory_space=pltpu.VMEM)
SMEM = pl.BlockSpec(memory_space=pltpu.SMEM)
HBM = pl.BlockSpec(memory_space=pltpu.HBM)
F32 = jnp.float32
BF16 = jnp.bfloat16


def params(mib):
    return pltpu.CompilerParams(vmem_limit_bytes=mib * 1024 * 1024)


class Sizes:
    def __init__(self, parts, bins_here, levels_here, rows, width):
        self.B, self.nb, self.L, self.R, self.W = parts, bins_here, levels_here, rows, width
        self.C = width // parts
        self.mt = bins_here // LANES
        self.main = self.mt * LANES
        self.nr = bins_here - self.main
        self.no = 2 * levels_here
        self.NB = parts * bins_here
        self.CH = self.NB + LANES
        self.edge_rows = (0, 1, rows - 2, rows - 1)
        self.inner_rows = tuple(range(2, rows - 2))
        self.half = parts // 2
        assert self.half & (self.half - 1) == 0 and self.half > 1
        assert self.nr * parts == LANES and self.no * parts == LANES

    def folds(self, rows):
        out, base = [], len(rows) * self.mt
        for count, lane in ((self.nr, self.B * self.main), (self.no, self.NB)):
            used = min(LANES // count, len(rows))
            deep = len(rows) // used
            assert deep * used == len(rows)
            out.append((count, used, deep, base, lane))
            base += deep
        return out, base

    def slabs(self, rows):
        return self.folds(rows)[1]


def exchange_share(z, k, odd, part):
    core = part % 2
    flip, delta = (k // z.half) ^ core, (k % z.half) ^ core
    return (odd ^ flip) * z.half + ((part // 2) ^ delta)


def exchange_part(z, k, odd, part):
    core = (k // z.half) ^ odd ^ (part % 2)
    delta = (k % z.half) ^ core
    return ((part // 2) ^ delta) * 2 + core


def lane_group(width):
    return lax.broadcasted_iota(jnp.int32, (1, LANES), 1) // width


def pack_kernel(z, odd, part, spec_in, ocean_in, mask, *refs):
    B, R, C, W, mt = z.B, z.R, z.C, z.W, z.mt
    outs, (spec, ocean, wide, sems) = refs[: 2 * B], refs[2 * B :]
    E = C + 2 * PAD
    at = 0
    copies = []
    for half in range(W // LANES):
        cols = pl.ds(half * LANES, LANES)
        for n, (src, dst) in enumerate(((spec_in, spec), (ocean_in, ocean))):
            copies.append(pltpu.make_async_copy(src.at[:, cols], dst.at[half], sems.at[n, half]))
            copies[-1].start()
    sea = mask[...].astype(F32)
    sea = jnp.concatenate([sea, jnp.zeros((R, LANES), F32)], axis=1)
    wide[:, 0:PAD, :] = jnp.zeros((wide.shape[0], PAD, LANES), F32)
    wide[:, PAD + W : W + 2 * PAD, :] = jnp.zeros((wide.shape[0], PAD, LANES), F32)
    for which, rows in enumerate((z.edge_rows, z.inner_rows)):
        folds, slabs = z.folds(rows)
        for half in range(W // LANES):
            if which == 0:
                for copy in copies[2 * half : 2 * half + 2]:
                    copy.wait()
            cols = slice(PAD + half * LANES, PAD + (half + 1) * LANES)
            for i, r in enumerate(rows):
                for t in range(mt):
                    block = spec[half, pl.ds(t * LANES * R + r, LANES, stride=R), :]
                    wide[at + i * mt + t, cols] = block.T
            for (count, used, deep, base, _), src, first in zip(folds, (spec, ocean), (z.main, 0)):
                for rr in range(deep):
                    pieces = [
                        src[half, pl.ds(first * R + rows[rr + i * deep], count, stride=R), :]
                        for i in range(used)
                    ]
                    if used * count < LANES:
                        pieces.append(jnp.zeros((LANES - used * count, LANES), F32))
                    wide[at + base + rr, cols] = jnp.concatenate(pieces, axis=0).T
        for k in range(B):
            out = outs[which * B + k]
            share = exchange_share(z, k, odd[0], part[0])
            start = pl.multiple_of(share * C, PAD)
            block = wide[at : at + slabs, pl.ds(start, E), :]
            out[0 : slabs * E] = block.reshape(slabs * E, LANES)
            if which == 0:
                shift = lax.rem(W + LANES + PAD - start, W + LANES)
                out[slabs * E : slabs * E + R] = pltpu.roll(sea, shift, axis=1)[:, :LANES]
        at += slabs


def spread_line(line):
    return jnp.broadcast_to(line, (LANES, LANES)).T


def unpack_kernel(z, rows, odd, part, *refs):
    B, mt = z.B, z.mt
    got, outs = refs[:B], refs[B:]
    E = z.C + 2 * PAD
    if rows == z.edge_rows:
        sea = outs[-1]
        outs = outs[:-1]
        lines = got[0][z.slabs(rows) * E : z.slabs(rows) * E + z.R]
        for r in range(z.R):
            sea[r] = spread_line(lines[r : r + 1])[:E]
    places = [(ref, i) for ref in outs for i in range(ref.shape[0])]
    src = [exchange_part(z, k, odd[0], part[0]) for k in range(B)]
    for k in range(B):
        for t in range(mt):
            lanes = pl.ds(pl.multiple_of(src[k] * z.main + t * LANES, LANES), LANES)
            for i, (ref, at) in enumerate(places):
                ref[at, :, lanes] = got[k][(i * mt + t) * E : (i * mt + t + 1) * E]
    for count, used, deep, base, lane in z.folds(rows)[0]:
        group = lane_group(count)
        for i, (ref, at) in enumerate(places):
            tile = jnp.zeros(ref.shape[1:2] + (LANES,), F32)
            for k in range(B):
                shift = lax.rem((src[k] - i // deep) * count + LANES, LANES)
                slab = base + i % deep
                moved = pltpu.roll(got[k][slab * E : (slab + 1) * E], shift, axis=1)
                tile = jnp.where(group == src[k], moved, tile)
            ref[at, :, lane : lane + LANES] = tile
    if rows == z.edge_rows:
        for i, (ref, at) in enumerate(places):
            r = rows[i]
            ref[at, 0:1, 0:LANES] = lines[r : r + 1]


def send_back_kernel(z, rows, odd, part, *refs):
    B, mt = z.B, z.mt
    states, outs = refs[:-B], refs[-B:]
    places = [(ref, i) for ref in states for i in range(ref.shape[0])]
    for k in range(B):
        src = exchange_part(z, k, odd[0], part[0])
        for t in range(mt):
            lanes = pl.ds(pl.multiple_of(src * z.main + t * LANES, LANES), LANES)
            for i, (ref, at) in enumerate(places):
                outs[k][i * mt + t] = ref[at, :, lanes]
        for count, used, deep, base, lane in z.folds(rows)[0]:
            group = lane_group(count)
            for rr in range(deep):
                tile = jnp.zeros((z.C, LANES), F32)
                for i in range(used):
                    ref, at = places[rr + i * deep]
                    shift = lax.rem((i - src) * count + LANES, LANES)
                    moved = pltpu.roll(ref[at, :, lane : lane + LANES], shift, axis=1)
                    tile = jnp.where(group == i, moved, tile)
                outs[k][base + rr] = tile


def restore_kernel(z, odd, part, *refs):
    B, R, C, mt = z.B, z.R, z.C, z.mt
    got, (spec_out, ocean_out, wide, spec, ocean) = refs[: 2 * B], refs[2 * B :]
    at = 0
    for which, rows in enumerate((z.edge_rows, z.inner_rows)):
        folds, slabs = z.folds(rows)
        for k in range(B):
            c = exchange_share(z, k, odd[0], part[0])
            wide[at : at + slabs, pl.ds(pl.multiple_of(c * C, PAD), C), :] = got[which * B + k][...]
        for half in range(z.W // LANES):
            cols = slice(half * LANES, (half + 1) * LANES)
            for i, r in enumerate(rows):
                for t in range(mt):
                    place = pl.ds(t * LANES * R + r, LANES, stride=R)
                    spec[half, place, :] = wide[at + i * mt + t, cols].T
            for (count, used, deep, base, _), dst, first in zip(folds, (spec, ocean), (z.main, 0)):
                for rr in range(deep):
                    turned = wide[at + base + rr, cols].T
                    for i in range(used):
                        place = pl.ds(first * R + rows[rr + i * deep], count, stride=R)
                        dst[half, place, :] = turned[i * count : (i + 1) * count]
        at += slabs
    for half in range(z.W // LANES):
        cols = slice(half * LANES, (half + 1) * LANES)
        spec_out[:, cols] = spec[half]
        ocean_out[:, cols] = ocean[half]


def weights_kernel(z, linear, square, drift, weights, drift_weights):
    B, nb, main, nr, NB, L = z.B, z.nb, z.main, z.nr, z.NB, z.L

    def put(dst, first, lanes, turned):
        for s in range(B):
            dst[first + s * main : first + (s + 1) * main, lanes] = turned[
                s * nb : s * nb + main
            ]
            tail = first + B * main + s * nr
            dst[tail : tail + nr, lanes] = turned[s * nb + main : (s + 1) * nb]

    for n, source in enumerate((linear, square)):
        for s in range(B):
            for t in range(z.mt):
                block = source[s * nb + t * LANES : s * nb + (t + 1) * LANES, :]
                lane = s * main + t * LANES
                put(weights, n * NB, slice(lane, lane + LANES), block.T)
        tails = [source[s * nb + main : (s + 1) * nb, :] for s in range(B)]
        block = jnp.concatenate(tails, axis=0)
        put(weights, n * NB, slice(B * main, NB), block.T)

    row = lax.broadcasted_iota(jnp.int32, (LANES, LANES), 0)
    lane = lax.broadcasted_iota(jnp.int32, (LANES, LANES), 1)
    part, comp, level = lane // (2 * L), (lane // L) % 2, lane % L
    pick = jnp.where(row == 2 * (part * L + level) + 1 - comp, 1.0, 0.0).astype(BF16)
    turned = jnp.dot(drift[...].T, pick, preferred_element_type=F32).astype(BF16)
    put(drift_weights, 0, slice(0, LANES), turned)


def advance(
    z, sea_rows, rows, outs, cut, sea_at, speed, weights, drift_weights, moved, moved_twice,
    known=None, kept=None,
):
    NB, CH, L = z.NB, z.CH, z.L
    known, kept = known or {}, kept or {}
    n = len(rows)
    first = [r for r in range(1, n - 1) if r not in known]
    assert first == list(range(first[0], first[-1] + 1))
    E = rows[0][0].shape[1]
    N = E - 2 * cut
    keep = slice(cut, cut + N)
    sea_cols = pl.ds(sea_at, E)
    places = [(ref, i) for ref in outs for i in range(ref.shape[0])]

    def sea_row(place):
        return place[0][place[1], sea_cols]

    for r in range(min(first[0] - 1, 1), max(first[-1] + 2, n - 1)):
        ref, i = rows[r]
        surface = ref[i, :, NB:CH]
        moved[0, r] = DOPPLER * jnp.tanh(jnp.broadcast_to(surface[:, 0:1], (E, LANES)))
        moved[1, r] = DOPPLER * jnp.tanh(jnp.broadcast_to(surface[:, L : L + 1], (E, LANES)))

    def advect(read, write, start, stop, speed_cx, speed_cy):
        def along_x(r):
            energy = read(r)
            speed_x = speed_cx + moved[0, r]
            return (
                energy,
                jnp.maximum(speed_x, 0.0) * energy,
                jnp.minimum(speed_x, 0.0) * energy,
            )

        _, plus_before, _ = along_x(start - 1)
        energy, plus, minus = along_x(start)
        for r in range(start, stop):
            energy_next, plus_next, minus_next = along_x(r + 1)
            speed_y = speed_cy + moved[1, r]
            plus_y = jnp.maximum(speed_y, 0.0) * energy
            minus_y = jnp.minimum(speed_y, 0.0) * energy
            result = (
                energy
                - ((plus - plus_before) + (minus_next - minus))
                - (
                    (plus_y - pltpu.roll(plus_y, 1, axis=0))
                    + (pltpu.roll(minus_y, E - 1, axis=0) - minus_y)
                )
            )
            write(r, result * sea_row(sea_rows[r]))
            plus_before, energy, plus, minus = plus, energy_next, plus_next, minus_next

    def one_tile(j, carry):
        lanes = pl.ds(pl.multiple_of(j * LANES, LANES), LANES)
        speed_cx = speed[0:1, lanes]
        speed_cy = speed[1:2, lanes]

        def read_first(r):
            ref, i = rows[r]
            return ref[i, :, lanes]

        def write_first(r, value):
            moved[2, r] = value
            if r in kept:
                ref, i = kept[r]
                ref[i, :, lanes] = value

        def read_second(r):
            if r in known:
                ref, i = known[r]
                return ref[i, :, lanes]
            return moved[2, r]

        def write_second(r, value):
            moved_twice[r - 2, :, lanes] = value[keep]

        advect(read_first, write_first, first[0], first[-1] + 1, speed_cx, speed_cy)
        advect(read_second, write_second, 2, n - 2, speed_cx, speed_cy)
        return carry

    lax.fori_loop(0, NB // LANES, one_tile, 0)

    count = len(places)
    own_sea = sea_rows[2 : n - 2]
    energy = moved_twice[...].reshape(count * N, NB)
    squares = energy * energy
    interaction = jnp.dot(
        energy.astype(BF16), weights[:NB], preferred_element_type=F32
    ) + jnp.dot(squares.astype(BF16), weights[NB:], preferred_element_type=F32)
    total = jnp.sum(squares, axis=1, keepdims=True)
    sea_here = jnp.concatenate([sea_row(place)[keep] for place in own_sea], axis=0)
    scale = (DT_SOURCE * sea_here[:, 0:1]) / (1.0 + total / NB)
    fresh = energy + scale * (interaction * energy)
    for i, (ref, at) in enumerate(places):
        ref[at, :, 0:NB] = fresh[i * N : (i + 1) * N]
    drift = jnp.dot(fresh.astype(BF16), drift_weights[...], preferred_element_type=F32)

    comp = (lax.broadcasted_iota(jnp.int32, (1, LANES), 1) // L) % 2
    sign = jnp.where(comp == 0, 1.0, -1.0).astype(F32)
    for i, (out, at) in enumerate(places):
        here, before, after = [
            ref[row, :, NB:CH] for ref, row in (rows[i + 2], rows[i + 1], rows[i + 3])
        ]
        lap = (
            (after + before)
            + (pltpu.roll(here, E - 1, axis=0) + pltpu.roll(here, 1, axis=0))
            - 4.0 * here
        )[keep]
        centre = here[keep]
        other = jnp.where(
            comp == 0, pltpu.roll(centre, LANES - L, axis=1), pltpu.roll(centre, L, axis=1)
        )
        turn = sign * (CORIOLIS * (other + drift[i * N : (i + 1) * N]))
        out[at, :, NB:CH] = (
            centre + DT_OCEAN * (turn + VISCOSITY * lap)
        ) * sea_row(own_sea[i])[keep]


def listed(*refs):
    return [(ref, i) for ref in refs for i in range(ref.shape[0])]


def inner_kernel(z, first, cut, sea_at, top, inner, bottom, sea, speed, weights, drift_weights, *refs):
    out, for_edges, (moved, moved_twice) = refs[0], refs[1:-2], refs[-2:]
    kept = {}
    if for_edges:
        kept = {1 + i: (for_edges[0], i) for i in range(EDGE)}
        kept |= {z.R - 1 - EDGE + i: (for_edges[1], i) for i in range(EDGE)}
    advance(
        z, listed(sea), listed(top, inner, bottom), [out], cut, sea_at, speed, weights,
        drift_weights, moved, moved_twice, kept=kept,
    )


def read_sea(halo, sea):
    for i in range(EDGE):
        sea[i] = spread_line(halo[i, 0:1, 0:LANES])[: halo.shape[1]]
    return sea


def top_kernel(z, first, cut, sea_at, up, top, inner, sea, *refs):
    inputs, outs = refs[:-4] if first else refs[:-3], refs[-4:] if first else refs[-3:]
    *given, speed, weights, drift_weights = inputs
    out, moved, moved_twice = outs[0], outs[-2], outs[-1]
    sea_up = read_sea(up, outs[1]) if first else given.pop(0)
    known = {3 + i: (given[0], i) for i in range(EDGE)} if given else {}
    rows = listed(up, top) + listed(inner)[:EDGE]
    sea_rows = (listed(sea_up) + listed(sea))[: len(rows)]
    advance(
        z, sea_rows, rows, [out], cut, sea_at, speed, weights, drift_weights, moved,
        moved_twice, known=known,
    )


def bottom_kernel(z, first, cut, sea_at, down, bottom, inner, sea, *refs):
    inputs, outs = refs[:-4] if first else refs[:-3], refs[-4:] if first else refs[-3:]
    *given, speed, weights, drift_weights = inputs
    out, moved, moved_twice = outs[0], outs[-2], outs[-1]
    sea_down = read_sea(down, outs[1]) if first else given.pop(0)
    known = {1 + i: (given[0], i) for i in range(EDGE)} if given else {}
    rows = listed(inner)[-EDGE:] + listed(bottom, down)
    sea_rows = (listed(sea) + listed(sea_down))[-len(rows) :]
    advance(
        z, sea_rows, rows, [out], cut, sea_at, speed, weights, drift_weights, moved,
        moved_twice, known=known,
    )


def speeds(z):
    lane = jnp.arange(z.NB, dtype=jnp.int32)
    head = (lane // z.main) * z.nb + lane % z.main
    rest = lane - z.B * z.main
    tail = (rest // z.nr) * z.nb + z.main + rest % z.nr
    bin_index = jnp.where(lane < z.B * z.main, head, tail)
    direction = (bin_index // NFREQ).astype(F32)
    frequency = (bin_index % NFREQ).astype(F32)
    group_speed = 0.4 / (1.0 + frequency / 16.0)
    bin_angle = (2.0 * jnp.pi / NDIR) * direction
    zeros = jnp.zeros_like(bin_angle)
    rows = [group_speed * jnp.cos(bin_angle), group_speed * jnp.sin(bin_angle)] + [zeros] * 6
    return jnp.stack(rows)


def cost(flops, moved):
    return pl.CostEstimate(flops=int(flops), bytes_accessed=int(moved), transcendentals=0)


def per_device(G, B, spectrum, sea_mask, kernel_linear, kernel_square, drift_kernel, ocean):
    nb, R, W = spectrum.shape
    L = ocean.shape[1]
    z = Sizes(B, nb, L, R, W)
    C, NB, CH = z.C, z.NB, z.CH
    half = B // 2
    axes = ("geo", "bins")
    geo, part = lax.axis_index("geo"), lax.axis_index("bins")

    def device_at(q, c):
        return ((q // 2) * 2 + c // half) * B + 2 * (c % half) + q % 2

    forward = [
        [
            (g * B + b, device_at(g, exchange_share(z, k, g % 2, b)))
            for g in range(G)
            for b in range(B)
        ]
        for k in range(B)
    ]
    pairs = [(q, c) for q in range(G) for c in range(B)]
    to_next_row = [(device_at(q, c), device_at((q + 1) % G, c)) for q, c in pairs]
    to_prev_row = [(t, s) for s, t in to_next_row]
    who = ((geo % 2).astype(jnp.int32).reshape(1), part.astype(jnp.int32).reshape(1))

    width = C + 2 * PAD
    blocks = [
        jax.ShapeDtypeStruct((z.slabs(rows) * width + more, LANES), F32)
        for rows, more in ((z.edge_rows, R), (z.inner_rows, 0))
        for _ in range(B)
    ]
    all_slabs = z.slabs(z.edge_rows) + z.slabs(z.inner_rows)
    columns_scratch = [
        pltpu.VMEM((W // LANES, nb * R, LANES), F32),
        pltpu.VMEM((W // LANES, 2 * L * R, LANES), F32),
    ]
    packed = pl.pallas_call(
        functools.partial(pack_kernel, z),
        out_shape=blocks,
        in_specs=[SMEM] * 2 + [HBM, HBM, VMEM],
        out_specs=[VMEM] * (2 * B),
        scratch_shapes=columns_scratch
        + [
            pltpu.VMEM((all_slabs, W + 2 * PAD, LANES), F32),
            pltpu.SemaphoreType.DMA((2, W // LANES)),
        ],
        compiler_params=params(58),
        name="pack",
    )(*who, spectrum.reshape(nb * R, W), ocean.reshape(2 * L * R, W), sea_mask)
    got = [lax.ppermute(packed[k], axes, forward[k]) for k in range(B)]

    weights, drift_weights = pl.pallas_call(
        functools.partial(weights_kernel, z),
        out_shape=(
            jax.ShapeDtypeStruct((2 * NB, NB), BF16),
            jax.ShapeDtypeStruct((NB, LANES), BF16),
        ),
        in_specs=[VMEM] * 3,
        out_specs=(VMEM,) * 2,
        compiler_params=params(24),
        cost_estimate=cost(2e9, 4 * NB * NB * 2),
        name="weights",
    )(kernel_linear, kernel_square, drift_kernel)
    speed = speeds(z)
    *got, weights, drift_weights, speed = lax.optimization_barrier(
        (*got, weights, drift_weights, speed)
    )

    def unpack(rows, received, shapes):
        return pl.pallas_call(
            functools.partial(unpack_kernel, z, rows),
            out_shape=[jax.ShapeDtypeStruct((n, width, lanes), F32) for n, lanes in shapes],
            in_specs=[SMEM] * 2 + [VMEM] * B,
            out_specs=[VMEM] * len(shapes),
            compiler_params=params(16),
            name="unpack",
        )(*who, *received)

    top, bottom, sea = unpack(
        z.edge_rows, got[:B], [(EDGE, CH), (EDGE, CH), (R, LANES)]
    )
    *blocks, top = lax.optimization_barrier((*packed[B:], top))
    got += [lax.ppermute(blocks[k], axes, forward[k]) for k in range(B)]
    (inner,) = unpack(z.inner_rows, got[B:], [(R - 2 * EDGE, CH)])

    def step_call(body, first, cut, sea_at, count, deepest, inputs, more=()):
        width = inputs[0].shape[1]
        n = width - 2 * cut
        shapes = [(count, n, CH)] + [(EDGE, width, lanes) for lanes in more]
        return pl.pallas_call(
            functools.partial(body, z, first, cut, sea_at),
            out_shape=[jax.ShapeDtypeStruct(shape, F32) for shape in shapes],
            in_specs=[VMEM] * (len(inputs) + 3),
            out_specs=[VMEM] * len(shapes),
            scratch_shapes=[
                pltpu.VMEM((3, deepest, width, LANES), F32),
                pltpu.VMEM((count, n, NB), F32),
            ],
            compiler_params=params(24),
            cost_estimate=cost(count * 1e8, count * 1e5),
            name=body.__name__,
        )(*inputs, speed, weights, drift_weights)

    sea_up, sea_down = [], []
    for step in range(STEPS):
        valid = EDGE * (STEPS - 1 - step)
        margin = (width - C) // 2
        cut = margin - valid if valid == 0 or (margin - valid) % 4 == 0 else 0
        sea_at = PAD - margin
        down = lax.ppermute(top, axes, to_prev_row)
        up = lax.ppermute(bottom, axes, to_next_row)
        first = step == 0

        def advance_inner():
            return step_call(
                inner_kernel, first, cut, sea_at, R - 2 * EDGE, R, (top, inner, bottom, sea),
                () if first else (NB, NB),
            )

        given = ()
        if not first:
            new_inner, *given = advance_inner()
        new_bottom, *found = step_call(
            bottom_kernel, first, cut, sea_at, EDGE, 3 * EDGE,
            (down, bottom, inner, sea, *sea_down, *given[1:]),
            (LANES,) if first else (),
        )
        sea_down = sea_down or found
        new_top, *found = step_call(
            top_kernel, first, cut, sea_at, EDGE, 3 * EDGE,
            (up, top, inner, sea, *sea_up, *given[:1]),
            (LANES,) if first else (),
        )
        sea_up = sea_up or found
        if first:
            inner, new_top = lax.optimization_barrier((inner, new_top))
            (new_inner,) = advance_inner()
        top, inner, bottom = new_top, new_inner, new_bottom
        width -= 2 * cut

    def send_back(rows, states):
        shape = jax.ShapeDtypeStruct((z.slabs(rows), C, LANES), F32)
        return pl.pallas_call(
            functools.partial(send_back_kernel, z, rows),
            out_shape=[shape] * B,
            in_specs=[SMEM] * 2 + [VMEM] * len(states),
            out_specs=[VMEM] * B,
            compiler_params=params(16),
            name="send_back",
        )(*who, *states)

    packed = send_back(z.inner_rows, [inner]), send_back(z.edge_rows, [top, bottom])
    packed = list(packed[1]) + list(packed[0])
    back = [
        lax.ppermute(packed[i], axes, [(t, s) for s, t in forward[i % B]]) for i in range(2 * B)
    ]
    spectrum_out, ocean_out = pl.pallas_call(
        functools.partial(restore_kernel, z),
        out_shape=(
            jax.ShapeDtypeStruct((nb * R, W), F32),
            jax.ShapeDtypeStruct((2 * L * R, W), F32),
        ),
        in_specs=[SMEM] * 2 + [VMEM] * (2 * B),
        out_specs=(VMEM,) * 2,
        scratch_shapes=[pltpu.VMEM((all_slabs, W, LANES), F32)] + columns_scratch,
        compiler_params=params(24),
        name="restore",
    )(*who, *back)
    return spectrum_out.reshape(nb, R, W), ocean_out.reshape(2, L, R, W)


def solution(mesh):
    return jax.shard_map(
        functools.partial(per_device, mesh.shape["geo"], mesh.shape["bins"]),
        mesh=mesh,
        in_specs=(
            P("bins", "geo", None),
            P("geo", None),
            P(),
            P(),
            P(),
            P(None, "bins", "geo", None),
        ),
        out_specs=(P("bins", "geo", None), P(None, "bins", "geo", None)),
        check_vma=False,
    )
```

```python
import functools

import jax
import jax.numpy as jnp
from jax import lax
from jax.experimental import pallas as pl
from jax.experimental.pallas import tpu as pltpu
from jax.sharding import PartitionSpec as P

NDIR = 36
NFREQ = 32
STEPS = 3
SUB = 2
DT_SOURCE = 0.5
DT_OCEAN = 0.2
CORIOLIS = 1.0
VISCOSITY = 1.0
DOPPLER = 0.1

LANES = 128
PAD = 8
EDGE = 2
VMEM = pl.BlockSpec(memory_space=pltpu.VMEM)
SMEM = pl.BlockSpec(memory_space=pltpu.SMEM)
HBM = pl.BlockSpec(memory_space=pltpu.HBM)
F32 = jnp.float32
BF16 = jnp.bfloat16


def params(mib):
    return pltpu.CompilerParams(vmem_limit_bytes=mib * 1024 * 1024)


class Sizes:
    def __init__(self, parts, bins_here, levels_here, rows, width):
        self.B, self.nb, self.L, self.R, self.W = parts, bins_here, levels_here, rows, width
        self.C = width // parts
        self.mt = bins_here // LANES
        self.main = self.mt * LANES
        self.nr = bins_here - self.main
        self.no = 2 * levels_here
        self.NB = parts * bins_here
        self.CH = self.NB + LANES
        self.edge_rows = (0, 1, rows - 2, rows - 1)
        self.inner_rows = tuple(range(2, rows - 2))
        self.half = parts // 2
        assert self.half & (self.half - 1) == 0 and self.half > 1
        assert self.nr * parts == LANES and self.no * parts == LANES

    def folds(self, rows):
        out, base = [], len(rows) * self.mt
        for count, lane in ((self.nr, self.B * self.main), (self.no, self.NB)):
            used = min(LANES // count, len(rows))
            deep = len(rows) // used
            assert deep * used == len(rows)
            out.append((count, used, deep, base, lane))
            base += deep
        return out, base

    def slabs(self, rows):
        return self.folds(rows)[1]


def exchange_share(z, k, odd, part):
    core = part % 2
    flip, delta = (k // z.half) ^ core, (k % z.half) ^ core
    return (odd ^ flip) * z.half + ((part // 2) ^ delta)


def exchange_part(z, k, odd, part):
    core = (k // z.half) ^ odd ^ (part % 2)
    delta = (k % z.half) ^ core
    return ((part // 2) ^ delta) * 2 + core


def lane_group(width):
    return lax.broadcasted_iota(jnp.int32, (1, LANES), 1) // width


def pack_kernel(z, rows, odd, part, spec_in, ocean_in, mask_in, *refs):
    B, R, C, W, mt = z.B, z.R, z.C, z.W, z.mt
    outs, (spec, ocean, mask, wide, sems) = refs[:B], refs[B:]
    E = C + 2 * PAD
    copies = []
    for half in range(W // LANES):
        cols = pl.ds(half * LANES, LANES)
        for n, (src, dst) in enumerate(((spec_in, spec), (ocean_in, ocean))):
            copies.append(pltpu.make_async_copy(src.at[:, cols], dst.at[half], sems.at[n, half]))
            copies[-1].start()
    mask_copy = pltpu.make_async_copy(mask_in, mask, sems.at[2, 0])
    mask_copy.start()
    wide[:, 0:PAD, :] = jnp.zeros((wide.shape[0], PAD, LANES), F32)
    wide[:, PAD + W : W + 2 * PAD, :] = jnp.zeros((wide.shape[0], PAD, LANES), F32)
    folds, slabs = z.folds(rows)
    for half in range(W // LANES):
        for copy in copies[2 * half : 2 * half + 2]:
            copy.wait()
        cols = slice(PAD + half * LANES, PAD + (half + 1) * LANES)
        for i, r in enumerate(rows):
            for t in range(mt):
                block = spec[half, pl.ds(t * LANES * R + r, LANES, stride=R), :]
                wide[i * mt + t, cols] = block.T
        for (count, used, deep, base, _), src, first in zip(folds, (spec, ocean), (z.main, 0)):
            for rr in range(deep):
                pieces = [
                    src[half, pl.ds(first * R + rows[rr + i * deep], count, stride=R), :]
                    for i in range(used)
                ]
                if used * count < LANES:
                    pieces.append(jnp.zeros((LANES - used * count, LANES), F32))
                wide[base + rr, cols] = jnp.concatenate(pieces, axis=0).T
    mask_copy.wait()
    sea = jnp.concatenate([mask[...].astype(F32), jnp.zeros((R, LANES), F32)], axis=1)
    for k, out in enumerate(outs):
        share = exchange_share(z, k, odd[0], part[0])
        start = pl.multiple_of(share * C, PAD)
        block = wide[:, pl.ds(start, E), :]
        out[0 : slabs * E] = block.reshape(slabs * E, LANES)
        if rows == z.edge_rows:
            shift = lax.rem(W + LANES + PAD - start, W + LANES)
            out[slabs * E : slabs * E + R] = pltpu.roll(sea, shift, axis=1)[:, :LANES]


def spread_line(line):
    return jnp.broadcast_to(line, (LANES, LANES)).T


def unpack_kernel(z, rows, odd, part, *refs):
    B, mt = z.B, z.mt
    got, outs = refs[:B], refs[B:]
    E = z.C + 2 * PAD
    if rows == z.edge_rows:
        sea = outs[-1]
        outs = outs[:-1]
        lines = got[0][z.slabs(rows) * E : z.slabs(rows) * E + z.R]
        for r in range(z.R):
            sea[r] = spread_line(lines[r : r + 1])[:E]
    places = [(ref, i) for ref in outs for i in range(ref.shape[0])]
    src = [exchange_part(z, k, odd[0], part[0]) for k in range(B)]
    for k in range(B):
        for t in range(mt):
            lanes = pl.ds(pl.multiple_of(src[k] * z.main + t * LANES, LANES), LANES)
            for i, (ref, at) in enumerate(places):
                ref[at, :, lanes] = got[k][(i * mt + t) * E : (i * mt + t + 1) * E]
    for count, used, deep, base, lane in z.folds(rows)[0]:
        group = lane_group(count)
        for i, (ref, at) in enumerate(places):
            tile = jnp.zeros(ref.shape[1:2] + (LANES,), F32)
            for k in range(B):
                shift = lax.rem((src[k] - i // deep) * count + LANES, LANES)
                slab = base + i % deep
                moved = pltpu.roll(got[k][slab * E : (slab + 1) * E], shift, axis=1)
                tile = jnp.where(group == src[k], moved, tile)
            ref[at, :, lane : lane + LANES] = tile
    if rows == z.edge_rows:
        for i, (ref, at) in enumerate(places):
            r = rows[i]
            ref[at, 0:1, 0:LANES] = lines[r : r + 1]


def send_back_kernel(z, rows, odd, part, *refs):
    B, mt = z.B, z.mt
    states, outs = refs[:-B], refs[-B:]
    places = [(ref, i) for ref in states for i in range(ref.shape[0])]
    for k in range(B):
        src = exchange_part(z, k, odd[0], part[0])
        for t in range(mt):
            lanes = pl.ds(pl.multiple_of(src * z.main + t * LANES, LANES), LANES)
            for i, (ref, at) in enumerate(places):
                outs[k][i * mt + t] = ref[at, :, lanes]
        for count, used, deep, base, lane in z.folds(rows)[0]:
            group = lane_group(count)
            for rr in range(deep):
                tile = jnp.zeros((z.C, LANES), F32)
                for i in range(used):
                    ref, at = places[rr + i * deep]
                    shift = lax.rem((i - src) * count + LANES, LANES)
                    moved = pltpu.roll(ref[at, :, lane : lane + LANES], shift, axis=1)
                    tile = jnp.where(group == i, moved, tile)
                outs[k][base + rr] = tile


def restore_kernel(z, odd, part, *refs):
    B, R, C, mt = z.B, z.R, z.C, z.mt
    got, (spec_out, ocean_out, wide, spec, ocean) = refs[: 2 * B], refs[2 * B :]
    at = 0
    for which, rows in enumerate((z.edge_rows, z.inner_rows)):
        folds, slabs = z.folds(rows)
        for k in range(B):
            c = exchange_share(z, k, odd[0], part[0])
            wide[at : at + slabs, pl.ds(pl.multiple_of(c * C, PAD), C), :] = got[which * B + k][...]
        for half in range(z.W // LANES):
            cols = slice(half * LANES, (half + 1) * LANES)
            for i, r in enumerate(rows):
                for t in range(mt):
                    place = pl.ds(t * LANES * R + r, LANES, stride=R)
                    spec[half, place, :] = wide[at + i * mt + t, cols].T
            for (count, used, deep, base, _), dst, first in zip(folds, (spec, ocean), (z.main, 0)):
                for rr in range(deep):
                    turned = wide[at + base + rr, cols].T
                    for i in range(used):
                        place = pl.ds(first * R + rows[rr + i * deep], count, stride=R)
                        dst[half, place, :] = turned[i * count : (i + 1) * count]
        at += slabs
    for half in range(z.W // LANES):
        cols = slice(half * LANES, (half + 1) * LANES)
        spec_out[:, cols] = spec[half]
        ocean_out[:, cols] = ocean[half]


def weights_kernel(z, linear, square, drift, weights, drift_weights):
    B, nb, main, nr, NB, L = z.B, z.nb, z.main, z.nr, z.NB, z.L

    def put(dst, first, lanes, turned):
        for s in range(B):
            dst[first + s * main : first + (s + 1) * main, lanes] = turned[
                s * nb : s * nb + main
            ]
            tail = first + B * main + s * nr
            dst[tail : tail + nr, lanes] = turned[s * nb + main : (s + 1) * nb]

    for n, source in enumerate((linear, square)):
        for s in range(B):
            for t in range(z.mt):
                block = source[s * nb + t * LANES : s * nb + (t + 1) * LANES, :]
                lane = s * main + t * LANES
                put(weights, n * NB, slice(lane, lane + LANES), block.T)
        tails = [source[s * nb + main : (s + 1) * nb, :] for s in range(B)]
        block = jnp.concatenate(tails, axis=0)
        put(weights, n * NB, slice(B * main, NB), block.T)

    row = lax.broadcasted_iota(jnp.int32, (LANES, LANES), 0)
    lane = lax.broadcasted_iota(jnp.int32, (LANES, LANES), 1)
    part, comp, level = lane // (2 * L), (lane // L) % 2, lane % L
    pick = jnp.where(row == 2 * (part * L + level) + 1 - comp, 1.0, 0.0).astype(BF16)
    turned = jnp.dot(drift[...].T, pick, preferred_element_type=F32).astype(BF16)
    put(drift_weights, 0, slice(0, LANES), turned)


def advance(
    z, sea_rows, rows, outs, cut, sea_at, speed, weights, drift_weights, moved, moved_twice,
    known=None, kept=None,
):
    NB, CH, L = z.NB, z.CH, z.L
    known, kept = known or {}, kept or {}
    n = len(rows)
    first = [r for r in range(1, n - 1) if r not in known]
    assert first == list(range(first[0], first[-1] + 1))
    E = rows[0][0].shape[1]
    N = E - 2 * cut
    keep = slice(cut, cut + N)
    sea_cols = pl.ds(sea_at, E)
    places = [(ref, i) for ref in outs for i in range(ref.shape[0])]

    def sea_row(place):
        return place[0][place[1], sea_cols]

    for r in range(min(first[0] - 1, 1), max(first[-1] + 2, n - 1)):
        ref, i = rows[r]
        surface = ref[i, :, NB:CH]
        moved[0, r] = DOPPLER * jnp.tanh(jnp.broadcast_to(surface[:, 0:1], (E, LANES)))
        moved[1, r] = DOPPLER * jnp.tanh(jnp.broadcast_to(surface[:, L : L + 1], (E, LANES)))

    def advect(read, write, start, stop, speed_cx, speed_cy):
        plus_before, waiting = None, None
        for r in range(start - 1, stop + 1):
            energy = read(r)
            speed_x = speed_cx + moved[0, r]
            if r >= start:
                minus = jnp.minimum(speed_x, 0.0) * energy
            if r > start:
                write(r - 1, (waiting - minus) * sea_row(sea_rows[r - 1]))
            if r < stop:
                plus = jnp.maximum(speed_x, 0.0) * energy
            if start <= r < stop:
                speed_y = speed_cy + moved[1, r]
                plus_y = jnp.maximum(speed_y, 0.0) * energy
                minus_y = jnp.minimum(speed_y, 0.0) * energy
                waiting = (
                    energy
                    - ((plus - plus_before) - minus)
                    - (
                        (plus_y - pltpu.roll(plus_y, 1, axis=0))
                        + (pltpu.roll(minus_y, E - 1, axis=0) - minus_y)
                    )
                )
            plus_before = plus

    def one_tile(j, carry):
        lanes = pl.ds(pl.multiple_of(j * LANES, LANES), LANES)
        speed_cx = speed[0:1, lanes]
        speed_cy = speed[1:2, lanes]

        def read_first(r):
            ref, i = rows[r]
            return ref[i, :, lanes]

        def write_first(r, value):
            moved[2, r] = value
            if r in kept:
                ref, i = kept[r]
                ref[i, :, lanes] = value

        def read_second(r):
            if r in known:
                ref, i = known[r]
                return ref[i, :, lanes]
            return moved[2, r]

        def write_second(r, value):
            moved_twice[r - 2, :, lanes] = value[keep]

        advect(read_first, write_first, first[0], first[-1] + 1, speed_cx, speed_cy)
        advect(read_second, write_second, 2, n - 2, speed_cx, speed_cy)
        return carry

    lax.fori_loop(0, NB // LANES, one_tile, 0)

    count = len(places)
    own_sea = sea_rows[2 : n - 2]
    energy = moved_twice[...].reshape(count * N, NB)
    squares = energy * energy
    interaction = jnp.dot(
        energy.astype(BF16), weights[:NB], preferred_element_type=F32
    ) + jnp.dot(squares.astype(BF16), weights[NB:], preferred_element_type=F32)
    total = jnp.sum(squares, axis=1, keepdims=True)
    sea_here = jnp.concatenate([sea_row(place)[keep] for place in own_sea], axis=0)
    scale = (DT_SOURCE * sea_here[:, 0:1]) / (1.0 + total / NB)
    fresh = energy + scale * (interaction * energy)
    for i, (ref, at) in enumerate(places):
        ref[at, :, 0:NB] = fresh[i * N : (i + 1) * N]
    drift = jnp.dot(fresh.astype(BF16), drift_weights[...], preferred_element_type=F32)

    comp = (lax.broadcasted_iota(jnp.int32, (1, LANES), 1) // L) % 2
    sign = jnp.where(comp == 0, 1.0, -1.0).astype(F32)
    for i, (out, at) in enumerate(places):
        here, before, after = [
            ref[row, :, NB:CH] for ref, row in (rows[i + 2], rows[i + 1], rows[i + 3])
        ]
        lap = (
            (after + before)
            + (pltpu.roll(here, E - 1, axis=0) + pltpu.roll(here, 1, axis=0))
            - 4.0 * here
        )[keep]
        centre = here[keep]
        other = jnp.where(
            comp == 0, pltpu.roll(centre, LANES - L, axis=1), pltpu.roll(centre, L, axis=1)
        )
        turn = sign * (CORIOLIS * (other + drift[i * N : (i + 1) * N]))
        out[at, :, NB:CH] = (
            centre + DT_OCEAN * (turn + VISCOSITY * lap)
        ) * sea_row(own_sea[i])[keep]


def listed(*refs):
    return [(ref, i) for ref in refs for i in range(ref.shape[0])]


def inner_kernel(z, first, cut, sea_at, top, inner, bottom, sea, speed, weights, drift_weights, *refs):
    out, for_edges, (moved, moved_twice) = refs[0], refs[1:-2], refs[-2:]
    kept = {}
    if for_edges:
        kept = {1 + i: (for_edges[0], i) for i in range(EDGE)}
        kept |= {z.R - 1 - EDGE + i: (for_edges[1], i) for i in range(EDGE)}
    advance(
        z, listed(sea), listed(top, inner, bottom), [out], cut, sea_at, speed, weights,
        drift_weights, moved, moved_twice, kept=kept,
    )


def read_sea(halo, sea):
    for i in range(EDGE):
        sea[i] = spread_line(halo[i, 0:1, 0:LANES])[: halo.shape[1]]
    return sea


def top_kernel(z, first, cut, sea_at, up, top, inner, sea, *refs):
    inputs, outs = refs[:-4] if first else refs[:-3], refs[-4:] if first else refs[-3:]
    *given, speed, weights, drift_weights = inputs
    out, moved, moved_twice = outs[0], outs[-2], outs[-1]
    sea_up = read_sea(up, outs[1]) if first else given.pop(0)
    known = {3 + i: (given[0], i) for i in range(EDGE)} if given else {}
    rows = listed(up, top) + listed(inner)[:EDGE]
    sea_rows = (listed(sea_up) + listed(sea))[: len(rows)]
    advance(
        z, sea_rows, rows, [out], cut, sea_at, speed, weights, drift_weights, moved,
        moved_twice, known=known,
    )


def bottom_kernel(z, first, cut, sea_at, down, bottom, inner, sea, *refs):
    inputs, outs = refs[:-4] if first else refs[:-3], refs[-4:] if first else refs[-3:]
    *given, speed, weights, drift_weights = inputs
    out, moved, moved_twice = outs[0], outs[-2], outs[-1]
    sea_down = read_sea(down, outs[1]) if first else given.pop(0)
    known = {1 + i: (given[0], i) for i in range(EDGE)} if given else {}
    rows = listed(inner)[-EDGE:] + listed(bottom, down)
    sea_rows = (listed(sea) + listed(sea_down))[-len(rows) :]
    advance(
        z, sea_rows, rows, [out], cut, sea_at, speed, weights, drift_weights, moved,
        moved_twice, known=known,
    )


def speeds(z):
    lane = jnp.arange(z.NB, dtype=jnp.int32)
    head = (lane // z.main) * z.nb + lane % z.main
    rest = lane - z.B * z.main
    tail = (rest // z.nr) * z.nb + z.main + rest % z.nr
    bin_index = jnp.where(lane < z.B * z.main, head, tail)
    direction = (bin_index // NFREQ).astype(F32)
    frequency = (bin_index % NFREQ).astype(F32)
    group_speed = 0.4 / (1.0 + frequency / 16.0)
    bin_angle = (2.0 * jnp.pi / NDIR) * direction
    zeros = jnp.zeros_like(bin_angle)
    rows = [group_speed * jnp.cos(bin_angle), group_speed * jnp.sin(bin_angle)] + [zeros] * 6
    return jnp.stack(rows)


def cost(flops, moved):
    return pl.CostEstimate(flops=int(flops), bytes_accessed=int(moved), transcendentals=0)


def per_device(G, B, spectrum, sea_mask, kernel_linear, kernel_square, drift_kernel, ocean):
    nb, R, W = spectrum.shape
    L = ocean.shape[1]
    z = Sizes(B, nb, L, R, W)
    C, NB, CH = z.C, z.NB, z.CH
    half = B // 2
    axes = ("geo", "bins")
    geo, part = lax.axis_index("geo"), lax.axis_index("bins")

    def device_at(q, c):
        return ((q // 2) * 2 + c // half) * B + 2 * (c % half) + q % 2

    forward = [
        [
            (g * B + b, device_at(g, exchange_share(z, k, g % 2, b)))
            for g in range(G)
            for b in range(B)
        ]
        for k in range(B)
    ]
    pairs = [(q, c) for q in range(G) for c in range(B)]
    to_next_row = [(device_at(q, c), device_at((q + 1) % G, c)) for q, c in pairs]
    to_prev_row = [(t, s) for s, t in to_next_row]
    who = ((geo % 2).astype(jnp.int32).reshape(1), part.astype(jnp.int32).reshape(1))

    width = C + 2 * PAD
    all_slabs = z.slabs(z.edge_rows) + z.slabs(z.inner_rows)
    columns_scratch = [
        pltpu.VMEM((W // LANES, nb * R, LANES), F32),
        pltpu.VMEM((W // LANES, 2 * L * R, LANES), F32),
    ]
    def pack(rows):
        slabs = z.slabs(rows)
        lines = slabs * width + (R if rows == z.edge_rows else 0)
        return pl.pallas_call(
            functools.partial(pack_kernel, z, rows),
            out_shape=[jax.ShapeDtypeStruct((lines, LANES), F32)] * B,
            in_specs=[SMEM] * 2 + [HBM] * 3,
            out_specs=[VMEM] * B,
            scratch_shapes=columns_scratch
            + [
                pltpu.VMEM((R, W), jnp.int32),
                pltpu.VMEM((slabs, W + 2 * PAD, LANES), F32),
                pltpu.SemaphoreType.DMA((3, W // LANES)),
            ],
            compiler_params=params(58),
            name="pack",
        )(*who, spectrum.reshape(nb * R, W), ocean.reshape(2 * L * R, W), sea_mask)

    packed = pack(z.edge_rows)
    got = [lax.ppermute(packed[k], axes, forward[k]) for k in range(B)]
    packed = pack(z.inner_rows)

    weights, drift_weights = pl.pallas_call(
        functools.partial(weights_kernel, z),
        out_shape=(
            jax.ShapeDtypeStruct((2 * NB, NB), BF16),
            jax.ShapeDtypeStruct((NB, LANES), BF16),
        ),
        in_specs=[VMEM] * 3,
        out_specs=(VMEM,) * 2,
        compiler_params=params(24),
        cost_estimate=cost(2e9, 4 * NB * NB * 2),
        name="weights",
    )(kernel_linear, kernel_square, drift_kernel)
    speed = speeds(z)
    *got, weights, drift_weights, speed = lax.optimization_barrier(
        (*got, weights, drift_weights, speed)
    )

    def unpack(rows, received, shapes):
        return pl.pallas_call(
            functools.partial(unpack_kernel, z, rows),
            out_shape=[jax.ShapeDtypeStruct((n, width, lanes), F32) for n, lanes in shapes],
            in_specs=[SMEM] * 2 + [VMEM] * B,
            out_specs=[VMEM] * len(shapes),
            compiler_params=params(16),
            name="unpack",
        )(*who, *received)

    top, bottom, sea = unpack(
        z.edge_rows, got[:B], [(EDGE, CH), (EDGE, CH), (R, LANES)]
    )
    *blocks, top = lax.optimization_barrier((*packed[half:], top))
    blocks = list(packed[:half]) + blocks
    got = [lax.ppermute(blocks[k], axes, forward[k]) for k in range(B)]
    (inner,) = unpack(z.inner_rows, got, [(R - 2 * EDGE, CH)])

    def step_call(body, first, cut, sea_at, count, deepest, inputs, more=()):
        width = inputs[0].shape[1]
        n = width - 2 * cut
        shapes = [(count, n, CH)] + [(EDGE, width, lanes) for lanes in more]
        return pl.pallas_call(
            functools.partial(body, z, first, cut, sea_at),
            out_shape=[jax.ShapeDtypeStruct(shape, F32) for shape in shapes],
            in_specs=[VMEM] * (len(inputs) + 3),
            out_specs=[VMEM] * len(shapes),
            scratch_shapes=[
                pltpu.VMEM((3, deepest, width, LANES), F32),
                pltpu.VMEM((count, n, NB), F32),
            ],
            compiler_params=params(24),
            cost_estimate=cost(count * 1e8, count * 1e5),
            name=body.__name__,
        )(*inputs, speed, weights, drift_weights)

    sea_up, sea_down = [], []
    for step in range(STEPS):
        valid = EDGE * (STEPS - 1 - step)
        margin = (width - C) // 2
        cut = margin - valid if valid == 0 or (margin - valid) % 4 == 0 else 0
        sea_at = PAD - margin
        down = lax.ppermute(top, axes, to_prev_row)
        up = lax.ppermute(bottom, axes, to_next_row)
        first = step == 0

        def advance_inner():
            return step_call(
                inner_kernel, first, cut, sea_at, R - 2 * EDGE, R, (top, inner, bottom, sea),
                () if first else (NB, NB),
            )

        given = ()
        if not first:
            new_inner, *given = advance_inner()
        new_bottom, *found = step_call(
            bottom_kernel, first, cut, sea_at, EDGE, 3 * EDGE,
            (down, bottom, inner, sea, *sea_down, *given[1:]),
            (LANES,) if first else (),
        )
        sea_down = sea_down or found
        new_top, *found = step_call(
            top_kernel, first, cut, sea_at, EDGE, 3 * EDGE,
            (up, top, inner, sea, *sea_up, *given[:1]),
            (LANES,) if first else (),
        )
        sea_up = sea_up or found
        if first:
            inner, new_top = lax.optimization_barrier((inner, new_top))
            (new_inner,) = advance_inner()
        top, inner, bottom = new_top, new_inner, new_bottom
        width -= 2 * cut

    def send_back(rows, states):
        shape = jax.ShapeDtypeStruct((z.slabs(rows), C, LANES), F32)
        return pl.pallas_call(
            functools.partial(send_back_kernel, z, rows),
            out_shape=[shape] * B,
            in_specs=[SMEM] * 2 + [VMEM] * len(states),
            out_specs=[VMEM] * B,
            compiler_params=params(16),
            name="send_back",
        )(*who, *states)

    packed = send_back(z.inner_rows, [inner]), send_back(z.edge_rows, [top, bottom])
    packed = list(packed[1]) + list(packed[0])
    back = [
        lax.ppermute(packed[i], axes, [(t, s) for s, t in forward[i % B]]) for i in range(2 * B)
    ]
    spectrum_out, ocean_out = pl.pallas_call(
        functools.partial(restore_kernel, z),
        out_shape=(
            jax.ShapeDtypeStruct((nb * R, W), F32),
            jax.ShapeDtypeStruct((2 * L * R, W), F32),
        ),
        in_specs=[SMEM] * 2 + [VMEM] * (2 * B),
        out_specs=(VMEM,) * 2,
        scratch_shapes=[pltpu.VMEM((all_slabs, W, LANES), F32)] + columns_scratch,
        compiler_params=params(24),
        name="restore",
    )(*who, *back)
    return spectrum_out.reshape(nb, R, W), ocean_out.reshape(2, L, R, W)


def solution(mesh):
    return jax.shard_map(
        functools.partial(per_device, mesh.shape["geo"], mesh.shape["bins"]),
        mesh=mesh,
        in_specs=(
            P("bins", "geo", None),
            P("geo", None),
            P(),
            P(),
            P(),
            P(None, "bins", "geo", None),
        ),
        out_specs=(P("bins", "geo", None), P(None, "bins", "geo", None)),
        check_vma=False,
    )
```

```python
import functools

import jax
import jax.numpy as jnp
from jax import lax
from jax.experimental import pallas as pl
from jax.experimental.pallas import tpu as pltpu
from jax.sharding import PartitionSpec as P

NDIR = 36
NFREQ = 32
STEPS = 3
SUB = 2
DT_SOURCE = 0.5
DT_OCEAN = 0.2
CORIOLIS = 1.0
VISCOSITY = 1.0
DOPPLER = 0.1

LANES = 128
PAD = 8
EDGE = 2
VMEM = pl.BlockSpec(memory_space=pltpu.VMEM)
SMEM = pl.BlockSpec(memory_space=pltpu.SMEM)
HBM = pl.BlockSpec(memory_space=pltpu.HBM)
F32 = jnp.float32
BF16 = jnp.bfloat16


def params(mib):
    return pltpu.CompilerParams(vmem_limit_bytes=mib * 1024 * 1024)


class Sizes:
    def __init__(self, parts, bins_here, levels_here, rows, width):
        self.B, self.nb, self.L, self.R, self.W = parts, bins_here, levels_here, rows, width
        self.C = width // parts
        self.mt = bins_here // LANES
        self.main = self.mt * LANES
        self.nr = bins_here - self.main
        self.no = 2 * levels_here
        self.NB = parts * bins_here
        self.CH = self.NB + LANES
        self.edge_rows = (0, 1, rows - 2, rows - 1)
        self.inner_rows = tuple(range(2, rows - 2))
        self.half = parts // 2
        assert self.half & (self.half - 1) == 0 and self.half > 1
        assert self.nr * parts == LANES and self.no * parts == LANES

    def folds(self, rows):
        out, base = [], len(rows) * self.mt
        for count, lane in ((self.nr, self.B * self.main), (self.no, self.NB)):
            used = min(LANES // count, len(rows))
            deep = len(rows) // used
            assert deep * used == len(rows)
            out.append((count, used, deep, base, lane))
            base += deep
        return out, base

    def slabs(self, rows):
        return self.folds(rows)[1]


def exchange_share(z, k, odd, part):
    core = part % 2
    flip, delta = (k // z.half) ^ core, (k % z.half) ^ core
    return (odd ^ flip) * z.half + ((part // 2) ^ delta)


def exchange_part(z, k, odd, part):
    core = (k // z.half) ^ odd ^ (part % 2)
    delta = (k % z.half) ^ core
    return ((part // 2) ^ delta) * 2 + core


def lane_group(width):
    return lax.broadcasted_iota(jnp.int32, (1, LANES), 1) // width


def pack_kernel(z, rows, odd, part, spec_in, ocean_in, mask_in, *refs):
    B, R, C, W, mt = z.B, z.R, z.C, z.W, z.mt
    outs, (spec, ocean, mask, wide, sems) = refs[:B], refs[B:]
    E = C + 2 * PAD
    copies = []
    for half in range(W // LANES):
        cols = pl.ds(half * LANES, LANES)
        for n, (src, dst) in enumerate(((spec_in, spec), (ocean_in, ocean))):
            copies.append(pltpu.make_async_copy(src.at[:, cols], dst.at[half], sems.at[n, half]))
            copies[-1].start()
    mask_copy = pltpu.make_async_copy(mask_in, mask, sems.at[2, 0])
    mask_copy.start()
    wide[:, 0:PAD, :] = jnp.zeros((wide.shape[0], PAD, LANES), F32)
    wide[:, PAD + W : W + 2 * PAD, :] = jnp.zeros((wide.shape[0], PAD, LANES), F32)
    folds, slabs = z.folds(rows)
    for half in range(W // LANES):
        for copy in copies[2 * half : 2 * half + 2]:
            copy.wait()
        cols = slice(PAD + half * LANES, PAD + (half + 1) * LANES)
        for i, r in enumerate(rows):
            for t in range(mt):
                block = spec[half, pl.ds(t * LANES * R + r, LANES, stride=R), :]
                wide[i * mt + t, cols] = block.T
        for (count, used, deep, base, _), src, first in zip(folds, (spec, ocean), (z.main, 0)):
            for rr in range(deep):
                pieces = [
                    src[half, pl.ds(first * R + rows[rr + i * deep], count, stride=R), :]
                    for i in range(used)
                ]
                if used * count < LANES:
                    pieces.append(jnp.zeros((LANES - used * count, LANES), F32))
                wide[base + rr, cols] = jnp.concatenate(pieces, axis=0).T
    mask_copy.wait()
    sea = jnp.concatenate([mask[...].astype(F32), jnp.zeros((R, LANES), F32)], axis=1)
    for k, out in enumerate(outs):
        share = exchange_share(z, k, odd[0], part[0])
        start = pl.multiple_of(share * C, PAD)
        block = wide[:, pl.ds(start, E), :]
        out[0 : slabs * E] = block.reshape(slabs * E, LANES)
        if rows == z.edge_rows:
            shift = lax.rem(W + LANES + PAD - start, W + LANES)
            out[slabs * E : slabs * E + R] = pltpu.roll(sea, shift, axis=1)[:, :LANES]


def spread_line(line):
    return jnp.broadcast_to(line, (LANES, LANES)).T


def unpack_kernel(z, rows, odd, part, *refs):
    B, mt = z.B, z.mt
    got, outs = refs[:B], refs[B:]
    E = z.C + 2 * PAD
    if rows == z.edge_rows:
        sea = outs[-1]
        outs = outs[:-1]
        lines = got[0][z.slabs(rows) * E : z.slabs(rows) * E + z.R]
        for r in range(z.R):
            sea[r] = spread_line(lines[r : r + 1])[:E]
    places = [(ref, i) for ref in outs for i in range(ref.shape[0])]
    src = [exchange_part(z, k, odd[0], part[0]) for k in range(B)]
    for k in range(B):
        for t in range(mt):
            lanes = pl.ds(pl.multiple_of(src[k] * z.main + t * LANES, LANES), LANES)
            for i, (ref, at) in enumerate(places):
                ref[at, :, lanes] = got[k][(i * mt + t) * E : (i * mt + t + 1) * E]
    for count, used, deep, base, lane in z.folds(rows)[0]:
        group = lane_group(count)
        for i, (ref, at) in enumerate(places):
            tile = jnp.zeros(ref.shape[1:2] + (LANES,), F32)
            for k in range(B):
                shift = lax.rem((src[k] - i // deep) * count + LANES, LANES)
                slab = base + i % deep
                moved = pltpu.roll(got[k][slab * E : (slab + 1) * E], shift, axis=1)
                tile = jnp.where(group == src[k], moved, tile)
            ref[at, :, lane : lane + LANES] = tile
    if rows == z.edge_rows:
        for i, (ref, at) in enumerate(places):
            r = rows[i]
            ref[at, 0:1, 0:LANES] = lines[r : r + 1]


def send_back_kernel(z, rows, odd, part, *refs):
    B, mt = z.B, z.mt
    states, outs = refs[:-B], refs[-B:]
    places = [(ref, i) for ref in states for i in range(ref.shape[0])]
    for k in range(B):
        src = exchange_part(z, k, odd[0], part[0])
        for t in range(mt):
            lanes = pl.ds(pl.multiple_of(src * z.main + t * LANES, LANES), LANES)
            for i, (ref, at) in enumerate(places):
                outs[k][i * mt + t] = ref[at, :, lanes]
        for count, used, deep, base, lane in z.folds(rows)[0]:
            group = lane_group(count)
            for rr in range(deep):
                tile = jnp.zeros((z.C, LANES), F32)
                for i in range(used):
                    ref, at = places[rr + i * deep]
                    shift = lax.rem((i - src) * count + LANES, LANES)
                    moved = pltpu.roll(ref[at, :, lane : lane + LANES], shift, axis=1)
                    tile = jnp.where(group == i, moved, tile)
                outs[k][base + rr] = tile


def restore_kernel(z, odd, part, *refs):
    B, R, C, mt = z.B, z.R, z.C, z.mt
    got, (spec_out, ocean_out, wide, spec, ocean) = refs[: 2 * B], refs[2 * B :]
    at = 0
    for which, rows in enumerate((z.edge_rows, z.inner_rows)):
        folds, slabs = z.folds(rows)
        for k in range(B):
            c = exchange_share(z, k, odd[0], part[0])
            wide[at : at + slabs, pl.ds(pl.multiple_of(c * C, PAD), C), :] = got[which * B + k][...]
        for half in range(z.W // LANES):
            cols = slice(half * LANES, (half + 1) * LANES)
            for i, r in enumerate(rows):
                for t in range(mt):
                    place = pl.ds(t * LANES * R + r, LANES, stride=R)
                    spec[half, place, :] = wide[at + i * mt + t, cols].T
            for (count, used, deep, base, _), dst, first in zip(folds, (spec, ocean), (z.main, 0)):
                for rr in range(deep):
                    turned = wide[at + base + rr, cols].T
                    for i in range(used):
                        place = pl.ds(first * R + rows[rr + i * deep], count, stride=R)
                        dst[half, place, :] = turned[i * count : (i + 1) * count]
        at += slabs
    for half in range(z.W // LANES):
        cols = slice(half * LANES, (half + 1) * LANES)
        spec_out[:, cols] = spec[half]
        ocean_out[:, cols] = ocean[half]


def weights_kernel(z, linear, square, drift, weights, drift_weights):
    B, nb, main, nr, NB, L = z.B, z.nb, z.main, z.nr, z.NB, z.L

    def put(dst, first, lanes, turned):
        for s in range(B):
            dst[first + s * main : first + (s + 1) * main, lanes] = turned[
                s * nb : s * nb + main
            ]
            tail = first + B * main + s * nr
            dst[tail : tail + nr, lanes] = turned[s * nb + main : (s + 1) * nb]

    for n, source in enumerate((linear, square)):
        for s in range(B):
            for t in range(z.mt):
                block = source[s * nb + t * LANES : s * nb + (t + 1) * LANES, :]
                lane = s * main + t * LANES
                put(weights, n * NB, slice(lane, lane + LANES), block.T)
        tails = [source[s * nb + main : (s + 1) * nb, :] for s in range(B)]
        block = jnp.concatenate(tails, axis=0)
        put(weights, n * NB, slice(B * main, NB), block.T)

    row = lax.broadcasted_iota(jnp.int32, (LANES, LANES), 0)
    lane = lax.broadcasted_iota(jnp.int32, (LANES, LANES), 1)
    part, comp, level = lane // (2 * L), (lane // L) % 2, lane % L
    pick = jnp.where(row == 2 * (part * L + level) + 1 - comp, 1.0, 0.0).astype(BF16)
    turned = jnp.dot(drift[...].T, pick, preferred_element_type=F32).astype(BF16)
    put(drift_weights, 0, slice(0, LANES), turned)


def advance(
    z, sea_rows, rows, outs, cut, sea_at, speed, weights, drift_weights, moved, moved_twice,
    known=None, kept=None,
):
    NB, CH, L = z.NB, z.CH, z.L
    known, kept = known or {}, kept or {}
    n = len(rows)
    first = [r for r in range(1, n - 1) if r not in known]
    assert first == list(range(first[0], first[-1] + 1))
    E = rows[0][0].shape[1]
    N = E - 2 * cut
    keep = slice(cut, cut + N)
    sea_cols = pl.ds(sea_at, E)
    places = [(ref, i) for ref in outs for i in range(ref.shape[0])]

    def sea_row(place):
        return place[0][place[1], sea_cols]

    needed = range(min(first[0] - 1, 1), max(first[-1] + 2, n - 1))
    lane = lax.broadcasted_iota(jnp.int32, (1, LANES), 1)
    currents = jnp.zeros((E, LANES), F32)
    for r in needed:
        ref, i = rows[r]
        surface = ref[i, :, NB:CH]
        for c in range(2):
            brought = pltpu.roll(surface, (2 * r + c - c * L) % LANES, axis=1)
            currents = jnp.where(lane == 2 * r + c, brought, currents)
    currents = DOPPLER * jnp.tanh(currents)
    for r in needed:
        for c in range(2):
            at = 2 * r + c
            moved[c, r] = jnp.broadcast_to(currents[:, at : at + 1], (E, LANES))

    def advect(read, write, start, stop, speed_cx, speed_cy):
        plus_before, waiting = None, None
        for r in range(start - 1, stop + 1):
            energy = read(r)
            speed_x = speed_cx + moved[0, r]
            if r >= start:
                minus = jnp.minimum(speed_x, 0.0) * energy
            if r > start:
                write(r - 1, (waiting - minus) * sea_row(sea_rows[r - 1]))
            if r < stop:
                plus = jnp.maximum(speed_x, 0.0) * energy
            if start <= r < stop:
                speed_y = speed_cy + moved[1, r]
                plus_y = jnp.maximum(speed_y, 0.0) * energy
                minus_y = jnp.minimum(speed_y, 0.0) * energy
                waiting = (
                    energy
                    - ((plus - plus_before) - minus)
                    - (
                        (plus_y - pltpu.roll(plus_y, 1, axis=0))
                        + (pltpu.roll(minus_y, E - 1, axis=0) - minus_y)
                    )
                )
            plus_before = plus

    def one_tile(j, carry):
        lanes = pl.ds(pl.multiple_of(j * LANES, LANES), LANES)
        speed_cx = speed[0:1, lanes]
        speed_cy = speed[1:2, lanes]

        def read_first(r):
            ref, i = rows[r]
            return ref[i, :, lanes]

        def write_first(r, value):
            moved[2, r] = value
            if r in kept:
                ref, i = kept[r]
                ref[i, :, lanes] = value

        def read_second(r):
            if r in known:
                ref, i = known[r]
                return ref[i, :, lanes]
            return moved[2, r]

        def write_second(r, value):
            moved_twice[r - 2, :, lanes] = value[keep]

        advect(read_first, write_first, first[0], first[-1] + 1, speed_cx, speed_cy)
        advect(read_second, write_second, 2, n - 2, speed_cx, speed_cy)
        return carry

    lax.fori_loop(0, NB // LANES, one_tile, 0)

    count = len(places)
    own_sea = sea_rows[2 : n - 2]
    energy = moved_twice[...].reshape(count * N, NB)
    squares = energy * energy
    both = jnp.concatenate([energy.astype(BF16), squares.astype(BF16)], axis=1)
    interaction = jnp.dot(both, weights[...], preferred_element_type=F32)
    total = jnp.sum(squares, axis=1, keepdims=True)
    sea_here = jnp.concatenate([sea_row(place)[keep] for place in own_sea], axis=0)
    scale = (DT_SOURCE * sea_here[:, 0:1]) / (1.0 + total / NB)
    fresh = energy + scale * (interaction * energy)
    for i, (ref, at) in enumerate(places):
        ref[at, :, 0:NB] = fresh[i * N : (i + 1) * N]
    drift = jnp.dot(fresh.astype(BF16), drift_weights[...], preferred_element_type=F32)

    comp = (lax.broadcasted_iota(jnp.int32, (1, LANES), 1) // L) % 2
    sign = jnp.where(comp == 0, 1.0, -1.0).astype(F32)
    for i, (out, at) in enumerate(places):
        here, before, after = [
            ref[row, :, NB:CH] for ref, row in (rows[i + 2], rows[i + 1], rows[i + 3])
        ]
        lap = (
            (after + before)
            + (pltpu.roll(here, E - 1, axis=0) + pltpu.roll(here, 1, axis=0))
            - 4.0 * here
        )[keep]
        centre = here[keep]
        other = jnp.where(
            comp == 0, pltpu.roll(centre, LANES - L, axis=1), pltpu.roll(centre, L, axis=1)
        )
        turn = sign * (CORIOLIS * (other + drift[i * N : (i + 1) * N]))
        out[at, :, NB:CH] = (
            centre + DT_OCEAN * (turn + VISCOSITY * lap)
        ) * sea_row(own_sea[i])[keep]


def listed(*refs):
    return [(ref, i) for ref in refs for i in range(ref.shape[0])]


def inner_kernel(z, first, cut, sea_at, top, inner, bottom, sea, speed, weights, drift_weights, *refs):
    out, for_edges, (moved, moved_twice) = refs[0], refs[1:-2], refs[-2:]
    kept = {}
    if for_edges:
        kept = {1 + i: (for_edges[0], i) for i in range(EDGE)}
        kept |= {z.R - 1 - EDGE + i: (for_edges[1], i) for i in range(EDGE)}
    advance(
        z, listed(sea), listed(top, inner, bottom), [out], cut, sea_at, speed, weights,
        drift_weights, moved, moved_twice, kept=kept,
    )


def read_sea(halo, sea):
    for i in range(EDGE):
        sea[i] = spread_line(halo[i, 0:1, 0:LANES])[: halo.shape[1]]
    return sea


def top_kernel(z, first, cut, sea_at, up, top, inner, sea, *refs):
    inputs, outs = refs[:-4] if first else refs[:-3], refs[-4:] if first else refs[-3:]
    *given, speed, weights, drift_weights = inputs
    out, moved, moved_twice = outs[0], outs[-2], outs[-1]
    sea_up = read_sea(up, outs[1]) if first else given.pop(0)
    known = {3 + i: (given[0], i) for i in range(EDGE)} if given else {}
    rows = listed(up, top) + listed(inner)[:EDGE]
    sea_rows = (listed(sea_up) + listed(sea))[: len(rows)]
    advance(
        z, sea_rows, rows, [out], cut, sea_at, speed, weights, drift_weights, moved,
        moved_twice, known=known,
    )


def bottom_kernel(z, first, cut, sea_at, down, bottom, inner, sea, *refs):
    inputs, outs = refs[:-4] if first else refs[:-3], refs[-4:] if first else refs[-3:]
    *given, speed, weights, drift_weights = inputs
    out, moved, moved_twice = outs[0], outs[-2], outs[-1]
    sea_down = read_sea(down, outs[1]) if first else given.pop(0)
    known = {1 + i: (given[0], i) for i in range(EDGE)} if given else {}
    rows = listed(inner)[-EDGE:] + listed(bottom, down)
    sea_rows = (listed(sea) + listed(sea_down))[-len(rows) :]
    advance(
        z, sea_rows, rows, [out], cut, sea_at, speed, weights, drift_weights, moved,
        moved_twice, known=known,
    )


def speeds(z):
    lane = jnp.arange(z.NB, dtype=jnp.int32)
    head = (lane // z.main) * z.nb + lane % z.main
    rest = lane - z.B * z.main
    tail = (rest // z.nr) * z.nb + z.main + rest % z.nr
    bin_index = jnp.where(lane < z.B * z.main, head, tail)
    direction = (bin_index // NFREQ).astype(F32)
    frequency = (bin_index % NFREQ).astype(F32)
    group_speed = 0.4 / (1.0 + frequency / 16.0)
    bin_angle = (2.0 * jnp.pi / NDIR) * direction
    zeros = jnp.zeros_like(bin_angle)
    rows = [group_speed * jnp.cos(bin_angle), group_speed * jnp.sin(bin_angle)] + [zeros] * 6
    return jnp.stack(rows)


def cost(flops, moved):
    return pl.CostEstimate(flops=int(flops), bytes_accessed=int(moved), transcendentals=0)


def per_device(G, B, spectrum, sea_mask, kernel_linear, kernel_square, drift_kernel, ocean):
    nb, R, W = spectrum.shape
    L = ocean.shape[1]
    z = Sizes(B, nb, L, R, W)
    C, NB, CH = z.C, z.NB, z.CH
    half = B // 2
    axes = ("geo", "bins")
    geo, part = lax.axis_index("geo"), lax.axis_index("bins")

    def device_at(q, c):
        return ((q // 2) * 2 + c // half) * B + 2 * (c % half) + q % 2

    forward = [
        [
            (g * B + b, device_at(g, exchange_share(z, k, g % 2, b)))
            for g in range(G)
            for b in range(B)
        ]
        for k in range(B)
    ]
    pairs = [(q, c) for q in range(G) for c in range(B)]
    to_next_row = [(device_at(q, c), device_at((q + 1) % G, c)) for q, c in pairs]
    to_prev_row = [(t, s) for s, t in to_next_row]
    who = ((geo % 2).astype(jnp.int32).reshape(1), part.astype(jnp.int32).reshape(1))

    width = C + 2 * PAD
    all_slabs = z.slabs(z.edge_rows) + z.slabs(z.inner_rows)
    columns_scratch = [
        pltpu.VMEM((W // LANES, nb * R, LANES), F32),
        pltpu.VMEM((W // LANES, 2 * L * R, LANES), F32),
    ]
    def pack(rows):
        slabs = z.slabs(rows)
        lines = slabs * width + (R if rows == z.edge_rows else 0)
        return pl.pallas_call(
            functools.partial(pack_kernel, z, rows),
            out_shape=[jax.ShapeDtypeStruct((lines, LANES), F32)] * B,
            in_specs=[SMEM] * 2 + [HBM] * 3,
            out_specs=[VMEM] * B,
            scratch_shapes=columns_scratch
            + [
                pltpu.VMEM((R, W), jnp.int32),
                pltpu.VMEM((slabs, W + 2 * PAD, LANES), F32),
                pltpu.SemaphoreType.DMA((3, W // LANES)),
            ],
            compiler_params=params(58),
            name="pack",
        )(*who, spectrum.reshape(nb * R, W), ocean.reshape(2 * L * R, W), sea_mask)

    packed = pack(z.edge_rows)
    got = [lax.ppermute(packed[k], axes, forward[k]) for k in range(B)]
    packed = pack(z.inner_rows)

    weights, drift_weights = pl.pallas_call(
        functools.partial(weights_kernel, z),
        out_shape=(
            jax.ShapeDtypeStruct((2 * NB, NB), BF16),
            jax.ShapeDtypeStruct((NB, LANES), BF16),
        ),
        in_specs=[VMEM] * 3,
        out_specs=(VMEM,) * 2,
        compiler_params=params(24),
        cost_estimate=cost(2e9, 4 * NB * NB * 2),
        name="weights",
    )(kernel_linear, kernel_square, drift_kernel)
    speed = speeds(z)
    *got, weights, drift_weights, speed = lax.optimization_barrier(
        (*got, weights, drift_weights, speed)
    )

    def unpack(rows, received, shapes):
        return pl.pallas_call(
            functools.partial(unpack_kernel, z, rows),
            out_shape=[jax.ShapeDtypeStruct((n, width, lanes), F32) for n, lanes in shapes],
            in_specs=[SMEM] * 2 + [VMEM] * B,
            out_specs=[VMEM] * len(shapes),
            compiler_params=params(16),
            name="unpack",
        )(*who, *received)

    top, bottom, sea = unpack(
        z.edge_rows, got[:B], [(EDGE, CH), (EDGE, CH), (R, LANES)]
    )
    *blocks, top = lax.optimization_barrier((*packed[half:], top))
    blocks = list(packed[:half]) + blocks
    got = [lax.ppermute(blocks[k], axes, forward[k]) for k in range(B)]
    (inner,) = unpack(z.inner_rows, got, [(R - 2 * EDGE, CH)])

    def step_call(body, first, cut, sea_at, count, deepest, inputs, more=()):
        width = inputs[0].shape[1]
        n = width - 2 * cut
        shapes = [(count, n, CH)] + [(EDGE, width, lanes) for lanes in more]
        return pl.pallas_call(
            functools.partial(body, z, first, cut, sea_at),
            out_shape=[jax.ShapeDtypeStruct(shape, F32) for shape in shapes],
            in_specs=[VMEM] * (len(inputs) + 3),
            out_specs=[VMEM] * len(shapes),
            scratch_shapes=[
                pltpu.VMEM((3, deepest, width, LANES), F32),
                pltpu.VMEM((count, n, NB), F32),
            ],
            compiler_params=params(24),
            cost_estimate=cost(count * 1e8, count * 1e5),
            name=body.__name__,
        )(*inputs, speed, weights, drift_weights)

    sea_up, sea_down = [], []
    for step in range(STEPS):
        valid = EDGE * (STEPS - 1 - step)
        margin = (width - C) // 2
        cut = margin - valid if valid == 0 or (margin - valid) % 4 == 0 else 0
        sea_at = PAD - margin
        down = lax.ppermute(top, axes, to_prev_row)
        up = lax.ppermute(bottom, axes, to_next_row)
        first = step == 0

        def advance_inner():
            return step_call(
                inner_kernel, first, cut, sea_at, R - 2 * EDGE, R, (top, inner, bottom, sea),
                () if first else (NB, NB),
            )

        given = ()
        if not first:
            new_inner, *given = advance_inner()
        new_bottom, *found = step_call(
            bottom_kernel, first, cut, sea_at, EDGE, 3 * EDGE,
            (down, bottom, inner, sea, *sea_down, *given[1:]),
            (LANES,) if first else (),
        )
        sea_down = sea_down or found
        new_top, *found = step_call(
            top_kernel, first, cut, sea_at, EDGE, 3 * EDGE,
            (up, top, inner, sea, *sea_up, *given[:1]),
            (LANES,) if first else (),
        )
        sea_up = sea_up or found
        if first:
            inner, new_top = lax.optimization_barrier((inner, new_top))
            (new_inner,) = advance_inner()
        top, inner, bottom = new_top, new_inner, new_bottom
        width -= 2 * cut

    def send_back(rows, states):
        shape = jax.ShapeDtypeStruct((z.slabs(rows), C, LANES), F32)
        return pl.pallas_call(
            functools.partial(send_back_kernel, z, rows),
            out_shape=[shape] * B,
            in_specs=[SMEM] * 2 + [VMEM] * len(states),
            out_specs=[VMEM] * B,
            compiler_params=params(16),
            name="send_back",
        )(*who, *states)

    packed = send_back(z.inner_rows, [inner]), send_back(z.edge_rows, [top, bottom])
    packed = list(packed[1]) + list(packed[0])
    back = [
        lax.ppermute(packed[i], axes, [(t, s) for s, t in forward[i % B]]) for i in range(2 * B)
    ]
    spectrum_out, ocean_out = pl.pallas_call(
        functools.partial(restore_kernel, z),
        out_shape=(
            jax.ShapeDtypeStruct((nb * R, W), F32),
            jax.ShapeDtypeStruct((2 * L * R, W), F32),
        ),
        in_specs=[SMEM] * 2 + [VMEM] * (2 * B),
        out_specs=(VMEM,) * 2,
        scratch_shapes=[pltpu.VMEM((all_slabs, W, LANES), F32)] + columns_scratch,
        compiler_params=params(24),
        name="restore",
    )(*who, *back)
    return spectrum_out.reshape(nb, R, W), ocean_out.reshape(2, L, R, W)


def solution(mesh):
    return jax.shard_map(
        functools.partial(per_device, mesh.shape["geo"], mesh.shape["bins"]),
        mesh=mesh,
        in_specs=(
            P("bins", "geo", None),
            P("geo", None),
            P(),
            P(),
            P(),
            P(None, "bins", "geo", None),
        ),
        out_specs=(P("bins", "geo", None), P(None, "bins", "geo", None)),
        check_vma=False,
    )
```

```python
import functools

import jax
import jax.numpy as jnp
from jax import lax
from jax.experimental import pallas as pl
from jax.experimental.pallas import tpu as pltpu
from jax.sharding import PartitionSpec as P

NDIR = 36
NFREQ = 32
STEPS = 3
SUB = 2
DT_SOURCE = 0.5
DT_OCEAN = 0.2
CORIOLIS = 1.0
VISCOSITY = 1.0
DOPPLER = 0.1

LANES = 128
SUBLANES = 8
PAD = 8
EDGE = 2
VMEM = pl.BlockSpec(memory_space=pltpu.VMEM)
SMEM = pl.BlockSpec(memory_space=pltpu.SMEM)
HBM = pl.BlockSpec(memory_space=pltpu.HBM)
F32 = jnp.float32
BF16 = jnp.bfloat16


def params(mib):
    return pltpu.CompilerParams(vmem_limit_bytes=mib * 1024 * 1024)


class Sizes:
    def __init__(self, parts, bins_here, levels_here, rows, width):
        self.B, self.nb, self.L, self.R, self.W = parts, bins_here, levels_here, rows, width
        self.C = width // parts
        self.mt = bins_here // LANES
        self.main = self.mt * LANES
        self.nr = bins_here - self.main
        self.no = 2 * levels_here
        self.NB = parts * bins_here
        self.CH = self.NB + LANES
        self.edge_rows = (0, 1, rows - 2, rows - 1)
        self.inner_rows = tuple(range(2, rows - 2))
        self.half = parts // 2
        assert self.half & (self.half - 1) == 0 and self.half > 1
        assert self.nr * parts == LANES and self.no * parts == LANES

    def folds(self, rows):
        out, base = [], len(rows) * self.mt
        for count, tile in ((self.nr, self.B * self.mt), (self.no, self.NB // LANES)):
            used = min(LANES // count, len(rows))
            deep = len(rows) // used
            assert deep * used == len(rows)
            out.append((count, used, deep, base, tile))
            base += deep
        return out, base

    def slabs(self, rows):
        return self.folds(rows)[1]


def exchange_share(z, k, odd, part):
    core = part % 2
    flip, delta = (k // z.half) ^ core, (k % z.half) ^ core
    return (odd ^ flip) * z.half + ((part // 2) ^ delta)


def exchange_part(z, k, odd, part):
    core = (k // z.half) ^ odd ^ (part % 2)
    delta = (k % z.half) ^ core
    return ((part // 2) ^ delta) * 2 + core


def lane_group(width):
    return lax.broadcasted_iota(jnp.int32, (1, LANES), 1) // width


def pack_kernel(z, rows, odd, part, spec_in, ocean_in, mask_in, *refs):
    B, R, C, W, mt = z.B, z.R, z.C, z.W, z.mt
    outs, (spec, ocean, mask, wide, sems) = refs[:B], refs[B:]
    E = C + 2 * PAD
    copies = []
    for half in range(W // LANES):
        cols = pl.ds(half * LANES, LANES)
        for n, (src, dst) in enumerate(((spec_in, spec), (ocean_in, ocean))):
            copies.append(pltpu.make_async_copy(src.at[:, cols], dst.at[half], sems.at[n, half]))
            copies[-1].start()
    mask_copy = pltpu.make_async_copy(mask_in, mask, sems.at[2, 0])
    mask_copy.start()
    wide[:, 0:PAD, :] = jnp.zeros((wide.shape[0], PAD, LANES), F32)
    wide[:, PAD + W : W + 2 * PAD, :] = jnp.zeros((wide.shape[0], PAD, LANES), F32)
    folds, slabs = z.folds(rows)
    for half in range(W // LANES):
        for copy in copies[2 * half : 2 * half + 2]:
            copy.wait()
        cols = slice(PAD + half * LANES, PAD + (half + 1) * LANES)
        for i, r in enumerate(rows):
            for t in range(mt):
                block = spec[half, pl.ds(t * LANES * R + r, LANES, stride=R), :]
                wide[i * mt + t, cols] = block.T
        for (count, used, deep, base, _), src, first in zip(folds, (spec, ocean), (z.main, 0)):
            for rr in range(deep):
                pieces = [
                    src[half, pl.ds(first * R + rows[rr + i * deep], count, stride=R), :]
                    for i in range(used)
                ]
                if used * count < LANES:
                    pieces.append(jnp.zeros((LANES - used * count, LANES), F32))
                wide[base + rr, cols] = jnp.concatenate(pieces, axis=0).T
    mask_copy.wait()
    sea = jnp.concatenate([mask[...].astype(F32), jnp.zeros((R, LANES), F32)], axis=1)
    for k, out in enumerate(outs):
        share = exchange_share(z, k, odd[0], part[0])
        start = pl.multiple_of(share * C, PAD)
        block = wide[:, pl.ds(start, E), :]
        out[0 : slabs * E] = block.reshape(slabs * E, LANES)
        if rows == z.edge_rows:
            shift = lax.rem(W + LANES + PAD - start, W + LANES)
            out[slabs * E : slabs * E + R] = pltpu.roll(sea, shift, axis=1)[:, :LANES]


def spread_line(line):
    return jnp.broadcast_to(line, (LANES, LANES)).T


def unpack_kernel(z, rows, odd, part, *refs):
    B, mt = z.B, z.mt
    got, outs = refs[:B], refs[B:]
    E = z.C + 2 * PAD
    if rows == z.edge_rows:
        sea = outs[-1]
        outs = outs[:-1]
        lines = got[0][z.slabs(rows) * E : z.slabs(rows) * E + z.R]
        for r in range(z.R):
            sea[r] = spread_line(lines[r : r + 1])[:E]
    places = listed(*outs)
    src = [exchange_part(z, k, odd[0], part[0]) for k in range(B)]
    for k in range(B):
        for t in range(mt):
            for i, (ref, at) in enumerate(places):
                ref[src[k] * mt + t, at] = got[k][(i * mt + t) * E : (i * mt + t + 1) * E]
    for count, used, deep, base, home in z.folds(rows)[0]:
        group = lane_group(count)
        for i, (ref, at) in enumerate(places):
            tile = jnp.zeros((E, LANES), F32)
            for k in range(B):
                shift = lax.rem((src[k] - i // deep) * count + LANES, LANES)
                slab = base + i % deep
                moved = pltpu.roll(got[k][slab * E : (slab + 1) * E], shift, axis=1)
                tile = jnp.where(group == src[k], moved, tile)
            ref[home, at] = tile
    if rows == z.edge_rows:
        for i, (ref, at) in enumerate(places):
            r = rows[i]
            ref[0, at, 0:1] = lines[r : r + 1]


def send_back_kernel(z, rows, odd, part, *refs):
    B, mt = z.B, z.mt
    states, outs = refs[:-B], refs[-B:]
    places = listed(*states)
    for k in range(B):
        src = exchange_part(z, k, odd[0], part[0])
        for t in range(mt):
            for i, (ref, at) in enumerate(places):
                outs[k][i * mt + t] = ref[src * mt + t, at]
        for count, used, deep, base, home in z.folds(rows)[0]:
            group = lane_group(count)
            for rr in range(deep):
                tile = jnp.zeros((z.C, LANES), F32)
                for i in range(used):
                    ref, at = places[rr + i * deep]
                    shift = lax.rem((i - src) * count + LANES, LANES)
                    moved = pltpu.roll(ref[home, at], shift, axis=1)
                    tile = jnp.where(group == i, moved, tile)
                outs[k][base + rr] = tile


def restore_kernel(z, odd, part, *refs):
    B, R, C, mt = z.B, z.R, z.C, z.mt
    got, (spec_out, ocean_out, wide, spec, ocean) = refs[: 2 * B], refs[2 * B :]
    at = 0
    for which, rows in enumerate((z.edge_rows, z.inner_rows)):
        folds, slabs = z.folds(rows)
        for k in range(B):
            c = exchange_share(z, k, odd[0], part[0])
            wide[at : at + slabs, pl.ds(pl.multiple_of(c * C, PAD), C), :] = got[which * B + k][...]
        for half in range(z.W // LANES):
            cols = slice(half * LANES, (half + 1) * LANES)
            for i, r in enumerate(rows):
                for t in range(mt):
                    place = pl.ds(t * LANES * R + r, LANES, stride=R)
                    spec[half, place, :] = wide[at + i * mt + t, cols].T
            for (count, used, deep, base, _), dst, first in zip(folds, (spec, ocean), (z.main, 0)):
                for rr in range(deep):
                    turned = wide[at + base + rr, cols].T
                    for i in range(used):
                        place = pl.ds(first * R + rows[rr + i * deep], count, stride=R)
                        dst[half, place, :] = turned[i * count : (i + 1) * count]
        at += slabs
    for half in range(z.W // LANES):
        cols = slice(half * LANES, (half + 1) * LANES)
        spec_out[:, cols] = spec[half]
        ocean_out[:, cols] = ocean[half]


def weights_kernel(z, linear, square, drift, weights, drift_weights):
    B, nb, main, nr, NB, L = z.B, z.nb, z.main, z.nr, z.NB, z.L

    def put(dst, first, lanes, turned):
        for s in range(B):
            dst[first + s * main : first + (s + 1) * main, lanes] = turned[
                s * nb : s * nb + main
            ]
            tail = first + B * main + s * nr
            dst[tail : tail + nr, lanes] = turned[s * nb + main : (s + 1) * nb]

    for n, source in enumerate((linear, square)):
        for s in range(B):
            for t in range(z.mt):
                block = source[s * nb + t * LANES : s * nb + (t + 1) * LANES, :]
                lane = s * main + t * LANES
                put(weights, n * NB, slice(lane, lane + LANES), block.T)
        tails = [source[s * nb + main : (s + 1) * nb, :] for s in range(B)]
        block = jnp.concatenate(tails, axis=0)
        put(weights, n * NB, slice(B * main, NB), block.T)

    row = lax.broadcasted_iota(jnp.int32, (LANES, LANES), 0)
    lane = lax.broadcasted_iota(jnp.int32, (LANES, LANES), 1)
    part, comp, level = lane // (2 * L), (lane // L) % 2, lane % L
    pick = jnp.where(row == 2 * (part * L + level) + 1 - comp, 1.0, 0.0).astype(BF16)
    turned = jnp.dot(drift[...].T, pick, preferred_element_type=F32).astype(BF16)
    put(drift_weights, 0, slice(0, LANES), turned)


def advance(
    z, sea_rows, rows, outs, cut, sea_at, speed, weights, drift_weights, moved, moved_twice,
    known=None, kept=None,
):
    NB, L, tiles = z.NB, z.L, z.NB // LANES
    known, kept = known or {}, kept or {}
    n = len(rows)
    first = [r for r in range(1, n - 1) if r not in known]
    assert first == list(range(first[0], first[-1] + 1))
    E = rows[0][0].shape[2]
    N = E - 2 * cut
    keep = slice(cut, cut + N)
    places = listed(*outs)
    T = E // SUBLANES
    offset = -cut % SUBLANES

    def apart(start):
        return [pl.ds(start + t, SUBLANES, stride=T) for t in range(T)]

    def sea_row(place):
        return place[0][place[1], pl.ds(sea_at, E)]

    def shift_up(parts):
        return [pltpu.roll(parts[-1], 1, axis=0)] + parts[:-1]

    def shift_down(parts):
        return parts[1:] + [pltpu.roll(parts[0], SUBLANES - 1, axis=0)]

    for r in range(min(first[0] - 1, 1), max(first[-1] + 2, n - 1)):
        ref, i = rows[r]
        surface = ref[tiles, i]
        moved[0, r] = DOPPLER * jnp.tanh(jnp.broadcast_to(surface[:, 0:1], (E, LANES)))
        moved[1, r] = DOPPLER * jnp.tanh(jnp.broadcast_to(surface[:, L : L + 1], (E, LANES)))

    def advect(read, write, start, stop, speed_cx, speed_cy):
        plus_before, waiting = None, None
        for r in range(start - 1, stop + 1):
            energy = read(r)
            speed_x = [speed_cx + moved[0, r, at, :] for at in apart(0)]
            if r >= start:
                minus = [jnp.minimum(v, 0.0) * e for v, e in zip(speed_x, energy)]
            if r > start:
                ref, i = sea_rows[r - 1]
                sea = [ref[i, at, :] for at in apart(sea_at)]
                write(r - 1, [(w - m) * s for w, m, s in zip(waiting, minus, sea)])
            if r < stop:
                plus = [jnp.maximum(v, 0.0) * e for v, e in zip(speed_x, energy)]
            if start <= r < stop:
                speed_y = [speed_cy + moved[1, r, at, :] for at in apart(0)]
                plus_y = [jnp.maximum(v, 0.0) * e for v, e in zip(speed_y, energy)]
                minus_y = [jnp.minimum(v, 0.0) * e for v, e in zip(speed_y, energy)]
                waiting = [
                    e - ((p - before) - m) - ((py - south) + (north - my))
                    for e, p, before, m, py, south, north, my in zip(
                        energy, plus, plus_before, minus,
                        plus_y, shift_up(plus_y), shift_down(minus_y), minus_y,
                    )
                ]
            plus_before = plus

    def one_tile(j, carry):
        lanes = pl.ds(pl.multiple_of(j * LANES, LANES), LANES)
        speed_cx = speed[0:1, lanes]
        speed_cy = speed[1:2, lanes]

        def in_order(t):
            return slice(t * SUBLANES, (t + 1) * SUBLANES)

        def read_first(r):
            ref, i = rows[r]
            return [ref[j, i, at, :] for at in apart(0)]

        def write_first(r, parts):
            for t, part in enumerate(parts):
                moved[2, r, in_order(t)] = part
                if r in kept:
                    ref, i = kept[r]
                    ref[j, i, in_order(t)] = part

        def read_second(r):
            if r in known:
                ref, i = known[r]
                return [ref[j, i, in_order(t)] for t in range(T)]
            return [moved[2, r, in_order(t)] for t in range(T)]

        def write_second(r, parts):
            for at, part in zip(apart(offset), parts):
                moved_twice[j, r - 2, at, :] = part

        advect(read_first, write_first, first[0], first[-1] + 1, speed_cx, speed_cy)
        advect(read_second, write_second, 2, n - 2, speed_cx, speed_cy)
        return carry

    lax.fori_loop(0, tiles, one_tile, 0)

    count = len(places)
    own_sea = sea_rows[2 : n - 2]
    own = slice(cut + offset, cut + offset + N)
    energy = jnp.concatenate(
        [moved_twice[j, :, own].reshape(count * N, LANES) for j in range(tiles)], axis=1
    )
    squares = energy * energy
    interaction = jnp.dot(
        energy.astype(BF16), weights[:NB], preferred_element_type=F32
    ) + jnp.dot(squares.astype(BF16), weights[NB:], preferred_element_type=F32)
    total = jnp.sum(squares, axis=1, keepdims=True)
    sea_here = jnp.concatenate([sea_row(place)[keep] for place in own_sea], axis=0)
    scale = (DT_SOURCE * sea_here[:, 0:1]) / (1.0 + total / NB)
    fresh = energy + scale * (interaction * energy)
    for i, (ref, at) in enumerate(places):
        for j in range(tiles):
            ref[j, at] = fresh[i * N : (i + 1) * N, j * LANES : (j + 1) * LANES]
    drift = jnp.dot(fresh.astype(BF16), drift_weights[...], preferred_element_type=F32)

    comp = (lax.broadcasted_iota(jnp.int32, (1, LANES), 1) // L) % 2
    sign = jnp.where(comp == 0, 1.0, -1.0).astype(F32)
    for i, (out, at) in enumerate(places):
        here, before, after = [
            ref[tiles, row] for ref, row in (rows[i + 2], rows[i + 1], rows[i + 3])
        ]
        lap = (
            (after + before)
            + (pltpu.roll(here, E - 1, axis=0) + pltpu.roll(here, 1, axis=0))
            - 4.0 * here
        )[keep]
        centre = here[keep]
        other = jnp.where(
            comp == 0, pltpu.roll(centre, LANES - L, axis=1), pltpu.roll(centre, L, axis=1)
        )
        turn = sign * (CORIOLIS * (other + drift[i * N : (i + 1) * N]))
        out[tiles, at] = (
            centre + DT_OCEAN * (turn + VISCOSITY * lap)
        ) * sea_row(own_sea[i])[keep]


def listed(*refs):
    return [(ref, i) for ref in refs for i in range(ref.shape[-3])]


def inner_kernel(z, first, cut, sea_at, top, inner, bottom, sea, speed, weights, drift_weights, *refs):
    out, for_edges, (moved, moved_twice) = refs[0], refs[1:-2], refs[-2:]
    kept = {}
    if for_edges:
        kept = {1 + i: (for_edges[0], i) for i in range(EDGE)}
        kept |= {z.R - 1 - EDGE + i: (for_edges[1], i) for i in range(EDGE)}
    advance(
        z, listed(sea), listed(top, inner, bottom), [out], cut, sea_at, speed, weights,
        drift_weights, moved, moved_twice, kept=kept,
    )


def read_sea(halo, sea):
    for i in range(EDGE):
        sea[i] = spread_line(halo[0, i, 0:1])[: halo.shape[2]]
    return sea


def top_kernel(z, first, cut, sea_at, up, top, inner, sea, *refs):
    inputs, outs = refs[:-4] if first else refs[:-3], refs[-4:] if first else refs[-3:]
    *given, speed, weights, drift_weights = inputs
    out, moved, moved_twice = outs[0], outs[-2], outs[-1]
    sea_up = read_sea(up, outs[1]) if first else given.pop(0)
    known = {3 + i: (given[0], i) for i in range(EDGE)} if given else {}
    rows = listed(up, top) + listed(inner)[:EDGE]
    sea_rows = (listed(sea_up) + listed(sea))[: len(rows)]
    advance(
        z, sea_rows, rows, [out], cut, sea_at, speed, weights, drift_weights, moved,
        moved_twice, known=known,
    )


def bottom_kernel(z, first, cut, sea_at, down, bottom, inner, sea, *refs):
    inputs, outs = refs[:-4] if first else refs[:-3], refs[-4:] if first else refs[-3:]
    *given, speed, weights, drift_weights = inputs
    out, moved, moved_twice = outs[0], outs[-2], outs[-1]
    sea_down = read_sea(down, outs[1]) if first else given.pop(0)
    known = {1 + i: (given[0], i) for i in range(EDGE)} if given else {}
    rows = listed(inner)[-EDGE:] + listed(bottom, down)
    sea_rows = (listed(sea) + listed(sea_down))[-len(rows) :]
    advance(
        z, sea_rows, rows, [out], cut, sea_at, speed, weights, drift_weights, moved,
        moved_twice, known=known,
    )


def speeds(z):
    lane = jnp.arange(z.NB, dtype=jnp.int32)
    head = (lane // z.main) * z.nb + lane % z.main
    rest = lane - z.B * z.main
    tail = (rest // z.nr) * z.nb + z.main + rest % z.nr
    bin_index = jnp.where(lane < z.B * z.main, head, tail)
    direction = (bin_index // NFREQ).astype(F32)
    frequency = (bin_index % NFREQ).astype(F32)
    group_speed = 0.4 / (1.0 + frequency / 16.0)
    bin_angle = (2.0 * jnp.pi / NDIR) * direction
    zeros = jnp.zeros_like(bin_angle)
    rows = [group_speed * jnp.cos(bin_angle), group_speed * jnp.sin(bin_angle)] + [zeros] * 6
    return jnp.stack(rows)


def cost(flops, moved):
    return pl.CostEstimate(flops=int(flops), bytes_accessed=int(moved), transcendentals=0)


def per_device(G, B, spectrum, sea_mask, kernel_linear, kernel_square, drift_kernel, ocean):
    nb, R, W = spectrum.shape
    L = ocean.shape[1]
    z = Sizes(B, nb, L, R, W)
    C, NB, CH = z.C, z.NB, z.CH
    half = B // 2
    axes = ("geo", "bins")
    geo, part = lax.axis_index("geo"), lax.axis_index("bins")

    def device_at(q, c):
        return ((q // 2) * 2 + c // half) * B + 2 * (c % half) + q % 2

    forward = [
        [
            (g * B + b, device_at(g, exchange_share(z, k, g % 2, b)))
            for g in range(G)
            for b in range(B)
        ]
        for k in range(B)
    ]
    pairs = [(q, c) for q in range(G) for c in range(B)]
    to_next_row = [(device_at(q, c), device_at((q + 1) % G, c)) for q, c in pairs]
    to_prev_row = [(t, s) for s, t in to_next_row]
    who = ((geo % 2).astype(jnp.int32).reshape(1), part.astype(jnp.int32).reshape(1))

    width = C + 2 * PAD
    all_slabs = z.slabs(z.edge_rows) + z.slabs(z.inner_rows)
    columns_scratch = [
        pltpu.VMEM((W // LANES, nb * R, LANES), F32),
        pltpu.VMEM((W // LANES, 2 * L * R, LANES), F32),
    ]
    def pack(rows):
        slabs = z.slabs(rows)
        lines = slabs * width + (R if rows == z.edge_rows else 0)
        return pl.pallas_call(
            functools.partial(pack_kernel, z, rows),
            out_shape=[jax.ShapeDtypeStruct((lines, LANES), F32)] * B,
            in_specs=[SMEM] * 2 + [HBM] * 3,
            out_specs=[VMEM] * B,
            scratch_shapes=columns_scratch
            + [
                pltpu.VMEM((R, W), jnp.int32),
                pltpu.VMEM((slabs, W + 2 * PAD, LANES), F32),
                pltpu.SemaphoreType.DMA((3, W // LANES)),
            ],
            compiler_params=params(58),
            name="pack",
        )(*who, spectrum.reshape(nb * R, W), ocean.reshape(2 * L * R, W), sea_mask)

    packed = pack(z.edge_rows)
    got = [lax.ppermute(packed[k], axes, forward[k]) for k in range(B)]
    packed = pack(z.inner_rows)

    weights, drift_weights = pl.pallas_call(
        functools.partial(weights_kernel, z),
        out_shape=(
            jax.ShapeDtypeStruct((2 * NB, NB), BF16),
            jax.ShapeDtypeStruct((NB, LANES), BF16),
        ),
        in_specs=[VMEM] * 3,
        out_specs=(VMEM,) * 2,
        compiler_params=params(24),
        cost_estimate=cost(2e9, 4 * NB * NB * 2),
        name="weights",
    )(kernel_linear, kernel_square, drift_kernel)
    speed = speeds(z)
    *got, weights, drift_weights, speed = lax.optimization_barrier(
        (*got, weights, drift_weights, speed)
    )

    def state(rows, columns):
        return (CH // LANES, rows, columns, LANES)

    def unpack(rows, received, shapes):
        return pl.pallas_call(
            functools.partial(unpack_kernel, z, rows),
            out_shape=[jax.ShapeDtypeStruct(shape, F32) for shape in shapes],
            in_specs=[SMEM] * 2 + [VMEM] * B,
            out_specs=[VMEM] * len(shapes),
            compiler_params=params(16),
            name="unpack",
        )(*who, *received)

    top, bottom, sea = unpack(
        z.edge_rows, got[:B], [state(EDGE, width), state(EDGE, width), (R, width, LANES)]
    )
    *blocks, top = lax.optimization_barrier((*packed[half:], top))
    blocks = list(packed[:half]) + blocks
    got = [lax.ppermute(blocks[k], axes, forward[k]) for k in range(B)]
    (inner,) = unpack(z.inner_rows, got, [state(R - 2 * EDGE, width)])

    def step_call(body, first, cut, sea_at, count, deepest, inputs, more=()):
        width = inputs[0].shape[2]
        n = width - 2 * cut
        shapes = [state(count, n)] + [before + (EDGE, width, LANES) for before in more]
        return pl.pallas_call(
            functools.partial(body, z, first, cut, sea_at),
            out_shape=[jax.ShapeDtypeStruct(shape, F32) for shape in shapes],
            in_specs=[VMEM] * (len(inputs) + 3),
            out_specs=[VMEM] * len(shapes),
            scratch_shapes=[
                pltpu.VMEM((3, deepest, width, LANES), F32),
                pltpu.VMEM((NB // LANES, count, width + PAD, LANES), F32),
            ],
            compiler_params=params(24),
            cost_estimate=cost(count * 1e8, count * 1e5),
            name=body.__name__,
        )(*inputs, speed, weights, drift_weights)

    sea_up, sea_down = [], []
    for step in range(STEPS):
        valid = EDGE * (STEPS - 1 - step)
        margin = (width - C) // 2
        cut = margin - valid if valid == 0 or (margin - valid) % 4 == 0 else 0
        sea_at = PAD - margin
        down = lax.ppermute(top, axes, to_prev_row)
        up = lax.ppermute(bottom, axes, to_next_row)
        first = step == 0

        def advance_inner():
            return step_call(
                inner_kernel, first, cut, sea_at, R - 2 * EDGE, R, (top, inner, bottom, sea),
                () if first else ((NB // LANES,),) * 2,
            )

        given = ()
        if not first:
            new_inner, *given = advance_inner()
        new_bottom, *found = step_call(
            bottom_kernel, first, cut, sea_at, EDGE, 3 * EDGE,
            (down, bottom, inner, sea, *sea_down, *given[1:]),
            ((),) if first else (),
        )
        sea_down = sea_down or found
        new_top, *found = step_call(
            top_kernel, first, cut, sea_at, EDGE, 3 * EDGE,
            (up, top, inner, sea, *sea_up, *given[:1]),
            ((),) if first else (),
        )
        sea_up = sea_up or found
        if first:
            inner, new_top = lax.optimization_barrier((inner, new_top))
            (new_inner,) = advance_inner()
        top, inner, bottom = new_top, new_inner, new_bottom
        width -= 2 * cut

    def send_back(rows, states):
        shape = jax.ShapeDtypeStruct((z.slabs(rows), C, LANES), F32)
        return pl.pallas_call(
            functools.partial(send_back_kernel, z, rows),
            out_shape=[shape] * B,
            in_specs=[SMEM] * 2 + [VMEM] * len(states),
            out_specs=[VMEM] * B,
            compiler_params=params(16),
            name="send_back",
        )(*who, *states)

    packed = send_back(z.inner_rows, [inner]), send_back(z.edge_rows, [top, bottom])
    packed = list(packed[1]) + list(packed[0])
    back = [
        lax.ppermute(packed[i], axes, [(t, s) for s, t in forward[i % B]]) for i in range(2 * B)
    ]
    spectrum_out, ocean_out = pl.pallas_call(
        functools.partial(restore_kernel, z),
        out_shape=(
            jax.ShapeDtypeStruct((nb * R, W), F32),
            jax.ShapeDtypeStruct((2 * L * R, W), F32),
        ),
        in_specs=[SMEM] * 2 + [VMEM] * (2 * B),
        out_specs=(VMEM,) * 2,
        scratch_shapes=[pltpu.VMEM((all_slabs, W, LANES), F32)] + columns_scratch,
        compiler_params=params(24),
        name="restore",
    )(*who, *back)
    return spectrum_out.reshape(nb, R, W), ocean_out.reshape(2, L, R, W)


def solution(mesh):
    return jax.shard_map(
        functools.partial(per_device, mesh.shape["geo"], mesh.shape["bins"]),
        mesh=mesh,
        in_specs=(
            P("bins", "geo", None),
            P("geo", None),
            P(),
            P(),
            P(),
            P(None, "bins", "geo", None),
        ),
        out_specs=(P("bins", "geo", None), P(None, "bins", "geo", None)),
        check_vma=False,
    )
```

```python
import functools

import jax
import jax.numpy as jnp
from jax import lax
from jax.experimental import pallas as pl
from jax.experimental.pallas import tpu as pltpu
from jax.sharding import PartitionSpec as P

NDIR = 36
NFREQ = 32
STEPS = 3
SUB = 2
DT_SOURCE = 0.5
DT_OCEAN = 0.2
CORIOLIS = 1.0
VISCOSITY = 1.0
DOPPLER = 0.1

LANES = 128
SUBLANES = 8
PAD = 8
HALO = SUB * STEPS
EDGE = 2
VMEM = pl.BlockSpec(memory_space=pltpu.VMEM)
SMEM = pl.BlockSpec(memory_space=pltpu.SMEM)
HBM = pl.BlockSpec(memory_space=pltpu.HBM)
F32 = jnp.float32
BF16 = jnp.bfloat16


def params(mib):
    return pltpu.CompilerParams(vmem_limit_bytes=mib * 1024 * 1024)


class Sizes:
    def __init__(self, parts, bins_here, levels_here, rows, width):
        self.B, self.nb, self.L, self.R, self.W = parts, bins_here, levels_here, rows, width
        self.C = width // parts
        self.mt = bins_here // LANES
        self.main = self.mt * LANES
        self.nr = bins_here - self.main
        self.no = 2 * levels_here
        self.NB = parts * bins_here
        self.CH = self.NB + LANES
        self.edge_rows = (0, 1, rows - 2, rows - 1)
        self.inner_rows = tuple(range(2, rows - 2))
        self.half = parts // 2
        assert self.half & (self.half - 1) == 0 and self.half > 1
        assert self.nr * parts == LANES and self.no * parts == LANES

    def folds(self, rows):
        out, base = [], len(rows) * self.mt
        for count, tile in ((self.nr, self.B * self.mt), (self.no, self.NB // LANES)):
            used = min(LANES // count, len(rows))
            deep = len(rows) // used
            assert deep * used == len(rows)
            out.append((count, used, deep, base, tile))
            base += deep
        return out, base

    def slabs(self, rows):
        return self.folds(rows)[1]


def exchange_share(z, k, odd, part):
    core = part % 2
    flip, delta = (k // z.half) ^ core, (k % z.half) ^ core
    return (odd ^ flip) * z.half + ((part // 2) ^ delta)


def exchange_part(z, k, odd, part):
    core = (k // z.half) ^ odd ^ (part % 2)
    delta = (k % z.half) ^ core
    return ((part // 2) ^ delta) * 2 + core


def lane_group(width):
    return lax.broadcasted_iota(jnp.int32, (1, LANES), 1) // width


def pack_kernel(z, rows, odd, part, spec_in, ocean_in, mask_in, *refs):
    B, R, C, W, mt = z.B, z.R, z.C, z.W, z.mt
    outs, (spec, ocean, mask, wide, sems) = refs[:B], refs[B:]
    E, H = C + 2 * PAD, C + 2 * HALO
    copies = []
    for half in range(W // LANES):
        cols = pl.ds(half * LANES, LANES)
        for n, (src, dst) in enumerate(((spec_in, spec), (ocean_in, ocean))):
            copies.append(pltpu.make_async_copy(src.at[:, cols], dst.at[half], sems.at[n, half]))
            copies[-1].start()
    mask_copy = pltpu.make_async_copy(mask_in, mask, sems.at[2, 0])
    mask_copy.start()
    wide[:, 0:PAD, :] = jnp.zeros((wide.shape[0], PAD, LANES), F32)
    wide[:, PAD + W : W + 2 * PAD, :] = jnp.zeros((wide.shape[0], PAD, LANES), F32)
    folds, slabs = z.folds(rows)
    for half in range(W // LANES):
        for copy in copies[2 * half : 2 * half + 2]:
            copy.wait()
        cols = slice(PAD + half * LANES, PAD + (half + 1) * LANES)
        for i, r in enumerate(rows):
            for t in range(mt):
                block = spec[half, pl.ds(t * LANES * R + r, LANES, stride=R), :]
                wide[i * mt + t, cols] = block.T
        for (count, used, deep, base, _), src, first in zip(folds, (spec, ocean), (z.main, 0)):
            for rr in range(deep):
                pieces = [
                    src[half, pl.ds(first * R + rows[rr + i * deep], count, stride=R), :]
                    for i in range(used)
                ]
                if used * count < LANES:
                    pieces.append(jnp.zeros((LANES - used * count, LANES), F32))
                wide[base + rr, cols] = jnp.concatenate(pieces, axis=0).T
    mask_copy.wait()
    sea = jnp.concatenate([mask[...].astype(F32), jnp.zeros((R, LANES), F32)], axis=1)
    for k, out in enumerate(outs):
        share = exchange_share(z, k, odd[0], part[0])
        start = pl.multiple_of(share * C, PAD)
        for i in range(slabs):
            block = wide[i, pl.ds(start, E), :]
            out[i * H : (i + 1) * H] = block[PAD - HALO : PAD - HALO + H]
        if rows == z.edge_rows:
            shift = lax.rem(W + LANES + PAD - start, W + LANES)
            out[slabs * H : slabs * H + R] = pltpu.roll(sea, shift, axis=1)[:, :LANES]


def spread_line(line):
    return jnp.broadcast_to(line, (LANES, LANES)).T


def unpack_kernel(z, rows, odd, part, *refs):
    B, mt = z.B, z.mt
    got, outs = refs[:B], refs[B:]
    E, H = z.C + 2 * PAD, z.C + 2 * HALO
    brought = slice(PAD - HALO, PAD - HALO + H)
    if rows == z.edge_rows:
        sea = outs[-1]
        outs = outs[:-1]
        lines = got[0][z.slabs(rows) * H : z.slabs(rows) * H + z.R]
        for r in range(z.R):
            sea[r] = spread_line(lines[r : r + 1])[:E]
    places = listed(*outs)
    for ref in outs:
        for columns in (slice(0, PAD), slice(E - PAD, E)):
            ref[:, :, columns] = jnp.zeros(ref.shape[:2] + (PAD, LANES), F32)
    src = [exchange_part(z, k, odd[0], part[0]) for k in range(B)]
    for k in range(B):
        for t in range(mt):
            for i, (ref, at) in enumerate(places):
                slab = i * mt + t
                ref[src[k] * mt + t, at, brought] = got[k][slab * H : (slab + 1) * H]
    for count, used, deep, base, home in z.folds(rows)[0]:
        group = lane_group(count)
        for i, (ref, at) in enumerate(places):
            tile = jnp.zeros((H, LANES), F32)
            for k in range(B):
                shift = lax.rem((src[k] - i // deep) * count + LANES, LANES)
                slab = base + i % deep
                moved = pltpu.roll(got[k][slab * H : (slab + 1) * H], shift, axis=1)
                tile = jnp.where(group == src[k], moved, tile)
            ref[home, at, brought] = tile
    if rows == z.edge_rows:
        for i, (ref, at) in enumerate(places):
            r = rows[i]
            ref[0, at, 0:1] = lines[r : r + 1]


def send_back_kernel(z, rows, odd, part, *refs):
    B, mt = z.B, z.mt
    states, outs = refs[:-B], refs[-B:]
    places = listed(*states)
    for k in range(B):
        src = exchange_part(z, k, odd[0], part[0])
        for t in range(mt):
            for i, (ref, at) in enumerate(places):
                outs[k][i * mt + t] = ref[src * mt + t, at]
        for count, used, deep, base, home in z.folds(rows)[0]:
            group = lane_group(count)
            for rr in range(deep):
                tile = jnp.zeros((z.C, LANES), F32)
                for i in range(used):
                    ref, at = places[rr + i * deep]
                    shift = lax.rem((i - src) * count + LANES, LANES)
                    moved = pltpu.roll(ref[home, at], shift, axis=1)
                    tile = jnp.where(group == i, moved, tile)
                outs[k][base + rr] = tile


def restore_rows(z, rows, odd, part, got, wide, spec, ocean):
    R, C, mt = z.R, z.C, z.mt
    folds, slabs = z.folds(rows)
    for k, block in enumerate(got):
        share = exchange_share(z, k, odd[0], part[0])
        wide[:, pl.ds(pl.multiple_of(share * C, PAD), C), :] = block[...]
    for half in range(z.W // LANES):
        cols = slice(half * LANES, (half + 1) * LANES)
        for i, r in enumerate(rows):
            for t in range(mt):
                place = pl.ds(t * LANES * R + r, LANES, stride=R)
                spec[half, place, :] = wide[i * mt + t, cols].T
        for (count, used, deep, base, _), dst, first in zip(folds, (spec, ocean), (z.main, 0)):
            for rr in range(deep):
                turned = wide[base + rr, cols].T
                for i in range(used):
                    place = pl.ds(first * R + rows[rr + i * deep], count, stride=R)
                    dst[half, place, :] = turned[i * count : (i + 1) * count]
        yield half


def restore_inner_kernel(z, odd, part, *refs):
    got, (spec, ocean, wide) = refs[: z.B], refs[z.B :]
    for _ in restore_rows(z, z.inner_rows, odd, part, got, wide, spec, ocean):
        pass


def restore_kernel(z, odd, part, *refs):
    got, (_, _, spec_out, ocean_out, spec, ocean, wide, sems) = refs[: z.B], refs[z.B :]
    copies = []
    for half in restore_rows(z, z.edge_rows, odd, part, got, wide, spec, ocean):
        cols = pl.ds(half * LANES, LANES)
        for n, (src, dst) in enumerate(((spec, spec_out), (ocean, ocean_out))):
            copies.append(pltpu.make_async_copy(src.at[half], dst.at[:, cols], sems.at[n, half]))
            copies[-1].start()
    for copy in copies:
        copy.wait()


def weights_kernel(z, linear, square, drift, weights, drift_weights):
    B, nb, main, nr, NB, L = z.B, z.nb, z.main, z.nr, z.NB, z.L

    def put(dst, first, lanes, turned):
        for s in range(B):
            dst[first + s * main : first + (s + 1) * main, lanes] = turned[
                s * nb : s * nb + main
            ]
            tail = first + B * main + s * nr
            dst[tail : tail + nr, lanes] = turned[s * nb + main : (s + 1) * nb]

    for n, source in enumerate((linear, square)):
        for s in range(B):
            for t in range(z.mt):
                block = source[s * nb + t * LANES : s * nb + (t + 1) * LANES, :]
                lane = s * main + t * LANES
                put(weights, n * NB, slice(lane, lane + LANES), block.T)
        tails = [source[s * nb + main : (s + 1) * nb, :] for s in range(B)]
        block = jnp.concatenate(tails, axis=0)
        put(weights, n * NB, slice(B * main, NB), block.T)

    row = lax.broadcasted_iota(jnp.int32, (LANES, LANES), 0)
    lane = lax.broadcasted_iota(jnp.int32, (LANES, LANES), 1)
    part, comp, level = lane // (2 * L), (lane // L) % 2, lane % L
    pick = jnp.where(row == 2 * (part * L + level) + 1 - comp, 1.0, 0.0).astype(BF16)
    turned = jnp.dot(drift[...].T, pick, preferred_element_type=F32).astype(BF16)
    put(drift_weights, 0, slice(0, LANES), turned)


def advance(
    z, sea_rows, rows, outs, cut, sea_at, speed, weights, drift_weights, moved, moved_twice,
    known=None, kept=None,
):
    NB, L, tiles = z.NB, z.L, z.NB // LANES
    known, kept = known or {}, kept or {}
    n = len(rows)
    first = [r for r in range(1, n - 1) if r not in known]
    assert first == list(range(first[0], first[-1] + 1))
    E = rows[0][0].shape[2]
    N = E - 2 * cut
    keep = slice(cut, cut + N)
    places = listed(*outs)
    T = E // SUBLANES
    offset = -cut % SUBLANES

    def apart(start):
        return [pl.ds(start + t, SUBLANES, stride=T) for t in range(T)]

    def sea_row(place):
        return place[0][place[1], pl.ds(sea_at, E)]

    def shift_up(parts):
        return [pltpu.roll(parts[-1], 1, axis=0)] + parts[:-1]

    def shift_down(parts):
        return parts[1:] + [pltpu.roll(parts[0], SUBLANES - 1, axis=0)]

    for r in range(min(first[0] - 1, 1), max(first[-1] + 2, n - 1)):
        ref, i = rows[r]
        surface = ref[tiles, i]
        moved[0, r] = DOPPLER * jnp.tanh(jnp.broadcast_to(surface[:, 0:1], (E, LANES)))
        moved[1, r] = DOPPLER * jnp.tanh(jnp.broadcast_to(surface[:, L : L + 1], (E, LANES)))

    def advect(read, write, start, stop, speed_cx, speed_cy):
        plus_before, waiting = None, None
        for r in range(start - 1, stop + 1):
            energy = read(r)
            speed_x = [speed_cx + moved[0, r, at, :] for at in apart(0)]
            if r >= start:
                minus = [jnp.minimum(v, 0.0) * e for v, e in zip(speed_x, energy)]
            if r > start:
                ref, i = sea_rows[r - 1]
                sea = [ref[i, at, :] for at in apart(sea_at)]
                write(r - 1, [(w - m) * s for w, m, s in zip(waiting, minus, sea)])
            if r < stop:
                plus = [jnp.maximum(v, 0.0) * e for v, e in zip(speed_x, energy)]
            if start <= r < stop:
                speed_y = [speed_cy + moved[1, r, at, :] for at in apart(0)]
                plus_y = [jnp.maximum(v, 0.0) * e for v, e in zip(speed_y, energy)]
                minus_y = [jnp.minimum(v, 0.0) * e for v, e in zip(speed_y, energy)]
                waiting = [
                    e - ((p - before) - m) - ((py - south) + (north - my))
                    for e, p, before, m, py, south, north, my in zip(
                        energy, plus, plus_before, minus,
                        plus_y, shift_up(plus_y), shift_down(minus_y), minus_y,
                    )
                ]
            plus_before = plus

    def one_tile(j, carry):
        lanes = pl.ds(pl.multiple_of(j * LANES, LANES), LANES)
        speed_cx = speed[0:1, lanes]
        speed_cy = speed[1:2, lanes]

        def in_order(t):
            return slice(t * SUBLANES, (t + 1) * SUBLANES)

        def read_first(r):
            ref, i = rows[r]
            return [ref[j, i, at, :] for at in apart(0)]

        def write_first(r, parts):
            for t, part in enumerate(parts):
                moved[2, r, in_order(t)] = part
                if r in kept:
                    ref, i = kept[r]
                    ref[j, i, in_order(t)] = part

        def read_second(r):
            if r in known:
                ref, i = known[r]
                return [ref[j, i, in_order(t)] for t in range(T)]
            return [moved[2, r, in_order(t)] for t in range(T)]

        def write_second(r, parts):
            for at, part in zip(apart(offset), parts):
                moved_twice[j, r - 2, at, :] = part

        advect(read_first, write_first, first[0], first[-1] + 1, speed_cx, speed_cy)
        advect(read_second, write_second, 2, n - 2, speed_cx, speed_cy)
        return carry

    lax.fori_loop(0, tiles, one_tile, 0)

    count = len(places)
    own_sea = sea_rows[2 : n - 2]
    own = slice(cut + offset, cut + offset + N)
    energy = jnp.concatenate(
        [moved_twice[j, :, own].reshape(count * N, LANES) for j in range(tiles)], axis=1
    )
    squares = energy * energy
    interaction = jnp.dot(
        energy.astype(BF16), weights[:NB], preferred_element_type=F32
    ) + jnp.dot(squares.astype(BF16), weights[NB:], preferred_element_type=F32)
    total = jnp.sum(squares, axis=1, keepdims=True)
    sea_here = jnp.concatenate([sea_row(place)[keep] for place in own_sea], axis=0)
    scale = (DT_SOURCE * sea_here[:, 0:1]) / (1.0 + total / NB)
    fresh = energy + scale * (interaction * energy)
    for i, (ref, at) in enumerate(places):
        for j in range(tiles):
            ref[j, at] = fresh[i * N : (i + 1) * N, j * LANES : (j + 1) * LANES]
    drift = jnp.dot(fresh.astype(BF16), drift_weights[...], preferred_element_type=F32)

    comp = (lax.broadcasted_iota(jnp.int32, (1, LANES), 1) // L) % 2
    sign = jnp.where(comp == 0, 1.0, -1.0).astype(F32)
    for i, (out, at) in enumerate(places):
        here, before, after = [
            ref[tiles, row] for ref, row in (rows[i + 2], rows[i + 1], rows[i + 3])
        ]
        lap = (
            (after + before)
            + (pltpu.roll(here, E - 1, axis=0) + pltpu.roll(here, 1, axis=0))
            - 4.0 * here
        )[keep]
        centre = here[keep]
        other = jnp.where(
            comp == 0, pltpu.roll(centre, LANES - L, axis=1), pltpu.roll(centre, L, axis=1)
        )
        turn = sign * (CORIOLIS * (other + drift[i * N : (i + 1) * N]))
        out[tiles, at] = (
            centre + DT_OCEAN * (turn + VISCOSITY * lap)
        ) * sea_row(own_sea[i])[keep]


def listed(*refs):
    return [(ref, i) for ref in refs for i in range(ref.shape[-3])]


def inner_kernel(z, first, cut, sea_at, top, inner, bottom, sea, speed, weights, drift_weights, *refs):
    out, for_edges, (moved, moved_twice) = refs[0], refs[1:-2], refs[-2:]
    kept = {}
    if for_edges:
        kept = {1 + i: (for_edges[0], i) for i in range(EDGE)}
        kept |= {z.R - 1 - EDGE + i: (for_edges[1], i) for i in range(EDGE)}
    advance(
        z, listed(sea), listed(top, inner, bottom), [out], cut, sea_at, speed, weights,
        drift_weights, moved, moved_twice, kept=kept,
    )


def read_sea(halo, sea):
    for i in range(EDGE):
        sea[i] = spread_line(halo[0, i, 0:1])[: halo.shape[2]]
    return sea


def top_kernel(z, first, cut, sea_at, up, top, inner, sea, *refs):
    inputs, outs = refs[:-4] if first else refs[:-3], refs[-4:] if first else refs[-3:]
    *given, speed, weights, drift_weights = inputs
    out, moved, moved_twice = outs[0], outs[-2], outs[-1]
    sea_up = read_sea(up, outs[1]) if first else given.pop(0)
    known = {3 + i: (given[0], i) for i in range(EDGE)} if given else {}
    rows = listed(up, top) + listed(inner)[:EDGE]
    sea_rows = (listed(sea_up) + listed(sea))[: len(rows)]
    advance(
        z, sea_rows, rows, [out], cut, sea_at, speed, weights, drift_weights, moved,
        moved_twice, known=known,
    )


def bottom_kernel(z, first, cut, sea_at, down, bottom, inner, sea, *refs):
    inputs, outs = refs[:-4] if first else refs[:-3], refs[-4:] if first else refs[-3:]
    *given, speed, weights, drift_weights = inputs
    out, moved, moved_twice = outs[0], outs[-2], outs[-1]
    sea_down = read_sea(down, outs[1]) if first else given.pop(0)
    known = {1 + i: (given[0], i) for i in range(EDGE)} if given else {}
    rows = listed(inner)[-EDGE:] + listed(bottom, down)
    sea_rows = (listed(sea) + listed(sea_down))[-len(rows) :]
    advance(
        z, sea_rows, rows, [out], cut, sea_at, speed, weights, drift_weights, moved,
        moved_twice, known=known,
    )


def speeds(z):
    lane = jnp.arange(z.NB, dtype=jnp.int32)
    head = (lane // z.main) * z.nb + lane % z.main
    rest = lane - z.B * z.main
    tail = (rest // z.nr) * z.nb + z.main + rest % z.nr
    bin_index = jnp.where(lane < z.B * z.main, head, tail)
    direction = (bin_index // NFREQ).astype(F32)
    frequency = (bin_index % NFREQ).astype(F32)
    group_speed = 0.4 / (1.0 + frequency / 16.0)
    bin_angle = (2.0 * jnp.pi / NDIR) * direction
    zeros = jnp.zeros_like(bin_angle)
    rows = [group_speed * jnp.cos(bin_angle), group_speed * jnp.sin(bin_angle)] + [zeros] * 6
    return jnp.stack(rows)


def cost(flops, moved):
    return pl.CostEstimate(flops=int(flops), bytes_accessed=int(moved), transcendentals=0)


def per_device(G, B, spectrum, sea_mask, kernel_linear, kernel_square, drift_kernel, ocean):
    nb, R, W = spectrum.shape
    L = ocean.shape[1]
    z = Sizes(B, nb, L, R, W)
    C, NB, CH = z.C, z.NB, z.CH
    half = B // 2
    axes = ("geo", "bins")
    geo, part = lax.axis_index("geo"), lax.axis_index("bins")

    def device_at(q, c):
        return ((q // 2) * 2 + c // half) * B + 2 * (c % half) + q % 2

    forward = [
        [
            (g * B + b, device_at(g, exchange_share(z, k, g % 2, b)))
            for g in range(G)
            for b in range(B)
        ]
        for k in range(B)
    ]
    pairs = [(q, c) for q in range(G) for c in range(B)]
    to_next_row = [(device_at(q, c), device_at((q + 1) % G, c)) for q, c in pairs]
    to_prev_row = [(t, s) for s, t in to_next_row]
    who = ((geo % 2).astype(jnp.int32).reshape(1), part.astype(jnp.int32).reshape(1))

    width = C + 2 * PAD
    columns_scratch = [
        pltpu.VMEM((W // LANES, nb * R, LANES), F32),
        pltpu.VMEM((W // LANES, 2 * L * R, LANES), F32),
    ]
    def pack(rows):
        slabs = z.slabs(rows)
        lines = slabs * (C + 2 * HALO) + (R if rows == z.edge_rows else 0)
        return pl.pallas_call(
            functools.partial(pack_kernel, z, rows),
            out_shape=[jax.ShapeDtypeStruct((lines, LANES), F32)] * B,
            in_specs=[SMEM] * 2 + [HBM] * 3,
            out_specs=[VMEM] * B,
            scratch_shapes=columns_scratch
            + [
                pltpu.VMEM((R, W), jnp.int32),
                pltpu.VMEM((slabs, W + 2 * PAD, LANES), F32),
                pltpu.SemaphoreType.DMA((3, W // LANES)),
            ],
            compiler_params=params(58),
            name="pack",
        )(*who, spectrum.reshape(nb * R, W), ocean.reshape(2 * L * R, W), sea_mask)

    packed = pack(z.edge_rows)
    got = [lax.ppermute(packed[k], axes, forward[k]) for k in range(B)]
    packed = pack(z.inner_rows)

    weights, drift_weights = pl.pallas_call(
        functools.partial(weights_kernel, z),
        out_shape=(
            jax.ShapeDtypeStruct((2 * NB, NB), BF16),
            jax.ShapeDtypeStruct((NB, LANES), BF16),
        ),
        in_specs=[VMEM] * 3,
        out_specs=(VMEM,) * 2,
        compiler_params=params(24),
        cost_estimate=cost(2e9, 4 * NB * NB * 2),
        name="weights",
    )(kernel_linear, kernel_square, drift_kernel)
    speed = speeds(z)
    held_back = packed[half:]
    got, weights, drift_weights, speed, held_back = lax.optimization_barrier(
        (got, weights, drift_weights, speed, held_back)
    )

    def state(rows, columns):
        return (CH // LANES, rows, columns, LANES)

    def unpack(rows, received, shapes):
        return pl.pallas_call(
            functools.partial(unpack_kernel, z, rows),
            out_shape=[jax.ShapeDtypeStruct(shape, F32) for shape in shapes],
            in_specs=[SMEM] * 2 + [VMEM] * B,
            out_specs=[VMEM] * len(shapes),
            compiler_params=params(16),
            name="unpack",
        )(*who, *received)

    top, bottom, sea = unpack(
        z.edge_rows, got[:B], [state(EDGE, width), state(EDGE, width), (R, width, LANES)]
    )
    got = [lax.ppermute(packed[k], axes, forward[k]) for k in range(half)]
    held_back, got[0], _ = lax.optimization_barrier((held_back, got[0], top))
    got += [lax.ppermute(held_back[k], axes, forward[half + k]) for k in range(B - half)]
    (inner,) = unpack(z.inner_rows, got, [state(R - 2 * EDGE, width)])

    def step_call(body, first, cut, sea_at, count, deepest, inputs, more=()):
        width = inputs[0].shape[2]
        n = width - 2 * cut
        shapes = [state(count, n)] + [before + (EDGE, width, LANES) for before in more]
        return pl.pallas_call(
            functools.partial(body, z, first, cut, sea_at),
            out_shape=[jax.ShapeDtypeStruct(shape, F32) for shape in shapes],
            in_specs=[VMEM] * (len(inputs) + 3),
            out_specs=[VMEM] * len(shapes),
            scratch_shapes=[
                pltpu.VMEM((3, deepest, width, LANES), F32),
                pltpu.VMEM((NB // LANES, count, width + PAD, LANES), F32),
            ],
            compiler_params=params(24),
            cost_estimate=cost(count * 1e8, count * 1e5),
            name=body.__name__,
        )(*inputs, speed, weights, drift_weights)

    sea_up, sea_down = [], []
    for step in range(STEPS):
        valid = EDGE * (STEPS - 1 - step)
        margin = (width - C) // 2
        cut = margin - valid if valid == 0 or (margin - valid) % 4 == 0 else 0
        sea_at = PAD - margin
        down = lax.ppermute(top, axes, to_prev_row)
        up = lax.ppermute(bottom, axes, to_next_row)
        first = step == 0

        def advance_inner():
            return step_call(
                inner_kernel, first, cut, sea_at, R - 2 * EDGE, R, (top, inner, bottom, sea),
                () if first else ((NB // LANES,),) * 2,
            )

        given = ()
        if not first:
            new_inner, *given = advance_inner()
        new_bottom, *found = step_call(
            bottom_kernel, first, cut, sea_at, EDGE, 3 * EDGE,
            (down, bottom, inner, sea, *sea_down, *given[1:]),
            ((),) if first else (),
        )
        sea_down = sea_down or found
        new_top, *found = step_call(
            top_kernel, first, cut, sea_at, EDGE, 3 * EDGE,
            (up, top, inner, sea, *sea_up, *given[:1]),
            ((),) if first else (),
        )
        sea_up = sea_up or found
        if first:
            inner, new_top = lax.optimization_barrier((inner, new_top))
            (new_inner,) = advance_inner()
        top, inner, bottom = new_top, new_inner, new_bottom
        width -= 2 * cut

    def send_back(rows, states):
        shape = jax.ShapeDtypeStruct((z.slabs(rows), C, LANES), F32)
        return pl.pallas_call(
            functools.partial(send_back_kernel, z, rows),
            out_shape=[shape] * B,
            in_specs=[SMEM] * 2 + [VMEM] * len(states),
            out_specs=[VMEM] * B,
            compiler_params=params(16),
            name="send_back",
        )(*who, *states)

    packed = send_back(z.inner_rows, [inner]), send_back(z.edge_rows, [top, bottom])
    packed = list(packed[1]) + list(packed[0])
    back = [
        lax.ppermute(packed[i], axes, [(t, s) for s, t in forward[i % B]]) for i in range(2 * B)
    ]
    halves = [
        jax.ShapeDtypeStruct((W // LANES, nb * R, LANES), F32),
        jax.ShapeDtypeStruct((W // LANES, 2 * L * R, LANES), F32),
    ]
    held = pl.pallas_call(
        functools.partial(restore_inner_kernel, z),
        out_shape=halves,
        in_specs=[SMEM] * 2 + [VMEM] * B,
        out_specs=[VMEM] * 2,
        scratch_shapes=[pltpu.VMEM((z.slabs(z.inner_rows), W, LANES), F32)],
        compiler_params=params(16),
        name="restore_inner",
    )(*who, *back[B:])
    spectrum_out, ocean_out, *_ = pl.pallas_call(
        functools.partial(restore_kernel, z),
        out_shape=[
            jax.ShapeDtypeStruct((nb * R, W), F32),
            jax.ShapeDtypeStruct((2 * L * R, W), F32),
        ]
        + halves,
        in_specs=[SMEM] * 2 + [VMEM] * (B + 2),
        out_specs=[HBM] * 2 + [VMEM] * 2,
        scratch_shapes=[
            pltpu.VMEM((z.slabs(z.edge_rows), W, LANES), F32),
            pltpu.SemaphoreType.DMA((2, W // LANES)),
        ],
        input_output_aliases={B + 2: 2, B + 3: 3},
        compiler_params=params(16),
        name="restore",
    )(*who, *back[:B], *held)
    return spectrum_out.reshape(nb, R, W), ocean_out.reshape(2, L, R, W)


def solution(mesh):
    return jax.shard_map(
        functools.partial(per_device, mesh.shape["geo"], mesh.shape["bins"]),
        mesh=mesh,
        in_specs=(
            P("bins", "geo", None),
            P("geo", None),
            P(),
            P(),
            P(),
            P(None, "bins", "geo", None),
        ),
        out_specs=(P("bins", "geo", None), P(None, "bins", "geo", None)),
        check_vma=False,
    )
```

```python
import functools

import jax
import jax.numpy as jnp
from jax import lax
from jax.experimental import pallas as pl
from jax.experimental.pallas import tpu as pltpu
from jax.sharding import PartitionSpec as P

NDIR = 36
NFREQ = 32
STEPS = 3
SUB = 2
DT_SOURCE = 0.5
DT_OCEAN = 0.2
CORIOLIS = 1.0
VISCOSITY = 1.0
DOPPLER = 0.1

LANES = 128
SUBLANES = 8
PAD = 8
HALO = SUB * STEPS
EDGE = 2
VMEM = pl.BlockSpec(memory_space=pltpu.VMEM)
SMEM = pl.BlockSpec(memory_space=pltpu.SMEM)
HBM = pl.BlockSpec(memory_space=pltpu.HBM)
F32 = jnp.float32
BF16 = jnp.bfloat16


def params(mib):
    return pltpu.CompilerParams(vmem_limit_bytes=mib * 1024 * 1024)


class Sizes:
    def __init__(self, parts, bins_here, levels_here, rows, width):
        self.B, self.nb, self.L, self.R, self.W = parts, bins_here, levels_here, rows, width
        self.C = width // parts
        self.mt = bins_here // LANES
        self.main = self.mt * LANES
        self.nr = bins_here - self.main
        self.no = 2 * levels_here
        self.NB = parts * bins_here
        self.CH = self.NB + LANES
        self.edge_rows = (rows - 2, rows - 1, 0, 1)
        self.inner_rows = tuple(range(2, rows - 2))
        self.half = parts // 2
        assert self.half & (self.half - 1) == 0 and self.half > 1
        assert self.nr * parts == LANES and self.no * parts == LANES

    def folds(self, rows):
        out, base = [], len(rows) * self.mt
        for count, tile in ((self.nr, self.B * self.mt), (self.no, self.NB // LANES)):
            used = min(LANES // count, len(rows))
            deep = len(rows) // used
            assert deep * used == len(rows)
            out.append((count, used, deep, base, tile))
            base += deep
        return out, base

    def halo(self, rows):
        return HALO if rows == self.edge_rows else PAD

    def slabs(self, rows):
        return self.folds(rows)[1]


def exchange_share(z, k, odd, part):
    core = part % 2
    flip, delta = (k // z.half) ^ core, (k % z.half) ^ core
    return (odd ^ flip) * z.half + ((part // 2) ^ delta)


def exchange_part(z, k, odd, part):
    core = (k // z.half) ^ odd ^ (part % 2)
    delta = (k % z.half) ^ core
    return ((part // 2) ^ delta) * 2 + core


def lane_group(width):
    return lax.broadcasted_iota(jnp.int32, (1, LANES), 1) // width


def pack_kernel(z, rows, odd, part, spec_in, ocean_in, mask_in, *refs):
    B, R, C, W, mt = z.B, z.R, z.C, z.W, z.mt
    outs, (spec, ocean, mask, wide, sems) = refs[:B], refs[B:]
    E, H = C + 2 * PAD, C + 2 * z.halo(rows)
    brought = slice((E - H) // 2, (E + H) // 2)
    copies = []
    for half in range(W // LANES):
        cols = pl.ds(half * LANES, LANES)
        for n, (src, dst) in enumerate(((spec_in, spec), (ocean_in, ocean))):
            copies.append(pltpu.make_async_copy(src.at[:, cols], dst.at[half], sems.at[n, half]))
            copies[-1].start()
    mask_copy = pltpu.make_async_copy(mask_in, mask, sems.at[2, 0])
    mask_copy.start()
    wide[:, 0:PAD, :] = jnp.zeros((wide.shape[0], PAD, LANES), F32)
    wide[:, PAD + W : W + 2 * PAD, :] = jnp.zeros((wide.shape[0], PAD, LANES), F32)
    folds, slabs = z.folds(rows)
    for half in range(W // LANES):
        for copy in copies[2 * half : 2 * half + 2]:
            copy.wait()
        cols = slice(PAD + half * LANES, PAD + (half + 1) * LANES)
        for i, r in enumerate(rows):
            for t in range(mt):
                block = spec[half, pl.ds(t * LANES * R + r, LANES, stride=R), :]
                wide[i * mt + t, cols] = block.T
        for (count, used, deep, base, _), src, first in zip(folds, (spec, ocean), (z.main, 0)):
            for rr in range(deep):
                pieces = [
                    src[half, pl.ds(first * R + rows[rr + i * deep], count, stride=R), :]
                    for i in range(used)
                ]
                if used * count < LANES:
                    pieces.append(jnp.zeros((LANES - used * count, LANES), F32))
                wide[base + rr, cols] = jnp.concatenate(pieces, axis=0).T
    mask_copy.wait()
    sea = jnp.concatenate([mask[...].astype(F32), jnp.zeros((R, LANES), F32)], axis=1)
    for k, out in enumerate(outs):
        share = exchange_share(z, k, odd[0], part[0])
        start = pl.multiple_of(share * C, PAD)
        for i in range(slabs):
            block = wide[i, pl.ds(start, E), :]
            out[i * H : (i + 1) * H] = block[brought]
        if rows == z.edge_rows:
            shift = lax.rem(W + LANES + PAD - start, W + LANES)
            out[slabs * H : slabs * H + R] = pltpu.roll(sea, shift, axis=1)[:, :LANES]


def spread_line(line):
    return jnp.broadcast_to(line, (LANES, LANES)).T


def unpack_kernel(z, rows, odd, part, *refs):
    B, mt = z.B, z.mt
    got, outs = refs[:B], refs[B:]
    E, H = z.C + 2 * PAD, z.C + 2 * z.halo(rows)
    brought = slice((E - H) // 2, (E + H) // 2)
    if rows == z.edge_rows:
        sea = outs[-1]
        outs = outs[:-1]
        lines = got[0][z.slabs(rows) * H : z.slabs(rows) * H + z.R]
        for r in range(z.R):
            sea[r] = spread_line(lines[r : r + 1])[:E]
    places = listed(*outs)
    for ref in outs:
        for columns in (slice(0, PAD), slice(E - PAD, E)):
            ref[:, :, columns] = jnp.zeros(ref.shape[:2] + (PAD, LANES), F32)
    src = [exchange_part(z, k, odd[0], part[0]) for k in range(B)]
    for k in range(B):
        for t in range(mt):
            for i, (ref, at) in enumerate(places):
                slab = i * mt + t
                ref[src[k] * mt + t, at, brought] = got[k][slab * H : (slab + 1) * H]
    for count, used, deep, base, home in z.folds(rows)[0]:
        group = lane_group(count)
        for i, (ref, at) in enumerate(places):
            tile = jnp.zeros((H, LANES), F32)
            for k in range(B):
                shift = lax.rem((src[k] - i // deep) * count + LANES, LANES)
                slab = base + i % deep
                moved = pltpu.roll(got[k][slab * H : (slab + 1) * H], shift, axis=1)
                tile = jnp.where(group == src[k], moved, tile)
            ref[home, at, brought] = tile
    if rows == z.edge_rows:
        for i, (ref, at) in enumerate(places):
            r = rows[i]
            ref[0, at, 0:1] = lines[r : r + 1]


def send_back_kernel(z, rows, odd, part, *refs):
    B, mt = z.B, z.mt
    states, outs = refs[:-B], refs[-B:]
    places = listed(*states)
    for k in range(B):
        src = exchange_part(z, k, odd[0], part[0])
        for t in range(mt):
            for i, (ref, at) in enumerate(places):
                outs[k][i * mt + t] = ref[src * mt + t, at]
        for count, used, deep, base, home in z.folds(rows)[0]:
            group = lane_group(count)
            for rr in range(deep):
                tile = jnp.zeros((z.C, LANES), F32)
                for i in range(used):
                    ref, at = places[rr + i * deep]
                    shift = lax.rem((i - src) * count + LANES, LANES)
                    moved = pltpu.roll(ref[home, at], shift, axis=1)
                    tile = jnp.where(group == i, moved, tile)
                outs[k][base + rr] = tile


def restore_rows(z, rows, odd, part, got, wide, spec, ocean):
    R, C, mt = z.R, z.C, z.mt
    folds, slabs = z.folds(rows)
    for k, block in enumerate(got):
        share = exchange_share(z, k, odd[0], part[0])
        wide[:, pl.ds(pl.multiple_of(share * C, PAD), C), :] = block[...]
    for half in range(z.W // LANES):
        cols = slice(half * LANES, (half + 1) * LANES)
        for i, r in enumerate(rows):
            for t in range(mt):
                place = pl.ds(t * LANES * R + r, LANES, stride=R)
                spec[half, place, :] = wide[i * mt + t, cols].T
        for (count, used, deep, base, _), dst, first in zip(folds, (spec, ocean), (z.main, 0)):
            for rr in range(deep):
                turned = wide[base + rr, cols].T
                for i in range(used):
                    place = pl.ds(first * R + rows[rr + i * deep], count, stride=R)
                    dst[half, place, :] = turned[i * count : (i + 1) * count]
        yield half


def restore_inner_kernel(z, odd, part, *refs):
    got, (spec, ocean, wide) = refs[: z.B], refs[z.B :]
    for _ in restore_rows(z, z.inner_rows, odd, part, got, wide, spec, ocean):
        pass


def restore_kernel(z, odd, part, *refs):
    got, (_, _, spec_out, ocean_out, spec, ocean, wide, sems) = refs[: z.B], refs[z.B :]
    copies = []
    for half in restore_rows(z, z.edge_rows, odd, part, got, wide, spec, ocean):
        cols = pl.ds(half * LANES, LANES)
        for n, (src, dst) in enumerate(((spec, spec_out), (ocean, ocean_out))):
            copies.append(pltpu.make_async_copy(src.at[half], dst.at[:, cols], sems.at[n, half]))
            copies[-1].start()
    for copy in copies:
        copy.wait()


def weights_kernel(z, linear, square, drift, weights, drift_weights):
    B, nb, main, nr, NB, L = z.B, z.nb, z.main, z.nr, z.NB, z.L

    def put(dst, first, lanes, turned):
        for s in range(B):
            dst[first + s * main : first + (s + 1) * main, lanes] = turned[
                s * nb : s * nb + main
            ]
            tail = first + B * main + s * nr
            dst[tail : tail + nr, lanes] = turned[s * nb + main : (s + 1) * nb]

    for n, source in enumerate((linear, square)):
        for s in range(B):
            for t in range(z.mt):
                block = source[s * nb + t * LANES : s * nb + (t + 1) * LANES, :]
                lane = s * main + t * LANES
                put(weights, n * NB, slice(lane, lane + LANES), block.T)
        tails = [source[s * nb + main : (s + 1) * nb, :] for s in range(B)]
        block = jnp.concatenate(tails, axis=0)
        put(weights, n * NB, slice(B * main, NB), block.T)

    row = lax.broadcasted_iota(jnp.int32, (LANES, LANES), 0)
    lane = lax.broadcasted_iota(jnp.int32, (LANES, LANES), 1)
    part, comp, level = lane // (2 * L), (lane // L) % 2, lane % L
    pick = jnp.where(row == 2 * (part * L + level) + 1 - comp, 1.0, 0.0).astype(BF16)
    turned = jnp.dot(drift[...].T, pick, preferred_element_type=F32).astype(BF16)
    put(drift_weights, 0, slice(0, LANES), turned)


def advance(
    z, sea_rows, rows, outs, cut, sea_at, speed, weights, drift_weights, moved, moved_twice,
    known=None, kept=None,
):
    NB, L, tiles = z.NB, z.L, z.NB // LANES
    known, kept = known or {}, kept or {}
    n = len(rows)
    first = [r for r in range(1, n - 1) if r not in known]
    assert first == list(range(first[0], first[-1] + 1))
    E = rows[0][0].shape[2]
    N = E - 2 * cut
    keep = slice(cut, cut + N)
    places = listed(*outs)
    T = E // SUBLANES
    offset = -cut % SUBLANES

    def apart(start):
        return [pl.ds(start + t, SUBLANES, stride=T) for t in range(T)]

    def sea_row(place):
        return place[0][place[1], pl.ds(sea_at, E)]

    def shift_up(parts):
        return [pltpu.roll(parts[-1], 1, axis=0)] + parts[:-1]

    def shift_down(parts):
        return parts[1:] + [pltpu.roll(parts[0], SUBLANES - 1, axis=0)]

    for r in range(min(first[0] - 1, 1), max(first[-1] + 2, n - 1)):
        ref, i = rows[r]
        surface = ref[tiles, i]
        moved[0, r] = DOPPLER * jnp.tanh(jnp.broadcast_to(surface[:, 0:1], (E, LANES)))
        moved[1, r] = DOPPLER * jnp.tanh(jnp.broadcast_to(surface[:, L : L + 1], (E, LANES)))

    def advect(read, write, start, stop, speed_cx, speed_cy):
        plus_before, waiting = None, None
        for r in range(start - 1, stop + 1):
            energy = read(r)
            speed_x = [speed_cx + moved[0, r, at, :] for at in apart(0)]
            if r >= start:
                minus = [jnp.minimum(v, 0.0) * e for v, e in zip(speed_x, energy)]
            if r > start:
                ref, i = sea_rows[r - 1]
                sea = [ref[i, at, :] for at in apart(sea_at)]
                write(r - 1, [(w - m) * s for w, m, s in zip(waiting, minus, sea)])
            if r < stop:
                plus = [jnp.maximum(v, 0.0) * e for v, e in zip(speed_x, energy)]
            if start <= r < stop:
                speed_y = [speed_cy + moved[1, r, at, :] for at in apart(0)]
                plus_y = [jnp.maximum(v, 0.0) * e for v, e in zip(speed_y, energy)]
                minus_y = [jnp.minimum(v, 0.0) * e for v, e in zip(speed_y, energy)]
                waiting = [
                    e - ((p - before) - m) - ((py - south) + (north - my))
                    for e, p, before, m, py, south, north, my in zip(
                        energy, plus, plus_before, minus,
                        plus_y, shift_up(plus_y), shift_down(minus_y), minus_y,
                    )
                ]
            plus_before = plus

    def one_tile(j, carry):
        lanes = pl.ds(pl.multiple_of(j * LANES, LANES), LANES)
        speed_cx = speed[0:1, lanes]
        speed_cy = speed[1:2, lanes]

        def in_order(t):
            return slice(t * SUBLANES, (t + 1) * SUBLANES)

        def read_first(r):
            ref, i = rows[r]
            return [ref[j, i, at, :] for at in apart(0)]

        def write_first(r, parts):
            for t, part in enumerate(parts):
                moved[2, r, in_order(t)] = part
                if r in kept:
                    ref, i = kept[r]
                    ref[j, i, in_order(t)] = part

        def read_second(r):
            if r in known:
                ref, i = known[r]
                return [ref[j, i, in_order(t)] for t in range(T)]
            return [moved[2, r, in_order(t)] for t in range(T)]

        def write_second(r, parts):
            for at, part in zip(apart(offset), parts):
                moved_twice[j, r - 2, at, :] = part

        advect(read_first, write_first, first[0], first[-1] + 1, speed_cx, speed_cy)
        advect(read_second, write_second, 2, n - 2, speed_cx, speed_cy)
        return carry

    lax.fori_loop(0, tiles, one_tile, 0)

    count = len(places)
    own_sea = sea_rows[2 : n - 2]
    own = slice(cut + offset, cut + offset + N)
    energy = jnp.concatenate(
        [moved_twice[j, :, own].reshape(count * N, LANES) for j in range(tiles)], axis=1
    )
    squares = energy * energy
    interaction = jnp.dot(
        energy.astype(BF16), weights[:NB], preferred_element_type=F32
    ) + jnp.dot(squares.astype(BF16), weights[NB:], preferred_element_type=F32)
    total = jnp.sum(squares, axis=1, keepdims=True)
    sea_here = jnp.concatenate([sea_row(place)[keep] for place in own_sea], axis=0)
    scale = (DT_SOURCE * sea_here[:, 0:1]) / (1.0 + total / NB)
    fresh = energy + scale * (interaction * energy)
    for i, (ref, at) in enumerate(places):
        for j in range(tiles):
            ref[j, at] = fresh[i * N : (i + 1) * N, j * LANES : (j + 1) * LANES]
    drift = jnp.dot(fresh.astype(BF16), drift_weights[...], preferred_element_type=F32)

    comp = (lax.broadcasted_iota(jnp.int32, (1, LANES), 1) // L) % 2
    sign = jnp.where(comp == 0, 1.0, -1.0).astype(F32)
    for i, (out, at) in enumerate(places):
        here, before, after = [
            ref[tiles, row] for ref, row in (rows[i + 2], rows[i + 1], rows[i + 3])
        ]
        lap = (
            (after + before)
            + (pltpu.roll(here, E - 1, axis=0) + pltpu.roll(here, 1, axis=0))
            - 4.0 * here
        )[keep]
        centre = here[keep]
        other = jnp.where(
            comp == 0, pltpu.roll(centre, LANES - L, axis=1), pltpu.roll(centre, L, axis=1)
        )
        turn = sign * (CORIOLIS * (other + drift[i * N : (i + 1) * N]))
        out[tiles, at] = (
            centre + DT_OCEAN * (turn + VISCOSITY * lap)
        ) * sea_row(own_sea[i])[keep]


def listed(*refs):
    return [(ref, i) for ref in refs for i in range(ref.shape[-3])]


def inner_kernel(z, first, cut, sea_at, top, inner, bottom, sea, speed, weights, drift_weights, *refs):
    out, for_edges, (moved, moved_twice) = refs[0], refs[1:-2], refs[-2:]
    kept = {}
    if for_edges:
        kept = {1 + i: (for_edges[0], i) for i in range(EDGE)}
        kept |= {z.R - 1 - EDGE + i: (for_edges[1], i) for i in range(EDGE)}
    advance(
        z, listed(sea), listed(top, inner, bottom), [out], cut, sea_at, speed, weights,
        drift_weights, moved, moved_twice, kept=kept,
    )


def read_sea(halo, sea):
    for i in range(EDGE):
        sea[i] = spread_line(halo[0, i, 0:1])[: halo.shape[2]]
    return sea


def top_kernel(z, first, cut, sea_at, up, top, inner, sea, *refs):
    inputs, outs = refs[:-4] if first else refs[:-3], refs[-4:] if first else refs[-3:]
    *given, speed, weights, drift_weights = inputs
    out, moved, moved_twice = outs[0], outs[-2], outs[-1]
    sea_up = read_sea(up, outs[1]) if first else given.pop(0)
    known = {3 + i: (given[0], i) for i in range(EDGE)} if given else {}
    rows = listed(up, top) + listed(inner)[:EDGE]
    sea_rows = (listed(sea_up) + listed(sea))[: len(rows)]
    advance(
        z, sea_rows, rows, [out], cut, sea_at, speed, weights, drift_weights, moved,
        moved_twice, known=known,
    )


def bottom_kernel(z, first, cut, sea_at, down, bottom, inner, sea, *refs):
    inputs, outs = refs[:-4] if first else refs[:-3], refs[-4:] if first else refs[-3:]
    *given, speed, weights, drift_weights = inputs
    out, moved, moved_twice = outs[0], outs[-2], outs[-1]
    sea_down = read_sea(down, outs[1]) if first else given.pop(0)
    known = {1 + i: (given[0], i) for i in range(EDGE)} if given else {}
    rows = listed(inner)[-EDGE:] + listed(bottom, down)
    sea_rows = (listed(sea) + listed(sea_down))[-len(rows) :]
    advance(
        z, sea_rows, rows, [out], cut, sea_at, speed, weights, drift_weights, moved,
        moved_twice, known=known,
    )


def speeds(z):
    lane = jnp.arange(z.NB, dtype=jnp.int32)
    head = (lane // z.main) * z.nb + lane % z.main
    rest = lane - z.B * z.main
    tail = (rest // z.nr) * z.nb + z.main + rest % z.nr
    bin_index = jnp.where(lane < z.B * z.main, head, tail)
    direction = (bin_index // NFREQ).astype(F32)
    frequency = (bin_index % NFREQ).astype(F32)
    group_speed = 0.4 / (1.0 + frequency / 16.0)
    bin_angle = (2.0 * jnp.pi / NDIR) * direction
    zeros = jnp.zeros_like(bin_angle)
    rows = [group_speed * jnp.cos(bin_angle), group_speed * jnp.sin(bin_angle)] + [zeros] * 6
    return jnp.stack(rows)


def cost(flops, moved):
    return pl.CostEstimate(flops=int(flops), bytes_accessed=int(moved), transcendentals=0)


def per_device(G, B, spectrum, sea_mask, kernel_linear, kernel_square, drift_kernel, ocean):
    nb, R, W = spectrum.shape
    L = ocean.shape[1]
    z = Sizes(B, nb, L, R, W)
    C, NB, CH = z.C, z.NB, z.CH
    half = B // 2
    axes = ("geo", "bins")
    geo, part = lax.axis_index("geo"), lax.axis_index("bins")

    def device_at(q, c):
        return ((q // 2) * 2 + c // half) * B + 2 * (c % half) + q % 2

    forward = [
        [
            (g * B + b, device_at(g, exchange_share(z, k, g % 2, b)))
            for g in range(G)
            for b in range(B)
        ]
        for k in range(B)
    ]
    pairs = [(q, c) for q in range(G) for c in range(B)]
    to_next_row = [(device_at(q, c), device_at((q + 1) % G, c)) for q, c in pairs]
    to_prev_row = [(t, s) for s, t in to_next_row]
    who = ((geo % 2).astype(jnp.int32).reshape(1), part.astype(jnp.int32).reshape(1))

    width = C + 2 * PAD
    columns_scratch = [
        pltpu.VMEM((W // LANES, nb * R, LANES), F32),
        pltpu.VMEM((W // LANES, 2 * L * R, LANES), F32),
    ]
    def pack(rows, who):
        slabs = z.slabs(rows)
        lines = slabs * (C + 2 * z.halo(rows)) + (R if rows == z.edge_rows else 0)
        return pl.pallas_call(
            functools.partial(pack_kernel, z, rows),
            out_shape=[jax.ShapeDtypeStruct((lines, LANES), F32)] * B,
            in_specs=[SMEM] * 2 + [HBM] * 3,
            out_specs=[VMEM] * B,
            scratch_shapes=columns_scratch
            + [
                pltpu.VMEM((R, W), jnp.int32),
                pltpu.VMEM((slabs, W + 2 * PAD, LANES), F32),
                pltpu.SemaphoreType.DMA((3, W // LANES)),
            ],
            compiler_params=params(58),
            name="pack",
        )(*who, spectrum.reshape(nb * R, W), ocean.reshape(2 * L * R, W), sea_mask)

    packed = pack(z.edge_rows, who)
    got = [lax.ppermute(packed[k], axes, forward[k]) for k in range(B)]
    later, _ = lax.optimization_barrier((who, packed[0]))
    packed = pack(z.inner_rows, later)

    weights, drift_weights = pl.pallas_call(
        functools.partial(weights_kernel, z),
        out_shape=(
            jax.ShapeDtypeStruct((2 * NB, NB), BF16),
            jax.ShapeDtypeStruct((NB, LANES), BF16),
        ),
        in_specs=[VMEM] * 3,
        out_specs=(VMEM,) * 2,
        compiler_params=params(24),
        cost_estimate=cost(2e9, 4 * NB * NB * 2),
        name="weights",
    )(kernel_linear, kernel_square, drift_kernel)
    speed = speeds(z)
    *got, weights, drift_weights, speed = lax.optimization_barrier(
        (*got, weights, drift_weights, speed)
    )

    def state(rows, columns):
        return (CH // LANES, rows, columns, LANES)

    def unpack(rows, received, shapes):
        return pl.pallas_call(
            functools.partial(unpack_kernel, z, rows),
            out_shape=[jax.ShapeDtypeStruct(shape, F32) for shape in shapes],
            in_specs=[SMEM] * 2 + [VMEM] * B,
            out_specs=[VMEM] * len(shapes),
            compiler_params=params(16),
            name="unpack",
        )(*who, *received)

    bottom, top, sea = unpack(
        z.edge_rows, got[:B], [state(EDGE, width), state(EDGE, width), (R, width, LANES)]
    )
    *blocks, top = lax.optimization_barrier((*packed[half:], top))
    blocks = list(packed[:half]) + blocks
    got = [lax.ppermute(blocks[k], axes, forward[k]) for k in range(B)]
    (inner,) = unpack(z.inner_rows, got, [state(R - 2 * EDGE, width)])

    def step_call(body, first, cut, sea_at, count, deepest, inputs, more=()):
        width = inputs[0].shape[2]
        n = width - 2 * cut
        shapes = [state(count, n)] + [before + (EDGE, width, LANES) for before in more]
        return pl.pallas_call(
            functools.partial(body, z, first, cut, sea_at),
            out_shape=[jax.ShapeDtypeStruct(shape, F32) for shape in shapes],
            in_specs=[VMEM] * (len(inputs) + 3),
            out_specs=[VMEM] * len(shapes),
            scratch_shapes=[
                pltpu.VMEM((3, deepest, width, LANES), F32),
                pltpu.VMEM((NB // LANES, count, width + PAD, LANES), F32),
            ],
            compiler_params=params(24),
            cost_estimate=cost(count * 1e8, count * 1e5),
            name=body.__name__,
        )(*inputs, speed, weights, drift_weights)

    sea_up, sea_down = [], []
    for step in range(STEPS):
        valid = EDGE * (STEPS - 1 - step)
        margin = (width - C) // 2
        cut = margin - valid if valid == 0 or (margin - valid) % 4 == 0 else 0
        sea_at = PAD - margin
        down = lax.ppermute(top, axes, to_prev_row)
        up = lax.ppermute(bottom, axes, to_next_row)
        first = step == 0

        def advance_inner():
            return step_call(
                inner_kernel, first, cut, sea_at, R - 2 * EDGE, R, (top, inner, bottom, sea),
                () if first else ((NB // LANES,),) * 2,
            )

        given = ()
        if not first:
            new_inner, *given = advance_inner()
        new_bottom, *found = step_call(
            bottom_kernel, first, cut, sea_at, EDGE, 3 * EDGE,
            (down, bottom, inner, sea, *sea_down, *given[1:]),
            ((),) if first else (),
        )
        sea_down = sea_down or found
        new_top, *found = step_call(
            top_kernel, first, cut, sea_at, EDGE, 3 * EDGE,
            (up, top, inner, sea, *sea_up, *given[:1]),
            ((),) if first else (),
        )
        sea_up = sea_up or found
        if first:
            inner, new_top = lax.optimization_barrier((inner, new_top))
            (new_inner,) = advance_inner()
        top, inner, bottom = new_top, new_inner, new_bottom
        width -= 2 * cut

    def send_back(rows, states):
        shape = jax.ShapeDtypeStruct((z.slabs(rows), C, LANES), F32)
        return pl.pallas_call(
            functools.partial(send_back_kernel, z, rows),
            out_shape=[shape] * B,
            in_specs=[SMEM] * 2 + [VMEM] * len(states),
            out_specs=[VMEM] * B,
            compiler_params=params(16),
            name="send_back",
        )(*who, *states)

    packed = send_back(z.inner_rows, [inner]), send_back(z.edge_rows, [bottom, top])
    packed = list(packed[1]) + list(packed[0])
    back = [
        lax.ppermute(packed[i], axes, [(t, s) for s, t in forward[i % B]]) for i in range(2 * B)
    ]
    halves = [
        jax.ShapeDtypeStruct((W // LANES, nb * R, LANES), F32),
        jax.ShapeDtypeStruct((W // LANES, 2 * L * R, LANES), F32),
    ]
    held = pl.pallas_call(
        functools.partial(restore_inner_kernel, z),
        out_shape=halves,
        in_specs=[SMEM] * 2 + [VMEM] * B,
        out_specs=[VMEM] * 2,
        scratch_shapes=[pltpu.VMEM((z.slabs(z.inner_rows), W, LANES), F32)],
        compiler_params=params(16),
        name="restore_inner",
    )(*who, *back[B:])
    spectrum_out, ocean_out, *_ = pl.pallas_call(
        functools.partial(restore_kernel, z),
        out_shape=[
            jax.ShapeDtypeStruct((nb * R, W), F32),
            jax.ShapeDtypeStruct((2 * L * R, W), F32),
        ]
        + halves,
        in_specs=[SMEM] * 2 + [VMEM] * (B + 2),
        out_specs=[HBM] * 2 + [VMEM] * 2,
        scratch_shapes=[
            pltpu.VMEM((z.slabs(z.edge_rows), W, LANES), F32),
            pltpu.SemaphoreType.DMA((2, W // LANES)),
        ],
        input_output_aliases={B + 2: 2, B + 3: 3},
        compiler_params=params(16),
        name="restore",
    )(*who, *back[:B], *held)
    return spectrum_out.reshape(nb, R, W), ocean_out.reshape(2, L, R, W)


def solution(mesh):
    return jax.shard_map(
        functools.partial(per_device, mesh.shape["geo"], mesh.shape["bins"]),
        mesh=mesh,
        in_specs=(
            P("bins", "geo", None),
            P("geo", None),
            P(),
            P(),
            P(),
            P(None, "bins", "geo", None),
        ),
        out_specs=(P("bins", "geo", None), P(None, "bins", "geo", None)),
        check_vma=False,
    )
```

```python
import functools

import jax
import jax.numpy as jnp
from jax import lax
from jax.experimental import pallas as pl
from jax.experimental.pallas import tpu as pltpu
from jax.sharding import PartitionSpec as P

NDIR = 36
NFREQ = 32
STEPS = 3
SUB = 2
DT_SOURCE = 0.5
DT_OCEAN = 0.2
CORIOLIS = 1.0
VISCOSITY = 1.0
DOPPLER = 0.1

LANES = 128
SUBLANES = 8
PAD = 8
HALO = SUB * STEPS
EDGE = 2
VMEM = pl.BlockSpec(memory_space=pltpu.VMEM)
SMEM = pl.BlockSpec(memory_space=pltpu.SMEM)
HBM = pl.BlockSpec(memory_space=pltpu.HBM)
F32 = jnp.float32
BF16 = jnp.bfloat16


def params(mib):
    return pltpu.CompilerParams(vmem_limit_bytes=mib * 1024 * 1024)


class Sizes:
    def __init__(self, parts, bins_here, levels_here, rows, width):
        self.B, self.nb, self.L, self.R, self.W = parts, bins_here, levels_here, rows, width
        self.C = width // parts
        self.mt = bins_here // LANES
        self.main = self.mt * LANES
        self.nr = bins_here - self.main
        self.no = 2 * levels_here
        self.NB = parts * bins_here
        self.CH = self.NB + LANES
        self.edge_rows = (rows - 2, rows - 1, 0, 1)
        self.inner_rows = tuple(range(2, rows - 2))
        self.half = parts // 2
        assert self.half & (self.half - 1) == 0 and self.half > 1
        assert self.nr * parts == LANES and self.no * parts == LANES

    def folds(self, rows):
        out, base = [], len(rows) * self.mt
        for count, tile in ((self.nr, self.B * self.mt), (self.no, self.NB // LANES)):
            used = min(LANES // count, len(rows))
            deep = len(rows) // used
            assert deep * used == len(rows)
            out.append((count, used, deep, base, tile))
            base += deep
        return out, base

    def halo(self, rows):
        return HALO if rows == self.edge_rows else PAD

    def slabs(self, rows):
        return self.folds(rows)[1]


def exchange_share(z, k, odd, part):
    core = part % 2
    flip, delta = (k // z.half) ^ core, (k % z.half) ^ core
    return (odd ^ flip) * z.half + ((part // 2) ^ delta)


def exchange_part(z, k, odd, part):
    core = (k // z.half) ^ odd ^ (part % 2)
    delta = (k % z.half) ^ core
    return ((part // 2) ^ delta) * 2 + core


def lane_group(width):
    return lax.broadcasted_iota(jnp.int32, (1, LANES), 1) // width


def pack_kernel(z, rows, odd, part, spec_in, ocean_in, mask_in, *refs):
    B, R, C, W, mt = z.B, z.R, z.C, z.W, z.mt
    outs, (spec, ocean, mask, wide, sems) = refs[:B], refs[B:]
    E, H = C + 2 * PAD, C + 2 * z.halo(rows)
    brought = slice((E - H) // 2, (E + H) // 2)
    copies = []
    for half in range(W // LANES):
        cols = pl.ds(half * LANES, LANES)
        for n, (src, dst) in enumerate(((spec_in, spec), (ocean_in, ocean))):
            copies.append(pltpu.make_async_copy(src.at[:, cols], dst.at[half], sems.at[n, half]))
            copies[-1].start()
    mask_copy = pltpu.make_async_copy(mask_in, mask, sems.at[2, 0])
    mask_copy.start()
    wide[:, 0:PAD, :] = jnp.zeros((wide.shape[0], PAD, LANES), F32)
    wide[:, PAD + W : W + 2 * PAD, :] = jnp.zeros((wide.shape[0], PAD, LANES), F32)
    folds, slabs = z.folds(rows)
    for half in range(W // LANES):
        for copy in copies[2 * half : 2 * half + 2]:
            copy.wait()
        cols = slice(PAD + half * LANES, PAD + (half + 1) * LANES)
        for i, r in enumerate(rows):
            for t in range(mt):
                block = spec[half, pl.ds(t * LANES * R + r, LANES, stride=R), :]
                wide[i * mt + t, cols] = block.T
        for (count, used, deep, base, _), src, first in zip(folds, (spec, ocean), (z.main, 0)):
            for rr in range(deep):
                pieces = [
                    src[half, pl.ds(first * R + rows[rr + i * deep], count, stride=R), :]
                    for i in range(used)
                ]
                if used * count < LANES:
                    pieces.append(jnp.zeros((LANES - used * count, LANES), F32))
                wide[base + rr, cols] = jnp.concatenate(pieces, axis=0).T
    mask_copy.wait()
    sea = jnp.concatenate([mask[...].astype(F32), jnp.zeros((R, LANES), F32)], axis=1)
    for k, out in enumerate(outs):
        share = exchange_share(z, k, odd[0], part[0])
        start = pl.multiple_of(share * C, PAD)
        for i in range(slabs):
            block = wide[i, pl.ds(start, E), :]
            out[i * H : (i + 1) * H] = block[brought]
        if rows == z.edge_rows:
            shift = lax.rem(W + LANES + PAD - start, W + LANES)
            out[slabs * H : slabs * H + R] = pltpu.roll(sea, shift, axis=1)[:, :LANES]


def spread_line(line):
    return jnp.broadcast_to(line, (LANES, LANES)).T


def unpack_kernel(z, rows, odd, part, *refs):
    B, mt = z.B, z.mt
    got, outs = refs[:B], refs[B:]
    E, H = z.C + 2 * PAD, z.C + 2 * z.halo(rows)
    brought = slice((E - H) // 2, (E + H) // 2)
    if rows == z.edge_rows:
        sea = outs[-1]
        outs = outs[:-1]
        lines = got[0][z.slabs(rows) * H : z.slabs(rows) * H + z.R]
        for r in range(z.R):
            sea[r] = spread_line(lines[r : r + 1])[:E]
    places = listed(*outs)
    for ref in outs:
        for columns in (slice(0, PAD), slice(E - PAD, E)):
            ref[:, :, columns] = jnp.zeros(ref.shape[:2] + (PAD, LANES), F32)
    src = [exchange_part(z, k, odd[0], part[0]) for k in range(B)]
    for k in range(B):
        for t in range(mt):
            for i, (ref, at) in enumerate(places):
                slab = i * mt + t
                ref[src[k] * mt + t, at, brought] = got[k][slab * H : (slab + 1) * H]
    for count, used, deep, base, home in z.folds(rows)[0]:
        group = lane_group(count)
        for i, (ref, at) in enumerate(places):
            tile = jnp.zeros((H, LANES), F32)
            for k in range(B):
                shift = lax.rem((src[k] - i // deep) * count + LANES, LANES)
                slab = base + i % deep
                moved = pltpu.roll(got[k][slab * H : (slab + 1) * H], shift, axis=1)
                tile = jnp.where(group == src[k], moved, tile)
            ref[home, at, brought] = tile
    if rows == z.edge_rows:
        for i, (ref, at) in enumerate(places):
            r = rows[i]
            ref[0, at, 0:1] = lines[r : r + 1]


def send_back_kernel(z, rows, odd, part, *refs):
    B, mt = z.B, z.mt
    states, outs = refs[:-B], refs[-B:]
    places = listed(*states)
    for k in range(B):
        src = exchange_part(z, k, odd[0], part[0])
        for t in range(mt):
            for i, (ref, at) in enumerate(places):
                outs[k][i * mt + t] = ref[src * mt + t, at]
        for count, used, deep, base, home in z.folds(rows)[0]:
            group = lane_group(count)
            for rr in range(deep):
                tile = jnp.zeros((z.C, LANES), F32)
                for i in range(used):
                    ref, at = places[rr + i * deep]
                    shift = lax.rem((i - src) * count + LANES, LANES)
                    moved = pltpu.roll(ref[home, at], shift, axis=1)
                    tile = jnp.where(group == i, moved, tile)
                outs[k][base + rr] = tile


def restore_rows(z, rows, odd, part, got, wide, spec, ocean):
    R, C, mt = z.R, z.C, z.mt
    folds, slabs = z.folds(rows)
    for k, block in enumerate(got):
        share = exchange_share(z, k, odd[0], part[0])
        wide[:, pl.ds(pl.multiple_of(share * C, PAD), C), :] = block[...]
    for half in range(z.W // LANES):
        cols = slice(half * LANES, (half + 1) * LANES)
        for i, r in enumerate(rows):
            for t in range(mt):
                place = pl.ds(t * LANES * R + r, LANES, stride=R)
                spec[half, place, :] = wide[i * mt + t, cols].T
        for (count, used, deep, base, _), dst, first in zip(folds, (spec, ocean), (z.main, 0)):
            for rr in range(deep):
                turned = wide[base + rr, cols].T
                for i in range(used):
                    place = pl.ds(first * R + rows[rr + i * deep], count, stride=R)
                    dst[half, place, :] = turned[i * count : (i + 1) * count]
        yield half


def restore_inner_kernel(z, odd, part, *refs):
    got, (spec, ocean, wide) = refs[: z.B], refs[z.B :]
    for _ in restore_rows(z, z.inner_rows, odd, part, got, wide, spec, ocean):
        pass


def restore_kernel(z, odd, part, *refs):
    got, (_, _, spec_out, ocean_out, spec, ocean, wide, sems) = refs[: z.B], refs[z.B :]
    copies = []
    for half in restore_rows(z, z.edge_rows, odd, part, got, wide, spec, ocean):
        cols = pl.ds(half * LANES, LANES)
        for n, (src, dst) in enumerate(((spec, spec_out), (ocean, ocean_out))):
            copies.append(pltpu.make_async_copy(src.at[half], dst.at[:, cols], sems.at[n, half]))
            copies[-1].start()
    for copy in copies:
        copy.wait()


def weights_kernel(z, linear, square, drift, weights, drift_weights):
    B, nb, main, nr, NB, L = z.B, z.nb, z.main, z.nr, z.NB, z.L

    def put(dst, first, lanes, turned):
        for s in range(B):
            dst[first + s * main : first + (s + 1) * main, lanes] = turned[
                s * nb : s * nb + main
            ]
            tail = first + B * main + s * nr
            dst[tail : tail + nr, lanes] = turned[s * nb + main : (s + 1) * nb]

    for n, source in enumerate((linear, square)):
        for s in range(B):
            for t in range(z.mt):
                block = source[s * nb + t * LANES : s * nb + (t + 1) * LANES, :]
                lane = s * main + t * LANES
                put(weights, n * NB, slice(lane, lane + LANES), block.T)
        tails = [source[s * nb + main : (s + 1) * nb, :] for s in range(B)]
        block = jnp.concatenate(tails, axis=0)
        put(weights, n * NB, slice(B * main, NB), block.T)

    row = lax.broadcasted_iota(jnp.int32, (LANES, LANES), 0)
    lane = lax.broadcasted_iota(jnp.int32, (LANES, LANES), 1)
    part, comp, level = lane // (2 * L), (lane // L) % 2, lane % L
    pick = jnp.where(row == 2 * (part * L + level) + 1 - comp, 1.0, 0.0).astype(BF16)
    turned = jnp.dot(drift[...].T, pick, preferred_element_type=F32).astype(BF16)
    put(drift_weights, 0, slice(0, LANES), turned)


def advance(
    z, sea_rows, rows, outs, cut, sea_at, speed, weights, drift_weights, moved, moved_twice,
    known=None, kept=None,
):
    NB, L, tiles = z.NB, z.L, z.NB // LANES
    known, kept = known or {}, kept or {}
    n = len(rows)
    first = [r for r in range(1, n - 1) if r not in known]
    assert first == list(range(first[0], first[-1] + 1))
    E = rows[0][0].shape[2]
    N = E - 2 * cut
    keep = slice(cut, cut + N)
    places = listed(*outs)
    T = E // SUBLANES
    offset = -cut % SUBLANES

    def apart(start):
        return [pl.ds(start + t, SUBLANES, stride=T) for t in range(T)]

    def sea_row(place):
        return place[0][place[1], pl.ds(sea_at, E)]

    def shift_up(parts):
        return [pltpu.roll(parts[-1], 1, axis=0)] + parts[:-1]

    def shift_down(parts):
        return parts[1:] + [pltpu.roll(parts[0], SUBLANES - 1, axis=0)]

    def in_order(t):
        return slice(t * SUBLANES, (t + 1) * SUBLANES)

    for r in range(min(first[0] - 1, 1), max(first[-1] + 2, n - 1)):
        for t in range(T):
            ref, i = rows[r]
            current = DOPPLER * jnp.tanh(ref[tiles, i, apart(0)[t], :])
            for c in range(2):
                one = current[:, c * L : c * L + 1]
                moved[c, r, in_order(t)] = jnp.broadcast_to(one, (SUBLANES, LANES))
            ref, i = sea_rows[r]
            moved[3, r, in_order(t)] = ref[i, apart(sea_at)[t], :]

    def advect(read, write, start, stop, speed_cx, speed_cy):
        plus_before, waiting = None, None
        for r in range(start - 1, stop + 1):
            energy = read(r)
            speed_x = [speed_cx + moved[0, r, in_order(t)] for t in range(T)]
            if r >= start:
                minus = [jnp.minimum(v, 0.0) * e for v, e in zip(speed_x, energy)]
            if r > start:
                sea = [moved[3, r - 1, in_order(t)] for t in range(T)]
                write(r - 1, [(w - m) * s for w, m, s in zip(waiting, minus, sea)])
            if r < stop:
                plus = [jnp.maximum(v, 0.0) * e for v, e in zip(speed_x, energy)]
            if start <= r < stop:
                speed_y = [speed_cy + moved[1, r, in_order(t)] for t in range(T)]
                plus_y = [jnp.maximum(v, 0.0) * e for v, e in zip(speed_y, energy)]
                minus_y = [jnp.minimum(v, 0.0) * e for v, e in zip(speed_y, energy)]
                waiting = [
                    e - ((p - before) - m) - ((py - south) + (north - my))
                    for e, p, before, m, py, south, north, my in zip(
                        energy, plus, plus_before, minus,
                        plus_y, shift_up(plus_y), shift_down(minus_y), minus_y,
                    )
                ]
            plus_before = plus

    def one_tile(j, carry):
        lanes = pl.ds(pl.multiple_of(j * LANES, LANES), LANES)
        speed_cx = speed[0:1, lanes]
        speed_cy = speed[1:2, lanes]

        def read_first(r):
            ref, i = rows[r]
            return [ref[j, i, at, :] for at in apart(0)]

        def write_first(r, parts):
            for t, part in enumerate(parts):
                moved[2, r, in_order(t)] = part
                if r in kept:
                    ref, i = kept[r]
                    ref[j, i, in_order(t)] = part

        def read_second(r):
            if r in known:
                ref, i = known[r]
                return [ref[j, i, in_order(t)] for t in range(T)]
            return [moved[2, r, in_order(t)] for t in range(T)]

        def write_second(r, parts):
            for at, part in zip(apart(offset), parts):
                moved_twice[j, r - 2, at, :] = part

        advect(read_first, write_first, first[0], first[-1] + 1, speed_cx, speed_cy)
        advect(read_second, write_second, 2, n - 2, speed_cx, speed_cy)
        return carry

    lax.fori_loop(0, tiles, one_tile, 0)

    count = len(places)
    own_sea = sea_rows[2 : n - 2]
    own = slice(cut + offset, cut + offset + N)
    energy = jnp.concatenate(
        [moved_twice[j, :, own].reshape(count * N, LANES) for j in range(tiles)], axis=1
    )
    squares = energy * energy
    interaction = jnp.dot(
        energy.astype(BF16), weights[:NB], preferred_element_type=F32
    ) + jnp.dot(squares.astype(BF16), weights[NB:], preferred_element_type=F32)
    total = jnp.sum(squares, axis=1, keepdims=True)
    sea_here = jnp.concatenate([sea_row(place)[keep] for place in own_sea], axis=0)
    scale = (DT_SOURCE * sea_here[:, 0:1]) / (1.0 + total / NB)
    fresh = energy + scale * (interaction * energy)
    for i, (ref, at) in enumerate(places):
        for j in range(tiles):
            ref[j, at] = fresh[i * N : (i + 1) * N, j * LANES : (j + 1) * LANES]
    drift = jnp.dot(fresh.astype(BF16), drift_weights[...], preferred_element_type=F32)

    comp = (lax.broadcasted_iota(jnp.int32, (1, LANES), 1) // L) % 2
    sign = jnp.where(comp == 0, 1.0, -1.0).astype(F32)
    for i, (out, at) in enumerate(places):
        here, before, after = [
            ref[tiles, row] for ref, row in (rows[i + 2], rows[i + 1], rows[i + 3])
        ]
        lap = (
            (after + before)
            + (pltpu.roll(here, E - 1, axis=0) + pltpu.roll(here, 1, axis=0))
            - 4.0 * here
        )[keep]
        centre = here[keep]
        other = jnp.where(
            comp == 0, pltpu.roll(centre, LANES - L, axis=1), pltpu.roll(centre, L, axis=1)
        )
        turn = sign * (CORIOLIS * (other + drift[i * N : (i + 1) * N]))
        out[tiles, at] = (
            centre + DT_OCEAN * (turn + VISCOSITY * lap)
        ) * sea_row(own_sea[i])[keep]


def listed(*refs):
    return [(ref, i) for ref in refs for i in range(ref.shape[-3])]


def inner_kernel(z, first, cut, sea_at, top, inner, bottom, sea, speed, weights, drift_weights, *refs):
    out, for_edges, (moved, moved_twice) = refs[0], refs[1:-2], refs[-2:]
    kept = {}
    if for_edges:
        kept = {1 + i: (for_edges[0], i) for i in range(EDGE)}
        kept |= {z.R - 1 - EDGE + i: (for_edges[1], i) for i in range(EDGE)}
    advance(
        z, listed(sea), listed(top, inner, bottom), [out], cut, sea_at, speed, weights,
        drift_weights, moved, moved_twice, kept=kept,
    )


def read_sea(halo, sea):
    for i in range(EDGE):
        sea[i] = spread_line(halo[0, i, 0:1])[: halo.shape[2]]
    return sea


def top_kernel(z, first, cut, sea_at, up, top, inner, sea, *refs):
    inputs, outs = refs[:-4] if first else refs[:-3], refs[-4:] if first else refs[-3:]
    *given, speed, weights, drift_weights = inputs
    out, moved, moved_twice = outs[0], outs[-2], outs[-1]
    sea_up = read_sea(up, outs[1]) if first else given.pop(0)
    known = {3 + i: (given[0], i) for i in range(EDGE)} if given else {}
    rows = listed(up, top) + listed(inner)[:EDGE]
    sea_rows = (listed(sea_up) + listed(sea))[: len(rows)]
    advance(
        z, sea_rows, rows, [out], cut, sea_at, speed, weights, drift_weights, moved,
        moved_twice, known=known,
    )


def bottom_kernel(z, first, cut, sea_at, down, bottom, inner, sea, *refs):
    inputs, outs = refs[:-4] if first else refs[:-3], refs[-4:] if first else refs[-3:]
    *given, speed, weights, drift_weights = inputs
    out, moved, moved_twice = outs[0], outs[-2], outs[-1]
    sea_down = read_sea(down, outs[1]) if first else given.pop(0)
    known = {1 + i: (given[0], i) for i in range(EDGE)} if given else {}
    rows = listed(inner)[-EDGE:] + listed(bottom, down)
    sea_rows = (listed(sea) + listed(sea_down))[-len(rows) :]
    advance(
        z, sea_rows, rows, [out], cut, sea_at, speed, weights, drift_weights, moved,
        moved_twice, known=known,
    )


def speeds(z):
    lane = jnp.arange(z.NB, dtype=jnp.int32)
    head = (lane // z.main) * z.nb + lane % z.main
    rest = lane - z.B * z.main
    tail = (rest // z.nr) * z.nb + z.main + rest % z.nr
    bin_index = jnp.where(lane < z.B * z.main, head, tail)
    direction = (bin_index // NFREQ).astype(F32)
    frequency = (bin_index % NFREQ).astype(F32)
    group_speed = 0.4 / (1.0 + frequency / 16.0)
    bin_angle = (2.0 * jnp.pi / NDIR) * direction
    zeros = jnp.zeros_like(bin_angle)
    rows = [group_speed * jnp.cos(bin_angle), group_speed * jnp.sin(bin_angle)] + [zeros] * 6
    return jnp.stack(rows)


def cost(flops, moved):
    return pl.CostEstimate(flops=int(flops), bytes_accessed=int(moved), transcendentals=0)


def per_device(G, B, spectrum, sea_mask, kernel_linear, kernel_square, drift_kernel, ocean):
    nb, R, W = spectrum.shape
    L = ocean.shape[1]
    z = Sizes(B, nb, L, R, W)
    C, NB, CH = z.C, z.NB, z.CH
    half = B // 2
    axes = ("geo", "bins")
    geo, part = lax.axis_index("geo"), lax.axis_index("bins")

    def device_at(q, c):
        return ((q // 2) * 2 + c // half) * B + 2 * (c % half) + q % 2

    forward = [
        [
            (g * B + b, device_at(g, exchange_share(z, k, g % 2, b)))
            for g in range(G)
            for b in range(B)
        ]
        for k in range(B)
    ]
    pairs = [(q, c) for q in range(G) for c in range(B)]
    to_next_row = [(device_at(q, c), device_at((q + 1) % G, c)) for q, c in pairs]
    to_prev_row = [(t, s) for s, t in to_next_row]
    who = ((geo % 2).astype(jnp.int32).reshape(1), part.astype(jnp.int32).reshape(1))

    width = C + 2 * PAD
    columns_scratch = [
        pltpu.VMEM((W // LANES, nb * R, LANES), F32),
        pltpu.VMEM((W // LANES, 2 * L * R, LANES), F32),
    ]
    def pack(rows, who):
        slabs = z.slabs(rows)
        lines = slabs * (C + 2 * z.halo(rows)) + (R if rows == z.edge_rows else 0)
        return pl.pallas_call(
            functools.partial(pack_kernel, z, rows),
            out_shape=[jax.ShapeDtypeStruct((lines, LANES), F32)] * B,
            in_specs=[SMEM] * 2 + [HBM] * 3,
            out_specs=[VMEM] * B,
            scratch_shapes=columns_scratch
            + [
                pltpu.VMEM((R, W), jnp.int32),
                pltpu.VMEM((slabs, W + 2 * PAD, LANES), F32),
                pltpu.SemaphoreType.DMA((3, W // LANES)),
            ],
            compiler_params=params(58),
            name="pack",
        )(*who, spectrum.reshape(nb * R, W), ocean.reshape(2 * L * R, W), sea_mask)

    packed = pack(z.edge_rows, who)
    got = [lax.ppermute(packed[k], axes, forward[k]) for k in range(B)]
    later, _ = lax.optimization_barrier((who, packed[0]))
    packed = pack(z.inner_rows, later)

    weights, drift_weights = pl.pallas_call(
        functools.partial(weights_kernel, z),
        out_shape=(
            jax.ShapeDtypeStruct((2 * NB, NB), BF16),
            jax.ShapeDtypeStruct((NB, LANES), BF16),
        ),
        in_specs=[VMEM] * 3,
        out_specs=(VMEM,) * 2,
        compiler_params=params(24),
        cost_estimate=cost(2e9, 4 * NB * NB * 2),
        name="weights",
    )(kernel_linear, kernel_square, drift_kernel)
    speed = speeds(z)
    *got, weights, drift_weights, speed = lax.optimization_barrier(
        (*got, weights, drift_weights, speed)
    )

    def state(rows, columns):
        return (CH // LANES, rows, columns, LANES)

    def unpack(rows, received, shapes):
        return pl.pallas_call(
            functools.partial(unpack_kernel, z, rows),
            out_shape=[jax.ShapeDtypeStruct(shape, F32) for shape in shapes],
            in_specs=[SMEM] * 2 + [VMEM] * B,
            out_specs=[VMEM] * len(shapes),
            compiler_params=params(16),
            name="unpack",
        )(*who, *received)

    bottom, top, sea = unpack(
        z.edge_rows, got[:B], [state(EDGE, width), state(EDGE, width), (R, width, LANES)]
    )
    *blocks, top = lax.optimization_barrier((*packed[half:], top))
    blocks = list(packed[:half]) + blocks
    got = [lax.ppermute(blocks[k], axes, forward[k]) for k in range(B)]
    (inner,) = unpack(z.inner_rows, got, [state(R - 2 * EDGE, width)])

    def step_call(body, first, cut, sea_at, count, deepest, inputs, more=()):
        width = inputs[0].shape[2]
        n = width - 2 * cut
        shapes = [state(count, n)] + [before + (EDGE, width, LANES) for before in more]
        return pl.pallas_call(
            functools.partial(body, z, first, cut, sea_at),
            out_shape=[jax.ShapeDtypeStruct(shape, F32) for shape in shapes],
            in_specs=[VMEM] * (len(inputs) + 3),
            out_specs=[VMEM] * len(shapes),
            scratch_shapes=[
                pltpu.VMEM((4, deepest, width, LANES), F32),
                pltpu.VMEM((NB // LANES, count, width + PAD, LANES), F32),
            ],
            compiler_params=params(24),
            cost_estimate=cost(count * 1e8, count * 1e5),
            name=body.__name__,
        )(*inputs, speed, weights, drift_weights)

    sea_up, sea_down = [], []
    for step in range(STEPS):
        valid = EDGE * (STEPS - 1 - step)
        margin = (width - C) // 2
        cut = margin - valid if valid == 0 or (margin - valid) % 4 == 0 else 0
        sea_at = PAD - margin
        down = lax.ppermute(top, axes, to_prev_row)
        up = lax.ppermute(bottom, axes, to_next_row)
        first = step == 0

        def advance_inner():
            return step_call(
                inner_kernel, first, cut, sea_at, R - 2 * EDGE, R, (top, inner, bottom, sea),
                () if first else ((NB // LANES,),) * 2,
            )

        given = ()
        if not first:
            new_inner, *given = advance_inner()
        new_bottom, *found = step_call(
            bottom_kernel, first, cut, sea_at, EDGE, 3 * EDGE,
            (down, bottom, inner, sea, *sea_down, *given[1:]),
            ((),) if first else (),
        )
        sea_down = sea_down or found
        new_top, *found = step_call(
            top_kernel, first, cut, sea_at, EDGE, 3 * EDGE,
            (up, top, inner, sea, *sea_up, *given[:1]),
            ((),) if first else (),
        )
        sea_up = sea_up or found
        if first:
            inner, new_top = lax.optimization_barrier((inner, new_top))
            (new_inner,) = advance_inner()
        top, inner, bottom = new_top, new_inner, new_bottom
        width -= 2 * cut

    def send_back(rows, states):
        shape = jax.ShapeDtypeStruct((z.slabs(rows), C, LANES), F32)
        return pl.pallas_call(
            functools.partial(send_back_kernel, z, rows),
            out_shape=[shape] * B,
            in_specs=[SMEM] * 2 + [VMEM] * len(states),
            out_specs=[VMEM] * B,
            compiler_params=params(16),
            name="send_back",
        )(*who, *states)

    packed = send_back(z.inner_rows, [inner]), send_back(z.edge_rows, [bottom, top])
    packed = list(packed[1]) + list(packed[0])
    back = [
        lax.ppermute(packed[i], axes, [(t, s) for s, t in forward[i % B]]) for i in range(2 * B)
    ]
    halves = [
        jax.ShapeDtypeStruct((W // LANES, nb * R, LANES), F32),
        jax.ShapeDtypeStruct((W // LANES, 2 * L * R, LANES), F32),
    ]
    held = pl.pallas_call(
        functools.partial(restore_inner_kernel, z),
        out_shape=halves,
        in_specs=[SMEM] * 2 + [VMEM] * B,
        out_specs=[VMEM] * 2,
        scratch_shapes=[pltpu.VMEM((z.slabs(z.inner_rows), W, LANES), F32)],
        compiler_params=params(16),
        name="restore_inner",
    )(*who, *back[B:])
    spectrum_out, ocean_out, *_ = pl.pallas_call(
        functools.partial(restore_kernel, z),
        out_shape=[
            jax.ShapeDtypeStruct((nb * R, W), F32),
            jax.ShapeDtypeStruct((2 * L * R, W), F32),
        ]
        + halves,
        in_specs=[SMEM] * 2 + [VMEM] * (B + 2),
        out_specs=[HBM] * 2 + [VMEM] * 2,
        scratch_shapes=[
            pltpu.VMEM((z.slabs(z.edge_rows), W, LANES), F32),
            pltpu.SemaphoreType.DMA((2, W // LANES)),
        ],
        input_output_aliases={B + 2: 2, B + 3: 3},
        compiler_params=params(16),
        name="restore",
    )(*who, *back[:B], *held)
    return spectrum_out.reshape(nb, R, W), ocean_out.reshape(2, L, R, W)


def solution(mesh):
    return jax.shard_map(
        functools.partial(per_device, mesh.shape["geo"], mesh.shape["bins"]),
        mesh=mesh,
        in_specs=(
            P("bins", "geo", None),
            P("geo", None),
            P(),
            P(),
            P(),
            P(None, "bins", "geo", None),
        ),
        out_specs=(P("bins", "geo", None), P(None, "bins", "geo", None)),
        check_vma=False,
    )
```

```python
import functools

import jax
import jax.numpy as jnp
from jax import lax
from jax.experimental import pallas as pl
from jax.experimental.pallas import tpu as pltpu
from jax.sharding import PartitionSpec as P

NDIR = 36
NFREQ = 32
STEPS = 3
SUB = 2
DT_SOURCE = 0.5
DT_OCEAN = 0.2
CORIOLIS = 1.0
VISCOSITY = 1.0
DOPPLER = 0.1

LANES = 128
SUBLANES = 8
PAD = 8
HALO = SUB * STEPS
EDGE = 2
VMEM = pl.BlockSpec(memory_space=pltpu.VMEM)
SMEM = pl.BlockSpec(memory_space=pltpu.SMEM)
HBM = pl.BlockSpec(memory_space=pltpu.HBM)
F32 = jnp.float32
BF16 = jnp.bfloat16


def params(mib):
    return pltpu.CompilerParams(vmem_limit_bytes=mib * 1024 * 1024)


class Sizes:
    def __init__(self, parts, bins_here, levels_here, rows, width):
        self.B, self.nb, self.L, self.R, self.W = parts, bins_here, levels_here, rows, width
        self.C = width // parts
        self.mt = bins_here // LANES
        self.main = self.mt * LANES
        self.nr = bins_here - self.main
        self.no = 2 * levels_here
        self.NB = parts * bins_here
        self.CH = self.NB + LANES
        self.edge_rows = (rows - 2, rows - 1, 0, 1)
        self.inner_rows = tuple(range(2, rows - 2))
        self.half = parts // 2
        assert self.half & (self.half - 1) == 0 and self.half > 1
        assert self.nr * parts == LANES and self.no * parts == LANES

    def folds(self, rows):
        out, base = [], len(rows) * self.mt
        for count, tile in ((self.nr, self.B * self.mt), (self.no, self.NB // LANES)):
            used = min(LANES // count, len(rows))
            deep = len(rows) // used
            assert deep * used == len(rows)
            out.append((count, used, deep, base, tile))
            base += deep
        return out, base

    def halo(self, rows):
        return HALO if rows == self.edge_rows else PAD

    def slabs(self, rows):
        return self.folds(rows)[1]


def exchange_share(z, k, odd, part):
    core = part % 2
    flip, delta = (k // z.half) ^ core, (k % z.half) ^ core
    return (odd ^ flip) * z.half + ((part // 2) ^ delta)


def exchange_part(z, k, odd, part):
    core = (k // z.half) ^ odd ^ (part % 2)
    delta = (k % z.half) ^ core
    return ((part // 2) ^ delta) * 2 + core


def lane_group(width):
    return lax.broadcasted_iota(jnp.int32, (1, LANES), 1) // width


def pack_kernel(z, rows, odd, part, spec_in, ocean_in, mask_in, *refs):
    B, R, C, W, mt = z.B, z.R, z.C, z.W, z.mt
    outs, (spec, ocean, mask, wide, sems) = refs[:B], refs[B:]
    E, H = C + 2 * PAD, C + 2 * z.halo(rows)
    brought = slice((E - H) // 2, (E + H) // 2)
    copies = []
    for half in range(W // LANES):
        cols = pl.ds(half * LANES, LANES)
        for n, (src, dst) in enumerate(((spec_in, spec), (ocean_in, ocean))):
            copies.append(pltpu.make_async_copy(src.at[:, cols], dst.at[half], sems.at[n, half]))
            copies[-1].start()
    mask_copy = pltpu.make_async_copy(mask_in, mask, sems.at[2, 0])
    mask_copy.start()
    wide[:, 0:PAD, :] = jnp.zeros((wide.shape[0], PAD, LANES), F32)
    wide[:, PAD + W : W + 2 * PAD, :] = jnp.zeros((wide.shape[0], PAD, LANES), F32)
    folds, slabs = z.folds(rows)
    for half in range(W // LANES):
        for copy in copies[2 * half : 2 * half + 2]:
            copy.wait()
        cols = slice(PAD + half * LANES, PAD + (half + 1) * LANES)
        for i, r in enumerate(rows):
            for t in range(mt):
                block = spec[half, pl.ds(t * LANES * R + r, LANES, stride=R), :]
                wide[i * mt + t, cols] = block.T
        for (count, used, deep, base, _), src, first in zip(folds, (spec, ocean), (z.main, 0)):
            for rr in range(deep):
                pieces = [
                    src[half, pl.ds(first * R + rows[rr + i * deep], count, stride=R), :]
                    for i in range(used)
                ]
                if used * count < LANES:
                    pieces.append(jnp.zeros((LANES - used * count, LANES), F32))
                wide[base + rr, cols] = jnp.concatenate(pieces, axis=0).T
    mask_copy.wait()
    sea = jnp.concatenate([mask[...].astype(F32), jnp.zeros((R, LANES), F32)], axis=1)
    for k, out in enumerate(outs):
        share = exchange_share(z, k, odd[0], part[0])
        start = pl.multiple_of(share * C, PAD)
        for i in range(slabs):
            block = wide[i, pl.ds(start, E), :]
            out[i * H : (i + 1) * H] = block[brought]
        if rows == z.edge_rows:
            shift = lax.rem(W + LANES + PAD - start, W + LANES)
            out[slabs * H : slabs * H + R] = pltpu.roll(sea, shift, axis=1)[:, :LANES]


def spread_line(line):
    return jnp.broadcast_to(line, (LANES, LANES)).T


def unpack_kernel(z, rows, odd, part, *refs):
    B, mt = z.B, z.mt
    got, outs = refs[:B], refs[B:]
    E, H = z.C + 2 * PAD, z.C + 2 * z.halo(rows)
    brought = slice((E - H) // 2, (E + H) // 2)
    if rows == z.edge_rows:
        sea = outs[-1]
        outs = outs[:-1]
        lines = got[0][z.slabs(rows) * H : z.slabs(rows) * H + z.R]
        for r in range(z.R):
            sea[r] = spread_line(lines[r : r + 1])[:E]
    places = listed(*outs)
    for ref in outs:
        for columns in (slice(0, PAD), slice(E - PAD, E)):
            ref[:, :, columns] = jnp.zeros(ref.shape[:2] + (PAD, LANES), F32)
    src = [exchange_part(z, k, odd[0], part[0]) for k in range(B)]
    for k in range(B):
        for t in range(mt):
            for i, (ref, at) in enumerate(places):
                slab = i * mt + t
                ref[src[k] * mt + t, at, brought] = got[k][slab * H : (slab + 1) * H]
    for count, used, deep, base, home in z.folds(rows)[0]:
        group = lane_group(count)
        for i, (ref, at) in enumerate(places):
            tile = jnp.zeros((H, LANES), F32)
            for k in range(B):
                shift = lax.rem((src[k] - i // deep) * count + LANES, LANES)
                slab = base + i % deep
                moved = pltpu.roll(got[k][slab * H : (slab + 1) * H], shift, axis=1)
                tile = jnp.where(group == src[k], moved, tile)
            ref[home, at, brought] = tile
    if rows == z.edge_rows:
        for i, (ref, at) in enumerate(places):
            r = rows[i]
            ref[0, at, 0:1] = lines[r : r + 1]


def send_back_kernel(z, rows, odd, part, *refs):
    B, mt = z.B, z.mt
    states, outs = refs[:-B], refs[-B:]
    places = listed(*states)
    for k in range(B):
        src = exchange_part(z, k, odd[0], part[0])
        for t in range(mt):
            for i, (ref, at) in enumerate(places):
                outs[k][i * mt + t] = ref[src * mt + t, at]
        for count, used, deep, base, home in z.folds(rows)[0]:
            group = lane_group(count)
            for rr in range(deep):
                tile = jnp.zeros((z.C, LANES), F32)
                for i in range(used):
                    ref, at = places[rr + i * deep]
                    shift = lax.rem((i - src) * count + LANES, LANES)
                    moved = pltpu.roll(ref[home, at], shift, axis=1)
                    tile = jnp.where(group == i, moved, tile)
                outs[k][base + rr] = tile


def restore_rows(z, rows, odd, part, got, wide, spec, ocean):
    R, C, mt = z.R, z.C, z.mt
    folds, slabs = z.folds(rows)
    for k, block in enumerate(got):
        share = exchange_share(z, k, odd[0], part[0])
        wide[:, pl.ds(pl.multiple_of(share * C, PAD), C), :] = block[...]
    for half in range(z.W // LANES):
        cols = slice(half * LANES, (half + 1) * LANES)
        for i, r in enumerate(rows):
            for t in range(mt):
                place = pl.ds(t * LANES * R + r, LANES, stride=R)
                spec[half, place, :] = wide[i * mt + t, cols].T
        for (count, used, deep, base, _), dst, first in zip(folds, (spec, ocean), (z.main, 0)):
            for rr in range(deep):
                turned = wide[base + rr, cols].T
                for i in range(used):
                    place = pl.ds(first * R + rows[rr + i * deep], count, stride=R)
                    dst[half, place, :] = turned[i * count : (i + 1) * count]
        yield half


def restore_inner_kernel(z, odd, part, *refs):
    got, (spec, ocean, wide) = refs[: z.B], refs[z.B :]
    for _ in restore_rows(z, z.inner_rows, odd, part, got, wide, spec, ocean):
        pass


def restore_kernel(z, odd, part, *refs):
    got, (_, _, spec_out, ocean_out, spec, ocean, wide, sems) = refs[: z.B], refs[z.B :]
    copies = []
    for half in restore_rows(z, z.edge_rows, odd, part, got, wide, spec, ocean):
        cols = pl.ds(half * LANES, LANES)
        for n, (src, dst) in enumerate(((spec, spec_out), (ocean, ocean_out))):
            copies.append(pltpu.make_async_copy(src.at[half], dst.at[:, cols], sems.at[n, half]))
            copies[-1].start()
    for copy in copies:
        copy.wait()


def weights_kernel(z, linear, square, drift, weights, drift_weights):
    B, nb, main, nr, NB, L = z.B, z.nb, z.main, z.nr, z.NB, z.L

    def put(dst, first, lanes, turned):
        for s in range(B):
            dst[first + s * main : first + (s + 1) * main, lanes] = turned[
                s * nb : s * nb + main
            ]
            tail = first + B * main + s * nr
            dst[tail : tail + nr, lanes] = turned[s * nb + main : (s + 1) * nb]

    for n, source in enumerate((linear, square)):
        for s in range(B):
            for t in range(z.mt):
                block = source[s * nb + t * LANES : s * nb + (t + 1) * LANES, :]
                lane = s * main + t * LANES
                put(weights, n * NB, slice(lane, lane + LANES), block.T)
        tails = [source[s * nb + main : (s + 1) * nb, :] for s in range(B)]
        block = jnp.concatenate(tails, axis=0)
        put(weights, n * NB, slice(B * main, NB), block.T)

    row = lax.broadcasted_iota(jnp.int32, (LANES, LANES), 0)
    lane = lax.broadcasted_iota(jnp.int32, (LANES, LANES), 1)
    part, comp, level = lane // (2 * L), (lane // L) % 2, lane % L
    pick = jnp.where(row == 2 * (part * L + level) + 1 - comp, 1.0, 0.0).astype(BF16)
    turned = jnp.dot(drift[...].T, pick, preferred_element_type=F32).astype(BF16)
    put(drift_weights, 0, slice(0, LANES), turned)


def advance(
    z, sea_rows, rows, outs, cut, sea_at, speed, weights, drift_weights, moved, moved_twice,
    known=None, kept=None,
):
    NB, L, tiles = z.NB, z.L, z.NB // LANES
    known, kept = known or {}, kept or {}
    n = len(rows)
    first = [r for r in range(1, n - 1) if r not in known]
    assert first == list(range(first[0], first[-1] + 1))
    E = rows[0][0].shape[2]
    N = E - 2 * cut
    keep = slice(cut, cut + N)
    places = listed(*outs)
    T = E // SUBLANES
    offset = -cut % SUBLANES

    def apart(start):
        return [pl.ds(start + t, SUBLANES, stride=T) for t in range(T)]

    def sea_row(place):
        return place[0][place[1], pl.ds(sea_at, E)]

    def shift_up(parts):
        return [pltpu.roll(parts[-1], 1, axis=0)] + parts[:-1]

    def shift_down(parts):
        return parts[1:] + [pltpu.roll(parts[0], SUBLANES - 1, axis=0)]

    def in_order(t):
        return slice(t * SUBLANES, (t + 1) * SUBLANES)

    for r in range(min(first[0] - 1, 1), max(first[-1] + 2, n - 1)):
        for t in range(T):
            ref, i = rows[r]
            current = DOPPLER * jnp.tanh(ref[tiles, i, apart(0)[t], :])
            for c in range(2):
                one = current[:, c * L : c * L + 1]
                moved[c, r, in_order(t)] = jnp.broadcast_to(one, (SUBLANES, LANES))
            ref, i = sea_rows[r]
            moved[3, r, in_order(t)] = ref[i, apart(sea_at)[t], :]

    def advect(read, write, start, stop, speed_cx, speed_cy):
        plus_before, waiting = None, None
        for r in range(start - 1, stop + 1):
            energy = read(r)
            speed_x = [speed_cx + moved[0, r, in_order(t)] for t in range(T)]
            if r >= start:
                minus = [jnp.minimum(v, 0.0) * e for v, e in zip(speed_x, energy)]
            if r > start:
                sea = [moved[3, r - 1, in_order(t)] for t in range(T)]
                write(r - 1, [(w - m) * s for w, m, s in zip(waiting, minus, sea)])
            if r < stop:
                plus = [jnp.maximum(v, 0.0) * e for v, e in zip(speed_x, energy)]
            if start <= r < stop:
                speed_y = [speed_cy + moved[1, r, in_order(t)] for t in range(T)]
                plus_y = [jnp.maximum(v, 0.0) * e for v, e in zip(speed_y, energy)]
                minus_y = [jnp.minimum(v, 0.0) * e for v, e in zip(speed_y, energy)]
                waiting = [
                    e - ((p - before) - m) - ((py - south) + (north - my))
                    for e, p, before, m, py, south, north, my in zip(
                        energy, plus, plus_before, minus,
                        plus_y, shift_up(plus_y), shift_down(minus_y), minus_y,
                    )
                ]
            plus_before = plus

    def one_tile(j, carry):
        lanes = pl.ds(pl.multiple_of(j * LANES, LANES), LANES)
        speed_cx = speed[0:1, lanes]
        speed_cy = speed[1:2, lanes]

        def read_first(r):
            ref, i = rows[r]
            return [ref[j, i, at, :] for at in apart(0)]

        def write_first(r, parts):
            for t, part in enumerate(parts):
                moved[2, r, in_order(t)] = part
                if r in kept:
                    ref, i = kept[r]
                    ref[j, i, in_order(t)] = part

        def read_second(r):
            if r in known:
                ref, i = known[r]
                return [ref[j, i, in_order(t)] for t in range(T)]
            return [moved[2, r, in_order(t)] for t in range(T)]

        def write_second(r, parts):
            for at, part in zip(apart(offset), parts):
                moved_twice[j, r - 2, at, :] = part

        advect(read_first, write_first, first[0], first[-1] + 1, speed_cx, speed_cy)
        advect(read_second, write_second, 2, n - 2, speed_cx, speed_cy)
        return carry

    lax.fori_loop(0, tiles, one_tile, 0)

    count = len(places)
    own_sea = sea_rows[2 : n - 2]
    own = slice(cut + offset, cut + offset + N)
    energy = jnp.concatenate(
        [moved_twice[j, :, own].reshape(count * N, LANES) for j in range(tiles)], axis=1
    )
    squares = energy * energy
    both = jnp.concatenate([energy.astype(BF16), squares.astype(BF16)], axis=1)
    interaction = jnp.dot(both, weights[...], preferred_element_type=F32)
    total = jnp.sum(squares, axis=1, keepdims=True)
    sea_here = jnp.concatenate([sea_row(place)[keep] for place in own_sea], axis=0)
    scale = (DT_SOURCE * sea_here[:, 0:1]) / (1.0 + total / NB)
    fresh = energy + scale * (interaction * energy)
    for i, (ref, at) in enumerate(places):
        for j in range(tiles):
            ref[j, at] = fresh[i * N : (i + 1) * N, j * LANES : (j + 1) * LANES]
    drift = jnp.dot(fresh.astype(BF16), drift_weights[...], preferred_element_type=F32)

    comp = (lax.broadcasted_iota(jnp.int32, (1, LANES), 1) // L) % 2
    sign = jnp.where(comp == 0, 1.0, -1.0).astype(F32)
    for i, (out, at) in enumerate(places):
        here, before, after = [
            ref[tiles, row] for ref, row in (rows[i + 2], rows[i + 1], rows[i + 3])
        ]
        lap = (
            (after + before)
            + (pltpu.roll(here, E - 1, axis=0) + pltpu.roll(here, 1, axis=0))
            - 4.0 * here
        )[keep]
        centre = here[keep]
        other = jnp.where(
            comp == 0, pltpu.roll(centre, LANES - L, axis=1), pltpu.roll(centre, L, axis=1)
        )
        turn = sign * (CORIOLIS * (other + drift[i * N : (i + 1) * N]))
        out[tiles, at] = (
            centre + DT_OCEAN * (turn + VISCOSITY * lap)
        ) * sea_row(own_sea[i])[keep]


def listed(*refs):
    return [(ref, i) for ref in refs for i in range(ref.shape[-3])]


def inner_kernel(z, first, cut, sea_at, top, inner, bottom, sea, speed, weights, drift_weights, *refs):
    out, for_edges, (moved, moved_twice) = refs[0], refs[1:-2], refs[-2:]
    kept = {}
    if for_edges:
        kept = {1 + i: (for_edges[0], i) for i in range(EDGE)}
        kept |= {z.R - 1 - EDGE + i: (for_edges[1], i) for i in range(EDGE)}
    advance(
        z, listed(sea), listed(top, inner, bottom), [out], cut, sea_at, speed, weights,
        drift_weights, moved, moved_twice, kept=kept,
    )


def read_sea(halo, sea):
    for i in range(EDGE):
        sea[i] = spread_line(halo[0, i, 0:1])[: halo.shape[2]]
    return sea


def top_kernel(z, first, cut, sea_at, up, top, inner, sea, *refs):
    inputs, outs = refs[:-4] if first else refs[:-3], refs[-4:] if first else refs[-3:]
    *given, speed, weights, drift_weights = inputs
    out, moved, moved_twice = outs[0], outs[-2], outs[-1]
    sea_up = read_sea(up, outs[1]) if first else given.pop(0)
    known = {3 + i: (given[0], i) for i in range(EDGE)} if given else {}
    rows = listed(up, top) + listed(inner)[:EDGE]
    sea_rows = (listed(sea_up) + listed(sea))[: len(rows)]
    advance(
        z, sea_rows, rows, [out], cut, sea_at, speed, weights, drift_weights, moved,
        moved_twice, known=known,
    )


def bottom_kernel(z, first, cut, sea_at, down, bottom, inner, sea, *refs):
    inputs, outs = refs[:-4] if first else refs[:-3], refs[-4:] if first else refs[-3:]
    *given, speed, weights, drift_weights = inputs
    out, moved, moved_twice = outs[0], outs[-2], outs[-1]
    sea_down = read_sea(down, outs[1]) if first else given.pop(0)
    known = {1 + i: (given[0], i) for i in range(EDGE)} if given else {}
    rows = listed(inner)[-EDGE:] + listed(bottom, down)
    sea_rows = (listed(sea) + listed(sea_down))[-len(rows) :]
    advance(
        z, sea_rows, rows, [out], cut, sea_at, speed, weights, drift_weights, moved,
        moved_twice, known=known,
    )


def speeds(z):
    lane = jnp.arange(z.NB, dtype=jnp.int32)
    head = (lane // z.main) * z.nb + lane % z.main
    rest = lane - z.B * z.main
    tail = (rest // z.nr) * z.nb + z.main + rest % z.nr
    bin_index = jnp.where(lane < z.B * z.main, head, tail)
    direction = (bin_index // NFREQ).astype(F32)
    frequency = (bin_index % NFREQ).astype(F32)
    group_speed = 0.4 / (1.0 + frequency / 16.0)
    bin_angle = (2.0 * jnp.pi / NDIR) * direction
    zeros = jnp.zeros_like(bin_angle)
    rows = [group_speed * jnp.cos(bin_angle), group_speed * jnp.sin(bin_angle)] + [zeros] * 6
    return jnp.stack(rows)


def cost(flops, moved):
    return pl.CostEstimate(flops=int(flops), bytes_accessed=int(moved), transcendentals=0)


def per_device(G, B, spectrum, sea_mask, kernel_linear, kernel_square, drift_kernel, ocean):
    nb, R, W = spectrum.shape
    L = ocean.shape[1]
    z = Sizes(B, nb, L, R, W)
    C, NB, CH = z.C, z.NB, z.CH
    half = B // 2
    axes = ("geo", "bins")
    geo, part = lax.axis_index("geo"), lax.axis_index("bins")

    def device_at(q, c):
        return ((q // 2) * 2 + c // half) * B + 2 * (c % half) + q % 2

    forward = [
        [
            (g * B + b, device_at(g, exchange_share(z, k, g % 2, b)))
            for g in range(G)
            for b in range(B)
        ]
        for k in range(B)
    ]
    pairs = [(q, c) for q in range(G) for c in range(B)]
    to_next_row = [(device_at(q, c), device_at((q + 1) % G, c)) for q, c in pairs]
    to_prev_row = [(t, s) for s, t in to_next_row]
    who = ((geo % 2).astype(jnp.int32).reshape(1), part.astype(jnp.int32).reshape(1))

    width = C + 2 * PAD
    columns_scratch = [
        pltpu.VMEM((W // LANES, nb * R, LANES), F32),
        pltpu.VMEM((W // LANES, 2 * L * R, LANES), F32),
    ]
    def pack(rows, who):
        slabs = z.slabs(rows)
        lines = slabs * (C + 2 * z.halo(rows)) + (R if rows == z.edge_rows else 0)
        return pl.pallas_call(
            functools.partial(pack_kernel, z, rows),
            out_shape=[jax.ShapeDtypeStruct((lines, LANES), F32)] * B,
            in_specs=[SMEM] * 2 + [HBM] * 3,
            out_specs=[VMEM] * B,
            scratch_shapes=columns_scratch
            + [
                pltpu.VMEM((R, W), jnp.int32),
                pltpu.VMEM((slabs, W + 2 * PAD, LANES), F32),
                pltpu.SemaphoreType.DMA((3, W // LANES)),
            ],
            compiler_params=params(58),
            name="pack",
        )(*who, spectrum.reshape(nb * R, W), ocean.reshape(2 * L * R, W), sea_mask)

    packed = pack(z.edge_rows, who)
    got = [lax.ppermute(packed[k], axes, forward[k]) for k in range(B)]
    later, _ = lax.optimization_barrier((who, packed[0]))
    packed = pack(z.inner_rows, later)

    weights, drift_weights = pl.pallas_call(
        functools.partial(weights_kernel, z),
        out_shape=(
            jax.ShapeDtypeStruct((2 * NB, NB), BF16),
            jax.ShapeDtypeStruct((NB, LANES), BF16),
        ),
        in_specs=[VMEM] * 3,
        out_specs=(VMEM,) * 2,
        compiler_params=params(24),
        cost_estimate=cost(2e9, 4 * NB * NB * 2),
        name="weights",
    )(kernel_linear, kernel_square, drift_kernel)
    speed = speeds(z)
    *got, weights, drift_weights, speed = lax.optimization_barrier(
        (*got, weights, drift_weights, speed)
    )

    def state(rows, columns):
        return (CH // LANES, rows, columns, LANES)

    def unpack(rows, received, shapes):
        return pl.pallas_call(
            functools.partial(unpack_kernel, z, rows),
            out_shape=[jax.ShapeDtypeStruct(shape, F32) for shape in shapes],
            in_specs=[SMEM] * 2 + [VMEM] * B,
            out_specs=[VMEM] * len(shapes),
            compiler_params=params(16),
            name="unpack",
        )(*who, *received)

    bottom, top, sea = unpack(
        z.edge_rows, got[:B], [state(EDGE, width), state(EDGE, width), (R, width, LANES)]
    )
    *blocks, top = lax.optimization_barrier((*packed[half:], top))
    blocks = list(packed[:half]) + blocks
    got = [lax.ppermute(blocks[k], axes, forward[k]) for k in range(B)]
    (inner,) = unpack(z.inner_rows, got, [state(R - 2 * EDGE, width)])

    def step_call(body, first, cut, sea_at, count, deepest, inputs, more=()):
        width = inputs[0].shape[2]
        n = width - 2 * cut
        shapes = [state(count, n)] + [before + (EDGE, width, LANES) for before in more]
        return pl.pallas_call(
            functools.partial(body, z, first, cut, sea_at),
            out_shape=[jax.ShapeDtypeStruct(shape, F32) for shape in shapes],
            in_specs=[VMEM] * (len(inputs) + 3),
            out_specs=[VMEM] * len(shapes),
            scratch_shapes=[
                pltpu.VMEM((4, deepest, width, LANES), F32),
                pltpu.VMEM((NB // LANES, count, width + PAD, LANES), F32),
            ],
            compiler_params=params(24),
            cost_estimate=cost(count * 1e8, count * 1e5),
            name=body.__name__,
        )(*inputs, speed, weights, drift_weights)

    sea_up, sea_down = [], []
    for step in range(STEPS):
        valid = EDGE * (STEPS - 1 - step)
        margin = (width - C) // 2
        cut = margin - valid if valid == 0 or (margin - valid) % 4 == 0 else 0
        sea_at = PAD - margin
        down = lax.ppermute(top, axes, to_prev_row)
        up = lax.ppermute(bottom, axes, to_next_row)
        first = step == 0

        def advance_inner():
            return step_call(
                inner_kernel, first, cut, sea_at, R - 2 * EDGE, R, (top, inner, bottom, sea),
                () if first else ((NB // LANES,),) * 2,
            )

        given = ()
        if not first:
            new_inner, *given = advance_inner()
        new_bottom, *found = step_call(
            bottom_kernel, first, cut, sea_at, EDGE, 3 * EDGE,
            (down, bottom, inner, sea, *sea_down, *given[1:]),
            ((),) if first else (),
        )
        sea_down = sea_down or found
        new_top, *found = step_call(
            top_kernel, first, cut, sea_at, EDGE, 3 * EDGE,
            (up, top, inner, sea, *sea_up, *given[:1]),
            ((),) if first else (),
        )
        sea_up = sea_up or found
        if first:
            inner, new_top = lax.optimization_barrier((inner, new_top))
            (new_inner,) = advance_inner()
        top, inner, bottom = new_top, new_inner, new_bottom
        width -= 2 * cut

    def send_back(rows, states):
        shape = jax.ShapeDtypeStruct((z.slabs(rows), C, LANES), F32)
        return pl.pallas_call(
            functools.partial(send_back_kernel, z, rows),
            out_shape=[shape] * B,
            in_specs=[SMEM] * 2 + [VMEM] * len(states),
            out_specs=[VMEM] * B,
            compiler_params=params(16),
            name="send_back",
        )(*who, *states)

    packed = send_back(z.inner_rows, [inner]), send_back(z.edge_rows, [bottom, top])
    packed = list(packed[1]) + list(packed[0])
    back = [
        lax.ppermute(packed[i], axes, [(t, s) for s, t in forward[i % B]]) for i in range(2 * B)
    ]
    halves = [
        jax.ShapeDtypeStruct((W // LANES, nb * R, LANES), F32),
        jax.ShapeDtypeStruct((W // LANES, 2 * L * R, LANES), F32),
    ]
    held = pl.pallas_call(
        functools.partial(restore_inner_kernel, z),
        out_shape=halves,
        in_specs=[SMEM] * 2 + [VMEM] * B,
        out_specs=[VMEM] * 2,
        scratch_shapes=[pltpu.VMEM((z.slabs(z.inner_rows), W, LANES), F32)],
        compiler_params=params(16),
        name="restore_inner",
    )(*who, *back[B:])
    spectrum_out, ocean_out, *_ = pl.pallas_call(
        functools.partial(restore_kernel, z),
        out_shape=[
            jax.ShapeDtypeStruct((nb * R, W), F32),
            jax.ShapeDtypeStruct((2 * L * R, W), F32),
        ]
        + halves,
        in_specs=[SMEM] * 2 + [VMEM] * (B + 2),
        out_specs=[HBM] * 2 + [VMEM] * 2,
        scratch_shapes=[
            pltpu.VMEM((z.slabs(z.edge_rows), W, LANES), F32),
            pltpu.SemaphoreType.DMA((2, W // LANES)),
        ],
        input_output_aliases={B + 2: 2, B + 3: 3},
        compiler_params=params(16),
        name="restore",
    )(*who, *back[:B], *held)
    return spectrum_out.reshape(nb, R, W), ocean_out.reshape(2, L, R, W)


def solution(mesh):
    return jax.shard_map(
        functools.partial(per_device, mesh.shape["geo"], mesh.shape["bins"]),
        mesh=mesh,
        in_specs=(
            P("bins", "geo", None),
            P("geo", None),
            P(),
            P(),
            P(),
            P(None, "bins", "geo", None),
        ),
        out_specs=(P("bins", "geo", None), P(None, "bins", "geo", None)),
        check_vma=False,
    )
```
